32 devices in a mesh: batch: 4 (over y, x), seq: 8 (over z, core).
Axes of the slice: x: 2, y: 2, z: 4, core: 2. Of those that a mesh axis runs over, the one named last changes fastest.
Arguments:
- inputs: bfloat16 [4, 8192, 312], P('batch', 'seq'), may hold values from -6 to 6
- teacher_input: bfloat16 [4, 8192, 768], P('batch', 'seq'), may hold values from -6 to 6
- filled_slot_mask: int32 [4, 8192], P('batch'), may hold values 0 or 1
- seg_lengths: int32 [4, 32], P('batch'), may hold values from 1 to 511, as said below
- query_weight: bfloat16 [312, 312], replicated, may hold values from -0.3125 to 0.3125
- key_weight: bfloat16 [312, 312], replicated, may hold values from -0.3125 to 0.3125
- value_weight: bfloat16 [312, 312], replicated, may hold values from -0.3125 to 0.3125
- w_output: bfloat16 [312, 312], replicated, may hold values from -3.5 to 3.5
- gain_one: float32 [312], replicated, may hold values from 0.1 to 1.9
- shift_one: float32 [312], replicated, may hold values from -1.8 to 1.8
- w_inner: bfloat16 [312, 1200], replicated, may hold values from -0.3125 to 0.3125
- b_inner: float32 [1200], replicated, may hold values from -3 to 3
- w_outer: bfloat16 [1200, 312], replicated, may hold values from -0.1875 to 0.1875
- b_outer: float32 [312], replicated, may hold values from -1.8 to 1.8
- gain_two: float32 [312], replicated, may hold values from 0.1 to 1.9
- shift_two: float32 [312], replicated, may hold values from -1.8 to 1.8
- w_hidden: bfloat16 [312, 768], replicated, may hold values from -0.3125 to 0.3125
- teacher_query_weight: bfloat16 [768, 768], replicated, may hold values from -0.21875 to 0.21875
- teacher_key_weight: bfloat16 [768, 768], replicated, may hold values from -0.21875 to 0.21875
- teacher_value_weight: bfloat16 [768, 768], replicated, may hold values from -0.21875 to 0.21875
- teacher_output: bfloat16 [768, 768], replicated, may hold values from -2 to 2
- teacher_gain_one: float32 [768], replicated, may hold values from 0.1 to 1.9
- teacher_shift_one: float32 [768], replicated, may hold values from -1.8 to 1.8
- teacher_inner: bfloat16 [768, 3072], replicated, may hold values from -0.21875 to 0.21875
- teacher_outer: bfloat16 [3072, 768], replicated, may hold values from -0.109375 to 0.109375
- teacher_gain_two: float32 [768], replicated, may hold values from 0.1 to 1.9
- teacher_shift_two: float32 [768], replicated, may hold values from -1.8 to 1.8
Outputs:
- student_out: bfloat16 [4, 8192, 312], P('batch', 'seq')
- grad_inputs: bfloat16 [4, 8192, 312], P('batch', 'seq')
- loss: float32 [], replicated
- grad_w_query: float32 [312, 312], replicated
- grad_w_key: float32 [312, 312], replicated
- grad_w_value: float32 [312, 312], replicated
- grad_w_output: float32 [312, 312], replicated
- grad_gain_one: float32 [312], replicated
- grad_shift_one: float32 [312], replicated
- grad_w_inner: float32 [312, 1200], replicated
- grad_b_inner: float32 [1200], replicated
- grad_w_outer: float32 [1200, 312], replicated
- grad_b_outer: float32 [312], replicated
- grad_gain_two: float32 [312], replicated
- grad_shift_two: float32 [312], replicated
- grad_w_hidden: float32 [312, 768], replicated
The draws below stay inside these ranges and needn't reach their ends.
Inputs may be any that keep to these rules, and one draw needn't show every extreme that they name: `seg_lengths`: the segments of a row tile its 8192 slots in order from the first. Exactly one segment starts in each aligned window of 256 slots, and no segment starts at the first slot of a device's 1024 slots except the row's first.
All inputs are finite; a program needn't handle non-finite values. No bound on the sum of `filled_slot_mask` on one device may be relied on, other than what follows from the above.
Results may differ from the reference program's by a relative error of at most 0.0095.
Values may be sent and summed in bfloat16 or wider, within the bound.
A program may use at most 384 MiB of HBM per device.

```python
import jax
import jax.numpy as jnp
from jax import lax

HEADS = 12
HD_S = 26
FF_S = 1200
HD_T = 64
FF_T = 3072
DEVICE_TOKENS = 1024
HALFW = 256
STUDENT_WIDTH = 312
TEACHER_WIDTH = 768
QUERY_BLOCK = 512
KEY_REACH = 256
PACKED_ROWS = 4
ROW_LENGTH = 8192
SEGS = 32


def draw_seg_lengths(key, part):
    key = jax.random.fold_in(key, 7)
    key_offset, key_border, key_portion, key_within = jax.random.split(key, 4)
    windows = jnp.arange(SEGS, dtype=jnp.int32)
    per_shard = DEVICE_TOKENS // HALFW
    offsets = jax.random.randint(key_offset, (PACKED_ROWS, SEGS), 0, HALFW, dtype=jnp.int32)
    border_offsets = jax.random.randint(key_border, (PACKED_ROWS, SEGS), 1, HALFW, dtype=jnp.int32)
    border = (windows % per_shard == 0)[None, :]
    offsets = jnp.where(border, border_offsets, offsets)
    portion_select = jax.random.randint(key_portion, (PACKED_ROWS, 1), 0, ROW_LENGTH // DEVICE_TOKENS - 1, dtype=jnp.int32)
    within_pick = jax.random.randint(key_within, (PACKED_ROWS, 1), 1, per_shard, dtype=jnp.int32)
    chosen = portion_select * per_shard + within_pick
    offsets = jnp.where(windows[None, :] == chosen, 0, offsets)
    offsets = jnp.where(windows[None, :] == chosen + 1, HALFW - 1, offsets)
    offsets = jnp.where(windows[None, :] == 0, 0, offsets)
    start_positions = windows[None, :] * HALFW + offsets
    finish_point = jnp.concatenate([start_positions[:, 1:], jnp.full((PACKED_ROWS, 1), ROW_LENGTH, jnp.int32)], axis=1)
    return (finish_point - start_positions).astype(jnp.int32)


def plant(values, rng, low, high):
    extent = values.shape
    place = [jax.random.randint(jax.random.fold_in(rng, axis), (), 0, extent[axis]) for axis in range(len(extent))]
    values = values.at[tuple(place)].set(low)
    longest = extent.index(max(extent))
    place[longest] = (place[longest] + 1) % extent[longest]
    return values.at[tuple(place)].set(high)


def shard_levels(key, extent, pieces, smallest, largest):
    def one(axis_at, blocks):
        steps = jax.random.uniform(jax.random.fold_in(jax.random.fold_in(key, 6), axis_at), (blocks,), jnp.float32, smallest / len(pieces), largest / len(pieces))
        return jnp.repeat(jnp.exp(steps), extent[axis_at] // blocks).reshape((-1,) + (1,) * (len(extent) - axis_at - 1))

    loudness = one(*pieces[0])
    for cut in pieces[1:]:
        loudness = loudness * one(*cut)
    return loudness


def scatter_about(rng, dims, scale, reach, cuts=(), kind=jnp.bfloat16):
    loudness = shard_levels(rng, dims, cuts, -0.22, 0.18) if cuts else 1.0
    drawn = jax.random.normal(rng, dims, jnp.float32) * scale * loudness
    return jnp.minimum(jnp.maximum(drawn, -reach), reach).astype(kind)


def setup_inputs(seed: int = 0) -> dict:
    keys = jax.random.split(jax.random.key(seed), 28)
    inputs = scatter_about(keys[0], (PACKED_ROWS, ROW_LENGTH, STUDENT_WIDTH), 1.0, 6.0, ((0, 4), (1, 8)))
    teacher_input = scatter_about(keys[1], (PACKED_ROWS, ROW_LENGTH, TEACHER_WIDTH), 1.0, 6.0, ((0, 4), (1, 8)))
    filled_slot_mask = plant((jax.random.randint(keys[2], (PACKED_ROWS, ROW_LENGTH), 0, 8) < 7).astype(jnp.int32), jax.random.fold_in(keys[2], 1), 0, 1)
    seg_lengths = draw_seg_lengths(jax.random.fold_in(keys[27], 71), 0)
    query_weight = scatter_about(keys[4], (STUDENT_WIDTH, STUDENT_WIDTH), STUDENT_WIDTH ** -0.5, 0.3125)
    key_weight = scatter_about(keys[5], (STUDENT_WIDTH, STUDENT_WIDTH), STUDENT_WIDTH ** -0.5, 0.3125)
    value_weight = scatter_about(keys[6], (STUDENT_WIDTH, STUDENT_WIDTH), STUDENT_WIDTH ** -0.5, 0.3125)
    w_output = scatter_about(keys[7], (STUDENT_WIDTH, STUDENT_WIDTH), (max(3 * STUDENT_WIDTH // HALFW, 1)) ** -0.5, 3.5)
    gain_one = jnp.clip(1.0 + 0.18 * jax.random.normal(keys[8], (STUDENT_WIDTH,), jnp.float32), 0.1, 1.9)
    shift_one = scatter_about(keys[9], (STUDENT_WIDTH,), 0.3, 1.8, (), jnp.float32)
    w_inner = scatter_about(keys[10], (STUDENT_WIDTH, FF_S), STUDENT_WIDTH ** -0.5, 0.3125)
    b_inner = scatter_about(keys[11], (FF_S,), 0.5, 3.0, (), jnp.float32)
    w_outer = scatter_about(keys[12], (FF_S, STUDENT_WIDTH), FF_S ** -0.5, 0.1875)
    b_outer = scatter_about(keys[13], (STUDENT_WIDTH,), 0.3, 1.8, (), jnp.float32)
    gain_two = jnp.clip(1.0 + 0.18 * jax.random.normal(keys[14], (STUDENT_WIDTH,), jnp.float32), 0.1, 1.9)
    shift_two = scatter_about(keys[15], (STUDENT_WIDTH,), 0.3, 1.8, (), jnp.float32)
    w_hidden = scatter_about(keys[16], (STUDENT_WIDTH, TEACHER_WIDTH), STUDENT_WIDTH ** -0.5, 0.3125)
    teacher_query_weight = scatter_about(keys[17], (TEACHER_WIDTH, TEACHER_WIDTH), TEACHER_WIDTH ** -0.5, 0.21875)
    teacher_key_weight = scatter_about(keys[18], (TEACHER_WIDTH, TEACHER_WIDTH), TEACHER_WIDTH ** -0.5, 0.21875)
    teacher_value_weight = scatter_about(keys[19], (TEACHER_WIDTH, TEACHER_WIDTH), TEACHER_WIDTH ** -0.5, 0.21875)
    teacher_output = scatter_about(keys[20], (TEACHER_WIDTH, TEACHER_WIDTH), (max(3 * TEACHER_WIDTH // HALFW, 1)) ** -0.5, 2.0)
    teacher_gain_one = jnp.clip(1.0 + 0.18 * jax.random.normal(keys[21], (TEACHER_WIDTH,), jnp.float32), 0.1, 1.9)
    teacher_shift_one = scatter_about(keys[22], (TEACHER_WIDTH,), 0.3, 1.8, (), jnp.float32)
    teacher_inner = scatter_about(keys[23], (TEACHER_WIDTH, FF_T), TEACHER_WIDTH ** -0.5, 0.21875)
    teacher_outer = scatter_about(keys[24], (FF_T, TEACHER_WIDTH), FF_T ** -0.5, 0.109375)
    teacher_gain_two = jnp.clip(1.0 + 0.18 * jax.random.normal(keys[25], (TEACHER_WIDTH,), jnp.float32), 0.1, 1.9)
    teacher_shift_two = scatter_about(keys[26], (TEACHER_WIDTH,), 0.3, 1.8, (), jnp.float32)
    return dict(inputs=inputs, teacher_input=teacher_input, filled_slot_mask=filled_slot_mask, seg_lengths=seg_lengths, query_weight=query_weight, key_weight=key_weight, value_weight=value_weight, w_output=w_output, gain_one=gain_one, shift_one=shift_one, w_inner=w_inner, b_inner=b_inner, w_outer=w_outer, b_outer=b_outer, gain_two=gain_two, shift_two=shift_two, w_hidden=w_hidden, teacher_query_weight=teacher_query_weight, teacher_key_weight=teacher_key_weight, teacher_value_weight=teacher_value_weight, teacher_output=teacher_output, teacher_gain_one=teacher_gain_one, teacher_shift_one=teacher_shift_one, teacher_inner=teacher_inner, teacher_outer=teacher_outer, teacher_gain_two=teacher_gain_two, teacher_shift_two=teacher_shift_two)


EPSILON = 1e-05
NEGATIVE = -1e+30
HIGHEST = lax.Precision.HIGHEST

@jax.custom_vjp
def lower_precision(v):
    return lax.optimization_barrier(v.astype(jnp.bfloat16)).astype(jnp.float32)

@jax.custom_vjp
def lower_backward(v):
    return v

def low_keep(v):
    return (lower_precision(v), None)

def low_pass(kept, grad):
    return (grad,)

def back_keep(v):
    return (v, None)

def back_low(kept, grad):
    return (lower_precision(grad),)
lower_precision.defvjp(low_keep, low_pass)
lower_backward.defvjp(back_keep, back_low)

def matrix_product(left_side, right_side):
    return jnp.dot(left_side, right_side, precision=HIGHEST, preferred_element_type=jnp.float32)

def normalize(values, gain_vec, shift_vec):
    center = values - lax.optimization_barrier(jnp.mean(values, -1, keepdims=True))
    spread = lax.optimization_barrier(jnp.mean(center * center, -1, keepdims=True))
    return center * lax.rsqrt(spread + EPSILON) * gain_vec + shift_vec

def head_scores(query_vectors, key_rows, head_width):
    query_heads = query_vectors.reshape(query_vectors.shape[0], HEADS, head_width)
    key_heads = key_rows.reshape(key_rows.shape[0], HEADS, head_width)
    return jnp.einsum('qhd,khd->hqk', query_heads, key_heads, precision=HIGHEST) * head_width ** (-0.5)

def masked_softmax(scores, allowed):
    masked = jnp.where(allowed[None], scores, NEGATIVE)
    row_top = lax.optimization_barrier(jnp.max(masked, -1, keepdims=True))
    weights = jnp.exp(masked - row_top)
    return weights / lax.optimization_barrier(jnp.sum(weights, -1, keepdims=True))

def head_context(probabilities, value_rows, head_width):
    value_heads = value_rows.reshape(value_rows.shape[0], HEADS, head_width)
    mixed_rows = jnp.einsum('hqk,khd->qhd', probabilities, value_heads, precision=HIGHEST)
    return mixed_rows.reshape(mixed_rows.shape[0], HEADS * head_width)

def padded_row_set(array):
    return jnp.pad(array, ((0, 0), (KEY_REACH, KEY_REACH), (0, 0)))

def block_place(block_number):
    row_wise = ROW_LENGTH // QUERY_BLOCK
    row_number = (block_number // row_wise).astype(jnp.int32)
    first_slot = (block_number % row_wise * QUERY_BLOCK).astype(jnp.int32)
    return (row_number, first_slot)

def query_rows(block_number, array):
    row_number, first_slot = block_place(block_number)
    zero_start = jnp.zeros((), jnp.int32)
    return lax.dynamic_slice(array, (row_number, first_slot, zero_start), (1, QUERY_BLOCK, array.shape[2]))[0]

def key_window(block_number, padded):
    row_number, first_slot = block_place(block_number)
    zero_start = jnp.zeros((), jnp.int32)
    return lax.dynamic_slice(padded, (row_number, first_slot, zero_start), (1, QUERY_BLOCK + 2 * KEY_REACH, padded.shape[2]))[0]

def block_allowed(block_number, seg_padded, mask_padded):
    row_number, first_slot = block_place(block_number)
    window_size = QUERY_BLOCK + 2 * KEY_REACH
    seg_window = lax.dynamic_slice(seg_padded, (row_number, first_slot), (1, window_size))[0]
    mask_window = lax.dynamic_slice(mask_padded, (row_number, first_slot), (1, window_size))[0]
    own_slots = jnp.arange(QUERY_BLOCK, dtype=jnp.int32) + KEY_REACH
    seg_query = seg_window[KEY_REACH:KEY_REACH + QUERY_BLOCK]
    every_slot = jnp.arange(window_size, dtype=jnp.int32)
    allowed = (seg_query[:, None] == seg_window[None, :]) & ((mask_window[None, :] == 1) | (own_slots[:, None] == every_slot[None, :]))
    return (allowed, mask_window[KEY_REACH:KEY_REACH + QUERY_BLOCK].astype(jnp.float32))

def teacher_block(block_number, teacher_query_rows, teacher_key_padded, teacher_value_padded, seg_padded, mask_padded):
    allowed = block_allowed(block_number, seg_padded, mask_padded)[0]
    t_prob = masked_softmax(head_scores(query_rows(block_number, teacher_query_rows), key_window(block_number, teacher_key_padded), HD_T), allowed)
    return head_context(lower_precision(t_prob), key_window(block_number, teacher_value_padded), HD_T)

def student_block(block_number, query_vectors, padded_key, padded_value, teacher_query_rows, teacher_key_padded, seg_padded, mask_padded):
    allowed, valid_rows = block_allowed(block_number, seg_padded, mask_padded)
    t_prob = masked_softmax(head_scores(query_rows(block_number, teacher_query_rows), key_window(block_number, teacher_key_padded), HD_T), allowed)
    s_scores = lower_backward(head_scores(query_rows(block_number, query_vectors), key_window(block_number, padded_key), HD_S))
    s_prob = masked_softmax(s_scores, allowed)
    context = head_context(lower_precision(s_prob), key_window(block_number, padded_value), HD_S)
    prob_gap = s_prob - t_prob
    return (context, jnp.sum(valid_rows[None, :, None] * prob_gap * prob_gap))

def teacher_forward(flat_teacher, t_weights, seg_padded, mask_padded):
    teacher_query_weight, teacher_key_weight, teacher_value_weight, teacher_output, teacher_gain_one, teacher_shift_one, teacher_inner, teacher_outer, teacher_gain_two, teacher_shift_two = t_weights
    teacher_query_rows = lower_precision(matrix_product(flat_teacher, teacher_query_weight)).reshape(PACKED_ROWS, ROW_LENGTH, TEACHER_WIDTH)
    teacher_key_padded = padded_row_set(lower_precision(matrix_product(flat_teacher, teacher_key_weight)).reshape(PACKED_ROWS, ROW_LENGTH, TEACHER_WIDTH))
    teacher_value_padded = padded_row_set(lower_precision(matrix_product(flat_teacher, teacher_value_weight)).reshape(PACKED_ROWS, ROW_LENGTH, TEACHER_WIDTH))
    block_total = PACKED_ROWS * (ROW_LENGTH // QUERY_BLOCK)
    contexts = lax.map(lambda block_number: teacher_block(block_number, teacher_query_rows, teacher_key_padded, teacher_value_padded, seg_padded, mask_padded), jnp.arange(block_total, dtype=jnp.int32))
    context = lower_precision(contexts.reshape(-1, TEACHER_WIDTH))
    t_normed = normalize(flat_teacher + matrix_product(context, teacher_output), teacher_gain_one, teacher_shift_one)
    t_active = lower_precision(jax.nn.gelu(matrix_product(lower_precision(t_normed), teacher_inner), approximate=False))
    t_target = normalize(t_normed + matrix_product(t_active, teacher_outer), teacher_gain_two, teacher_shift_two)
    return (t_target, teacher_query_rows, teacher_key_padded)

def student_loss(params, flat_student, teacher_query_rows, teacher_key_padded, t_target, seg_padded, mask_padded, valid_flat):
    query_weight, key_weight, value_weight, w_output, gain_one, shift_one, w_inner, b_inner, w_outer, b_outer, gain_two, shift_two, w_hidden = params
    query_vectors = lower_backward(lower_precision(matrix_product(flat_student, query_weight))).reshape(PACKED_ROWS, ROW_LENGTH, STUDENT_WIDTH)
    padded_key = padded_row_set(lower_backward(lower_precision(matrix_product(flat_student, key_weight))).reshape(PACKED_ROWS, ROW_LENGTH, STUDENT_WIDTH))
    padded_value = padded_row_set(lower_backward(lower_precision(matrix_product(flat_student, value_weight))).reshape(PACKED_ROWS, ROW_LENGTH, STUDENT_WIDTH))
    run_block = jax.checkpoint(student_block)
    block_total = PACKED_ROWS * (ROW_LENGTH // QUERY_BLOCK)
    contexts, attention_terms = lax.map(lambda block_number: run_block(block_number, query_vectors, padded_key, padded_value, teacher_query_rows, teacher_key_padded, seg_padded, mask_padded), jnp.arange(block_total, dtype=jnp.int32))
    context = lower_backward(lower_precision(contexts.reshape(-1, STUDENT_WIDTH)))
    attended = lower_backward(matrix_product(context, w_output))
    normed = normalize(flat_student + attended, gain_one, shift_one)
    inner_pre = lower_backward(matrix_product(lower_precision(normed), w_inner) + b_inner)
    activated = lower_precision(jax.nn.gelu(inner_pre, approximate=False))
    outer_out = lower_backward(matrix_product(activated, w_outer) + b_outer)
    student_model = normalize(normed + outer_out, gain_two, shift_two)
    projected = lower_backward(matrix_product(lower_precision(student_model), w_hidden))
    hidden_gap = projected - t_target
    summed_total = TEACHER_WIDTH * jnp.sum(attention_terms) + jnp.sum(valid_flat[:, None] * hidden_gap * hidden_gap)
    return (summed_total, student_model)

def reference(inputs, teacher_input, filled_slot_mask, seg_lengths, query_weight, key_weight, value_weight, w_output, gain_one, shift_one, w_inner, b_inner, w_outer, b_outer, gain_two, shift_two, w_hidden, teacher_query_weight, teacher_key_weight, teacher_value_weight, teacher_output, teacher_gain_one, teacher_shift_one, teacher_inner, teacher_outer, teacher_gain_two, teacher_shift_two):
    slot_positions = jnp.arange(ROW_LENGTH, dtype=jnp.int32)
    start_positions = (jnp.cumsum(seg_lengths, axis=1) - seg_lengths).astype(jnp.int32)
    seg_ids = (lax.optimization_barrier(jnp.sum((start_positions[:, None, :] <= slot_positions[None, :, None]).astype(jnp.int32), axis=2)) - 1).astype(jnp.int32)
    seg_padded = jnp.pad(seg_ids, ((0, 0), (KEY_REACH, KEY_REACH)), constant_values=-1)
    mask_padded = jnp.pad(filled_slot_mask, ((0, 0), (KEY_REACH, KEY_REACH)))
    valid_flat = filled_slot_mask.reshape(-1).astype(jnp.float32)
    flat_teacher = teacher_input.reshape(-1, TEACHER_WIDTH).astype(jnp.float32)
    t_weights = (teacher_query_weight.astype(jnp.float32), teacher_key_weight.astype(jnp.float32), teacher_value_weight.astype(jnp.float32), teacher_output.astype(jnp.float32), teacher_gain_one.astype(jnp.float32), teacher_shift_one.astype(jnp.float32), teacher_inner.astype(jnp.float32), teacher_outer.astype(jnp.float32), teacher_gain_two.astype(jnp.float32), teacher_shift_two.astype(jnp.float32))
    t_target, teacher_query_rows, teacher_key_padded = teacher_forward(flat_teacher, t_weights, seg_padded, mask_padded)
    params = (query_weight.astype(jnp.float32), key_weight.astype(jnp.float32), value_weight.astype(jnp.float32), w_output.astype(jnp.float32), gain_one.astype(jnp.float32), shift_one.astype(jnp.float32), w_inner.astype(jnp.float32), b_inner.astype(jnp.float32), w_outer.astype(jnp.float32), b_outer.astype(jnp.float32), gain_two.astype(jnp.float32), shift_two.astype(jnp.float32), w_hidden.astype(jnp.float32))
    flat_student = inputs.reshape(-1, STUDENT_WIDTH).astype(jnp.float32)
    summed_total, pullback, student_model = jax.vjp(lambda weights_in, flat_in: student_loss(weights_in, flat_in, teacher_query_rows, teacher_key_padded, t_target, seg_padded, mask_padded, valid_flat), params, flat_student, has_aux=True)
    parameter_gradients, flat_gradient = pullback(jnp.ones((), jnp.float32))
    every_token = PACKED_ROWS * ROW_LENGTH
    return (student_model.reshape(PACKED_ROWS, ROW_LENGTH, STUDENT_WIDTH).astype(jnp.bfloat16), flat_gradient.reshape(PACKED_ROWS, ROW_LENGTH, STUDENT_WIDTH).astype(jnp.bfloat16), summed_total / (every_token * TEACHER_WIDTH), parameter_gradients[0] / every_token, parameter_gradients[1] / every_token, parameter_gradients[2] / every_token, parameter_gradients[3] / every_token, parameter_gradients[4] / every_token, parameter_gradients[5] / every_token, parameter_gradients[6] / every_token, parameter_gradients[7] / every_token, parameter_gradients[8] / every_token, parameter_gradients[9] / every_token, parameter_gradients[10] / every_token, parameter_gradients[11] / every_token, parameter_gradients[12] / every_token)
```

```python
from functools import partial

import jax
import jax.numpy as jnp
from jax import lax
from jax.experimental import pallas as pl
from jax.experimental.pallas import tpu as pltpu
from jax.sharding import PartitionSpec as P

HEADS = 12
HD_S = 26
HD_T = 64
WIN = 256
PAD = 32
SLOT_ONE = 26
PAIRS = HEADS // 2
CHUNK = 64
TAIL = 16
SLOTS = 4
BLOCK = 320
SUMS_AT = 1152
QKV_LANES = 384
MESH = pl.DeviceIdType.MESH
EPSILON = 1e-05
NEGATIVE = -1e30
LOG2E = 1.4426950408889634
F32 = jnp.float32
BF16 = jnp.bfloat16
VMEM = pl.BlockSpec(memory_space=pltpu.VMEM)
BIG = 60 << 20


def mm(left, right, dims):
    return lax.dot_general(left, right, ((dims[:1], dims[1:]), ((), ())), preferred_element_type=F32)


def nn(left, right):
    return mm(left, right, (1, 0))


def tn(left, right):
    return mm(left, right, (0, 0))


def nt(left, right):
    return mm(left, right, (1, 1))


def tt(left, right):
    return mm(left, right, (0, 1))


def pad_heads():
    row = lax.broadcasted_iota(jnp.int32, (HEADS * PAD, HEADS * HD_S), 0)
    col = lax.broadcasted_iota(jnp.int32, (HEADS * PAD, HEADS * HD_S), 1)
    spot = jnp.zeros((HEADS * PAD, HEADS * HD_S), F32)
    for head in range(HEADS):
        here = (row - head * PAD == col - head * HD_S) & (col >= head * HD_S) & (col < (head + 1) * HD_S)
        spot = jnp.where(here, 1.0, spot)
    return spot.astype(BF16)


def window_rows(mask_ref, lengths_ref, seq_index, windows, row_windows):
    lengths = lengths_ref[...].astype(F32)
    order = lax.broadcasted_iota(jnp.int32, lengths.shape, 1)
    lane = lax.broadcasted_iota(jnp.int32, (1, WIN), 1).astype(F32)
    out = []
    for j in range(windows + 2):
        number = seq_index * windows + (j - 1)
        inside = (number >= 0) & (number < row_windows)
        safe = jnp.clip(number, 0, row_windows - 1)
        start = jnp.sum(jnp.where(order < safe, lengths, 0.0), axis=1, keepdims=True)
        offset = start - (safe * WIN).astype(F32)
        late = (lane >= offset).astype(F32)
        filled = mask_ref[:, pl.ds(pl.multiple_of(safe * WIN, WIN), WIN)]
        filled = jnp.where(inside, filled.astype(F32), 0.0)
        out.append((late, filled))
    return out


def stack_rows(*rows):
    n = rows[0].shape[1]
    index = lax.broadcasted_iota(jnp.int32, (8, n), 0)
    block = jnp.zeros((8, n), F32)
    for k, row in enumerate(rows):
        block = jnp.where(index == k, row, block)
    return block.astype(BF16)


def attend_kernel(
    windows,
    row_windows,
    mask_ref,
    lengths_ref,
    xt_hbm,
    xs_ref,
    wtq_hbm,
    wtk_hbm,
    wtv_hbm,
    wq_ref,
    wk_ref,
    wv_ref,
    stats_ref,
    loss_ref,
    rows_ref,
    tctx_hbm,
    sctx_hbm,
    sq_hbm,
    skv_hbm,
    saved_e_hbm,
    saved_g_hbm,
    x_ref,
    xs_side_ref,
    wt_ref,
    bias_ref,
    wst_ref,
    tq_ref,
    tk_ref,
    tv_ref,
    sq_ref,
    skv_ref,
    tctx_ref,
    sctx_ref,
    e_ref,
    g_ref,
    work_ref,
    low_ref,
    in_sem,
    halo_send,
    halo_arrive,
    kv_sem,
    out_sem,
):
    slots = windows * WIN
    batch, seq = lax.axis_index("batch"), lax.axis_index("seq")
    peers = lax.axis_size("seq")
    has_left, has_right = seq > 0, seq < peers - 1
    width_t = x_ref.shape[1]
    extended = slots + 2 * WIN

    barrier = pltpu.get_barrier_semaphore()
    for move in (1, peers - 1):
        pl.semaphore_signal(barrier, inc=1, device_id=(batch, (seq + move) % peers), device_id_type=MESH)
    loads = [pltpu.make_async_copy(xt_hbm, x_ref.at[pl.ds(WIN, slots)], in_sem.at[0])]
    for k, w_hbm in enumerate((wtq_hbm, wtk_hbm, wtv_hbm)):
        loads.append(pltpu.make_async_copy(w_hbm, wt_ref.at[k], in_sem.at[1 + k]))
    for c in loads:
        c.start()
    pl.semaphore_wait(barrier, 2)

    def halo(side):
        device = (batch, seq - 1 + 2 * side)
        first = side * (slots - WIN)
        return [
            pltpu.make_async_remote_copy(
                src_ref=xt_hbm.at[pl.ds(first, WIN)],
                dst_ref=x_ref.at[pl.ds((1 - side) * (WIN + slots), WIN)],
                send_sem=halo_send.at[0, side],
                recv_sem=halo_arrive.at[0, 1 - side],
                device_id=device,
                device_id_type=MESH,
            ),
            pltpu.make_async_remote_copy(
                src_ref=xs_ref.at[:, pl.ds(first, WIN)],
                dst_ref=xs_side_ref.at[1 - side],
                send_sem=halo_send.at[1, side],
                recv_sem=halo_arrive.at[1, 1 - side],
                device_id=device,
                device_id_type=MESH,
            ),
        ]

    for side, present in ((0, has_left), (1, has_right)):

        @pl.when(present)
        def _():
            for c in halo(side):
                c.start()

        @pl.when(jnp.logical_not(present))
        def _():
            x_ref[side * (WIN + slots) : side * (WIN + slots) + WIN, :] = jnp.zeros((WIN, width_t), BF16)
            xs_side_ref[side] = jnp.zeros(xs_side_ref.shape[1:], BF16)

    info = window_rows(mask_ref, lengths_ref, seq, windows, row_windows)
    eye = lax.broadcasted_iota(jnp.int32, (WIN, WIN), 0) == lax.broadcasted_iota(jnp.int32, (WIN, WIN), 1)
    rows_ref[...] = jnp.zeros_like(rows_ref)
    for w in range(windows):
        late, filled = info[w + 1]
        late_l, filled_l = info[w]
        late_r, filled_r = info[w + 2]
        early = 1.0 - late
        here = slice(w * WIN, (w + 1) * WIN)
        rows_ref[0:1, here] = early
        rows_ref[1:2, here] = late
        rows_ref[2:3, here] = filled
        query = stack_rows(early, late)
        own = tn(stack_rows(NEGATIVE * (1.0 - early * filled), NEGATIVE * (1.0 - late * filled)), query)
        bias_ref[w, :WIN, :] = jnp.where(eye, 0.0, own)
        bias_ref[w, WIN:, :] = tn(
            stack_rows(
                NEGATIVE * (1.0 - late_l * filled_l), NEGATIVE * (1.0 - (1.0 - late_r) * filled_r)
            ),
            query,
        )
    loss_ref[...] = jnp.zeros_like(loss_ref)
    stats_ref[...] = jnp.zeros_like(stats_ref)
    spot = pad_heads()
    padded = HEADS * PAD
    row = lax.broadcasted_iota(jnp.int32, (padded, 1), 0) % PAD
    ones = (row >= SLOT_ONE) & (row < SLOT_ONE + 3)

    xs = xs_ref[...]
    for k, w_ref in enumerate((wq_ref, wk_ref, wv_ref)):
        wst_ref[k] = nt(spot, w_ref[...]).astype(BF16)
        made = nn(wst_ref[k], xs)
        if k == 0:
            sq_ref[...] = (made * (LOG2E * HD_S**-0.5)).astype(BF16)
        else:
            if k == 2:
                made = jnp.where(ones, 1.0, made)
            skv_ref[k - 1, :, WIN : WIN + slots] = made.astype(BF16)
    tail = (lax.broadcasted_iota(jnp.int32, (TAIL, extended), 0) == 0).astype(BF16)
    for head in range(HEADS):
        tv_ref[head * (HD_T + TAIL) + HD_T : (head + 1) * (HD_T + TAIL), :] = tail

    def put_values(made, first_head, lanes):
        for j in range(made.shape[0] // HD_T):
            at = (first_head + j) * (HD_T + TAIL)
            tv_ref[at : at + HD_T, lanes] = made[j * HD_T : (j + 1) * HD_T]

    part = width_t // 2
    loads[0].wait()
    for k in range(3):
        loads[1 + k].wait()
        for half in range(2):
            made = tt(wt_ref[k, :, half * part : (half + 1) * part], x_ref[WIN : WIN + slots, :])
            if k == 0:
                tq_ref[half * part : (half + 1) * part, :] = (made * (LOG2E * HD_T**-0.5)).astype(BF16)
            elif k == 1:
                tk_ref[half * part : (half + 1) * part, WIN : WIN + slots] = made.astype(BF16)
            else:
                put_values(made.astype(BF16), half * HEADS // 2, slice(WIN, WIN + slots))
    for side, present in ((0, has_left), (1, has_right)):

        @pl.when(present)
        def _():
            for sent, landed in zip(halo(side), halo(1 - side)):
                sent.wait_send()
                landed.wait_recv()

        lanes = slice(side * (WIN + slots), side * (WIN + slots) + WIN)
        for k in (1, 2):
            made = tt(wt_ref[k], x_ref[lanes, :]).astype(BF16)
            if k == 1:
                tk_ref[:, lanes] = made
            else:
                put_values(made, 0, lanes)
            made = nn(wst_ref[k], xs_side_ref[side])
            if k == 2:
                made = jnp.where(ones, 1.0, made)
            skv_ref[k - 1, :, lanes] = made.astype(BF16)
    finals = [
        pltpu.make_async_copy(sq_ref, sq_hbm, kv_sem.at[0]),
        pltpu.make_async_copy(skv_ref, skv_hbm, kv_sem.at[1]),
    ]
    for c in finals:
        c.start()

    def stores(pair, which):
        slot = pair % 2
        t_rows = pl.ds(pl.multiple_of(pair * 2 * HD_T, 2 * HD_T), 2 * HD_T)
        s_rows = pl.ds(pl.multiple_of(pair * 2 * PAD, 2 * PAD), 2 * PAD)
        heads = pl.ds(pair * 2, 2)
        ends = (
            (e_ref.at[slot], saved_e_hbm.at[:, heads]),
            (g_ref.at[slot], saved_g_hbm.at[:, heads]),
            (tctx_ref.at[t_rows], tctx_hbm.at[t_rows]),
            (sctx_ref.at[s_rows], sctx_hbm.at[s_rows]),
        )
        return [pltpu.make_async_copy(*ends[k], out_sem.at[k, pair]) for k in which]

    def one_pair(pair, carry):
        @pl.when(pair >= 2)
        def _():
            for c in stores(pair - 2, (0, 1)):
                c.wait()

        attend_pair(pair)
        for c in stores(pair, range(4)):
            c.start()
        return carry

    def attend_pair(pair):
        e_out, g_out = e_ref.at[pair % 2], g_ref.at[pair % 2]
        def rows_of(w):
            left = slice(w * WIN, (w + 1) * WIN)
            own = slice((w + 1) * WIN, (w + 2) * WIN)
            right = slice((w + 2) * WIN, (w + 3) * WIN)
            return left, own, right, rows_ref[0:1, left], rows_ref[1:2, left], rows_ref[2:3, left]

        def first_pass(w, q_ref, k_ref, rows, work_ref):
            left, own, right, early, late, _ = rows_of(w)
            query = q_ref[rows, left]
            query_fold = jnp.concatenate([query * early.astype(BF16), query * late.astype(BF16)], axis=0)
            keys = k_ref[rows, own]
            keys_fold = jnp.concatenate([k_ref[rows, left], k_ref[rows, right]], axis=0)
            top = None
            for part, (a, b) in enumerate(((keys, query), (keys_fold, query_fold))):
                raw = tn(a, b)
                for c in range(0, WIN, CHUNK):
                    block = raw[c : c + CHUNK] + bias_ref[w, part * WIN + c : part * WIN + c + CHUNK, :]
                    work_ref[part * WIN + c : part * WIN + c + CHUNK, :] = block
                    for r in range(0, CHUNK, 8):
                        piece = block[r : r + 8]
                        top = piece if top is None else jnp.maximum(top, piece)
            return jnp.max(top, axis=0, keepdims=True)

        def second_pass(work_ref, top, low_ref):
            for c in range(0, 2 * WIN, CHUNK):
                e = jnp.exp2(work_ref[c : c + CHUNK, :] - top)
                work_ref[c : c + CHUNK, :] = e
                low_ref[c : c + CHUNK, :] = e.astype(BF16)

        def mix(w, v_ref, rows, low_ref, head_width):
            left, own, right, early, late, _ = rows_of(w)
            values = v_ref[rows, own]
            values_fold = jnp.concatenate([v_ref[rows, left], v_ref[rows, right]], axis=0)
            mixed = nn(values, low_ref[:WIN, :])
            side = nn(values_fold, low_ref[WIN:, :])
            n = values.shape[0]
            mixed = mixed + early * side[:n] + late * side[n:]
            inverse = 1.0 / mixed[head_width : head_width + 1]
            return mixed[: -TAIL if head_width == HD_T else n] * inverse, inverse

        units = [(w, h) for w in range(windows) for h in range(2)]
        state = {}

        def refs(u):
            w, h = units[u]
            head = 2 * pair + h
            t_rows = pl.ds(pl.multiple_of(head * HD_T, HD_T), HD_T)
            s_rows = pl.ds(pl.multiple_of(head * PAD, PAD), PAD)
            v_rows = pl.ds(pl.multiple_of(head * (HD_T + TAIL), TAIL), HD_T + TAIL)
            slot = u % SLOTS
            return w, h, t_rows, s_rows, v_rows, work_ref.at[2 * slot], work_ref.at[2 * slot + 1], low_ref.at[slot]

        def score_stage(u):
            w, h, t_rows, s_rows, _, work_t, work_s, _ = refs(u)
            state[u] = [
                first_pass(w, tq_ref, tk_ref, t_rows, work_t),
                first_pass(w, sq_ref, skv_ref.at[0], s_rows, work_s),
            ]

        def power_stage(u):
            w, h, _, _, _, work_t, work_s, low_t = refs(u)
            second_pass(work_t, state[u][0], low_t)
            second_pass(work_s, state[u][1], e_out.at[w, h])

        def mix_stage(u):
            w, h, t_rows, s_rows, v_rows, _, _, low_t = refs(u)
            left = rows_of(w)[0]
            t_mixed, t_inv = mix(w, tv_ref, v_rows, low_t, HD_T)
            s_mixed, s_inv = mix(w, skv_ref.at[1], s_rows, e_out.at[w, h], SLOT_ONE)
            tctx_ref[t_rows, left] = t_mixed.astype(BF16)
            sctx_ref[s_rows, left] = s_mixed
            state[u] = [t_inv, s_inv]

        def gap_stage(u):
            w, h, _, _, _, work_t, work_s, _ = refs(u)
            left, _, _, _, _, filled = rows_of(w)
            t_inv, s_inv = state.pop(u)
            width = 2.0 * HEADS * HD_T
            scale_s = (width * filled) * s_inv * s_inv
            scale_t = (width * filled) * s_inv * t_inv
            square = jnp.zeros((8, WIN), F32)
            cross = jnp.zeros((8, WIN), F32)
            for c in range(0, 2 * WIN, CHUNK):
                s = work_s[c : c + CHUNK, :]
                gap = s * scale_s - work_t[c : c + CHUNK, :] * scale_t
                g_out[w, h, c : c + CHUNK, :] = gap.astype(BF16)
                for r in range(0, CHUNK, 8):
                    piece = gap[r : r + 8]
                    square += piece * piece
                    cross += piece * s[r : r + 8]
            square = jnp.sum(square, axis=0, keepdims=True)
            cross = jnp.sum(cross, axis=0, keepdims=True)
            back = 1.0 / (s_inv * width)
            stats_ref[pair, h : h + 1, left] = s_inv
            stats_ref[pair, 2 + h : 3 + h, left] = cross
            loss_ref[0:1, left] += square * back * back

        last = len(units)
        for u in range(last + 2):
            if u < last:
                score_stage(u)
            if 0 <= u - 1 < last:
                power_stage(u - 1)
            if 0 <= u - 2 < last:
                mix_stage(u - 2)
                gap_stage(u - 2)


    lax.fori_loop(0, PAIRS, one_pair, 0)
    for pair in range(PAIRS):
        for c in stores(pair, range(0 if pair >= PAIRS - 2 else 2, 4)):
            c.wait()
    for c in finals:
        c.wait()


def attend(mask, lengths, xt, xs, wtq, wtk, wtv, wq, wk, wv):
    slots, width_t = xt.shape
    width_s = xs.shape[0]
    windows = slots // WIN
    row_windows = mask.shape[1] // WIN
    padded = HEADS * PAD
    extended = slots + 2 * WIN
    sds = jax.ShapeDtypeStruct
    anywhere = pl.BlockSpec(memory_space=pl.ANY)
    saved = (windows, HEADS, 2 * WIN, WIN)
    return pl.pallas_call(
        partial(attend_kernel, windows, row_windows),
        out_shape=(
            sds((PAIRS, 8, slots), F32),
            sds((8, slots), F32),
            sds((8, slots), F32),
            sds((width_t, slots), BF16),
            sds((padded, slots), F32),
            sds((padded, slots), BF16),
            sds((2, padded, extended), BF16),
            sds(saved, BF16),
            sds(saved, BF16),
        ),
        in_specs=[VMEM, VMEM, anywhere, VMEM] + [anywhere] * 3 + [VMEM] * 3,
        out_specs=[VMEM] * 3 + [anywhere] * 6,
        scratch_shapes=[
            pltpu.VMEM((extended, width_t), BF16),
            pltpu.VMEM((2, width_s, WIN), BF16),
            pltpu.VMEM((3, width_t, width_t), BF16),
            pltpu.VMEM((windows, 2 * WIN, WIN), F32),
            pltpu.VMEM((3, padded, width_s), BF16),
            pltpu.VMEM((width_t, slots), BF16),
            pltpu.VMEM((width_t, extended), BF16),
            pltpu.VMEM((HEADS * (HD_T + TAIL), extended), BF16),
            pltpu.VMEM((padded, slots), BF16),
            pltpu.VMEM((2, padded, extended), BF16),
            pltpu.VMEM((width_t, slots), BF16),
            pltpu.VMEM((padded, slots), F32),
            pltpu.VMEM((2, windows, 2, 2 * WIN, WIN), BF16),
            pltpu.VMEM((2, windows, 2, 2 * WIN, WIN), BF16),
            pltpu.VMEM((2 * SLOTS, 2 * WIN, WIN), F32),
            pltpu.VMEM((SLOTS, 2 * WIN, WIN), BF16),
            pltpu.SemaphoreType.DMA((4,)),
            pltpu.SemaphoreType.DMA((2, 2)),
            pltpu.SemaphoreType.DMA((2, 2)),
            pltpu.SemaphoreType.DMA((2,)),
            pltpu.SemaphoreType.DMA((4, PAIRS)),
        ],
        compiler_params=pltpu.CompilerParams(
            vmem_limit_bytes=BIG, collective_id=1, has_side_effects=True
        ),
    )(mask, lengths, xt, xs, wtq, wtk, wtv, wq, wk, wv)


def normalize(values, gain, shift):
    n = values.shape[0]
    center = values - jnp.sum(values, axis=0, keepdims=True) * (1.0 / n)
    rscale = lax.rsqrt(jnp.sum(center * center, axis=0, keepdims=True) * (1.0 / n) + EPSILON)
    unit = center * rscale
    return unit * gain + shift, unit, rscale


def normalize_back(grad, unit, rscale, gain):
    n = grad.shape[0]
    scaled = grad * gain
    first = jnp.sum(scaled, axis=0, keepdims=True) * (1.0 / n)
    second = jnp.sum(scaled * unit, axis=0, keepdims=True) * (1.0 / n)
    return rscale * (scaled - first - unit * second)


def fold_lanes(values):
    total = values[:, :128]
    for at in range(128, values.shape[1], 128):
        total = total + values[:, at : at + 128]
    return total


ROOT_HALF = 0.7071067811865476
ROOT_PI = 0.3989422804014327


def dense_kernel(
    inner_pad,
    xt_ref,
    tctx_ref,
    xs_ref,
    sctx_ref,
    stats_ref,
    rows_ref,
    loss_ref,
    vec_t_ref,
    vec_s_ref,
    vec_b_ref,
    two_ref,
    tin_ref,
    tout_ref,
    wo_ref,
    w1_ref,
    w2_ref,
    wh_ref,
    out_ref,
    dctx_ref,
    dres_ref,
    pack_ref,
    ghid_ref,
    gouter_ref,
    ginner_ref,
    gwo_ref,
    gvec_ref,
    col_t_ref,
    col_s_ref,
    col_b_ref,
    wop_ref,
    act_ref,
    slope_ref,
):
    step = pl.program_id(0)
    width_s, units_s = w1_ref.shape
    width_t, units_t = tin_ref.shape
    tile = xt_ref.shape[0]

    @pl.when(step == 0)
    def _():
        col_t_ref[...] = jnp.transpose(vec_t_ref[...])
        col_s_ref[...] = jnp.transpose(vec_s_ref[...])
        col_b_ref[...] = jnp.transpose(vec_b_ref[...])
        wop_ref[...] = nn(pad_heads(), wo_ref[...]).astype(BF16)
        ghid_ref[...] = jnp.zeros_like(ghid_ref)
        gouter_ref[...] = jnp.zeros_like(gouter_ref)
        ginner_ref[...] = jnp.zeros_like(ginner_ref)
        gwo_ref[...] = jnp.zeros_like(gwo_ref)
        gvec_ref[...] = jnp.zeros_like(gvec_ref)
        act_ref[units_s:, :] = jnp.ones((inner_pad - units_s, tile), BF16)

    col_t = lambda k: col_t_ref[:, k : k + 1]
    col_s = lambda k: col_s_ref[:, k : k + 1]
    start = jnp.transpose(xt_ref[...]).astype(F32) + tn(two_ref[...], tctx_ref[...])
    t_normed = normalize(start, col_t(0), col_t(1))[0]
    t_low = t_normed.astype(BF16)
    t_sum = t_normed
    for at in range(0, units_t, width_t):
        pre = tn(tin_ref[:, at : at + width_t], t_low)
        active = (0.5 * pre * (1.0 + lax.erf(pre * ROOT_HALF))).astype(BF16)
        t_sum = t_sum + tn(tout_ref[at : at + width_t, :], active)
    target = normalize(t_sum, col_t(2), col_t(3))[0]
    gain_one, shift_one, b_outer, gain_two, shift_two = (col_s(k) for k in range(5))
    context = sctx_ref[...]
    context_low = context.astype(BF16)
    normed, unit_one, rscale_one = normalize(
        xs_ref[...].astype(F32) + tn(wop_ref[...], context_low), gain_one, shift_one
    )
    normed_low = normed.astype(BF16)
    pre = tn(w1_ref[...], normed_low) + col_b_ref[:, 0:1]
    half = 0.5 * (1.0 + lax.erf(pre * ROOT_HALF))
    slope_ref[...] = half + pre * (ROOT_PI * jnp.exp(-0.5 * pre * pre))
    act_ref[:units_s, :] = (pre * half).astype(BF16)
    student, unit_two, rscale_two = normalize(
        normed + nn(w2_ref[...], act_ref[:units_s, :]) + b_outer, gain_two, shift_two
    )
    student_low = student.astype(BF16)
    out_ref[...] = student_low
    gap = tn(wh_ref[...], student_low) - target
    filled = rows_ref[2:3, :]
    masked = filled * gap
    d_proj = (2.0 * masked).astype(BF16)
    ghid_ref[...] += nt(student_low, d_proj)
    d_student = nn(wh_ref[...], d_proj)
    d_two = normalize_back(d_student, unit_two, rscale_two, gain_two)
    d_outer = d_two.astype(BF16)
    gouter_ref[...] += nt(d_outer, act_ref[...])
    d_inner = (tn(w2_ref[...], d_outer) * slope_ref[...]).astype(BF16)
    ones = jnp.ones((8, tile), BF16)
    ginner_ref[:width_s, :units_s] += nt(normed_low, d_inner)
    ginner_ref[width_s:, :units_s] += nt(ones, d_inner)
    d_normed = nn(w1_ref[...], d_inner) + d_two
    d_one = normalize_back(d_normed, unit_one, rscale_one, gain_one)
    dres_ref[...] = d_one
    d_att = d_one.astype(BF16)
    gwo_ref[...] += nt(context_low, d_att)
    d_context = nn(wop_ref[...], d_att)
    row = lax.broadcasted_iota(jnp.int32, (PAD, tile), 0)
    for head in range(HEADS):
        pair, h = head // 2, head % 2
        inverse = stats_ref[pair, h : h + 1, :]
        cross = stats_ref[pair, 2 + h : 3 + h, :]
        rows = slice(head * PAD, (head + 1) * PAD)
        low = (d_context[rows] * inverse).astype(BF16).astype(F32)
        delta = -jnp.sum(low * context[rows], axis=0, keepdims=True) - inverse * cross
        high = delta.astype(BF16).astype(F32)
        rest = delta - high
        middle = rest.astype(BF16).astype(F32)
        low = jnp.where(row == SLOT_ONE, high, low)
        low = jnp.where(row == SLOT_ONE + 1, middle, low)
        low = jnp.where(row == SLOT_ONE + 2, rest - middle, low)
        dctx_ref[rows, :] = low.astype(BF16)
    for k, values in enumerate((d_normed * unit_one, d_normed, d_student * unit_two, d_student)):
        gvec_ref[:width_s, k * 128 : (k + 1) * 128] += fold_lanes(values)
    square = fold_lanes(masked * gap)
    gvec_ref[width_s : width_s + 8, :128] += jnp.sum(square.reshape(-1, 8, 128), axis=0)

    @pl.when(step == pl.num_programs(0) - 1)
    def _():
        low = lambda v: v.astype(BF16)
        pack_ref[...] = jnp.zeros_like(pack_ref)
        pack_ref[:width_s, :] = low(gouter_ref[...])
        pack_ref[BLOCK : BLOCK + width_s + 8, :] = low(ginner_ref[...])
        pack_ref[2 * BLOCK : 2 * BLOCK + width_s, :width_t] = low(ghid_ref[...])
        pack_ref[2 * BLOCK : 2 * BLOCK + width_s, width_t : width_t + width_s] = low(
            tn(pad_heads(), low(gwo_ref[...]))
        )
        lane = lax.broadcasted_iota(jnp.int32, (width_s, 128), 1)
        sums = jnp.zeros((width_s, 128), F32)
        for k in range(4):
            total = jnp.sum(gvec_ref[:width_s, k * 128 : (k + 1) * 128], axis=1, keepdims=True)
            sums = jnp.where(lane == k, total, sums)
        pack_ref[2 * BLOCK : 2 * BLOCK + width_s, SUMS_AT : SUMS_AT + 128] = low(sums)
        square = gvec_ref[width_s : width_s + 8, :128]
        row = lax.broadcasted_iota(jnp.int32, (8, 128), 0)
        for c in range(loss_ref.shape[1] // 128):
            square += jnp.where(row == c % 8, width_t * loss_ref[0:1, c * 128 : (c + 1) * 128], 0.0)
        pack_ref[2 * BLOCK + width_s : 2 * BLOCK + width_s + 8, :128] = low(square)


def dense(packed_rows, xt, tctx, xs, sctx, stats, rows, loss_rows, vec_t, vec_s, vec_b, two, tin, tout, wo, w1, w2, wh):
    slots, width_t = xt.shape
    width_s, units_s = w1.shape
    tile = 2 * WIN
    padded = HEADS * PAD
    inner_pad = -(-units_s // 128) * 128
    once = lambda a: pl.BlockSpec(a.shape, lambda i: (0,) * a.ndim, pipeline_mode=pl.Buffered(1))
    tiled = lambda n: pl.BlockSpec((n, tile), lambda i: (0, i))
    fixed = lambda *shape: pl.BlockSpec(shape, lambda i: (0,) * len(shape))
    sds = jax.ShapeDtypeStruct
    gshapes = [
        (width_s, width_t),
        (width_s, inner_pad),
        (width_s + 8, inner_pad),
        (padded, width_s),
        (width_s + 8, 512),
    ]
    return pl.pallas_call(
        partial(dense_kernel, inner_pad),
        grid=(slots // tile,),
        out_shape=[
            sds((width_s, slots), BF16),
            sds((padded, slots), BF16),
            sds((width_s, slots), F32),
            sds((packed_rows, inner_pad), BF16),
        ],
        in_specs=[
            pl.BlockSpec((tile, width_t), lambda i: (i, 0)),
            tiled(width_t),
            tiled(width_s),
            tiled(padded),
            pl.BlockSpec((PAIRS, 8, tile), lambda i: (0, 0, i)),
            tiled(8),
        ]
        + [once(a) for a in (loss_rows, vec_t, vec_s, vec_b, two, tin, tout, wo, w1, w2, wh)],
        out_specs=[tiled(width_s), tiled(padded), tiled(width_s), fixed(packed_rows, inner_pad)],
        scratch_shapes=[pltpu.VMEM(g, F32) for g in gshapes]
        + [
            pltpu.VMEM((width_t, 8), F32),
            pltpu.VMEM((width_s, 8), F32),
            pltpu.VMEM((units_s, 8), F32),
            pltpu.VMEM((padded, width_s), BF16),
            pltpu.VMEM((inner_pad, tile), BF16),
            pltpu.VMEM((units_s, tile), F32),
        ],
        compiler_params=pltpu.CompilerParams(vmem_limit_bytes=BIG, dimension_semantics=("arbitrary",)),
    )(xt, tctx, xs, sctx, stats, rows, loss_rows, vec_t, vec_s, vec_b, two, tin, tout, wo, w1, w2, wh)


def group_sizes():
    seq = lax.axis_size("seq")
    core = 2 if seq % 2 == 0 else 1
    chain = 4 if seq // core % 4 == 0 else 1
    return {"core": core, "batch": lax.axis_size("batch"), "chain": chain, "outer": seq // core // chain}


class Group:
    def __init__(self, name):
        batch, seq = lax.axis_index("batch"), lax.axis_index("seq")
        sizes = group_sizes()
        self.size = sizes[name]
        if name == "batch":
            self.place = batch
            self.device = lambda j: (j, seq)
        else:
            stride = {"core": 1, "chain": sizes["core"], "outer": sizes["core"] * sizes["chain"]}[name]
            self.place = seq // stride % self.size
            self.device = lambda j: (batch, seq + (j - self.place) * stride)

    def other(self, k):
        return (self.place + k) % self.size


class Chain:
    def __init__(self, names, source, scratch):
        self.names, self.source = names, source
        self.groups = [Group(n) for n in names]
        count = len(names)
        self.outer = Group("outer")
        self.received, self.sums = scratch[:count], scratch[count : 2 * count]
        self.around, self.whole, self.send, self.arrive = scratch[2 * count :]
        rows = self.whole.shape[0]
        self.rows, self.base, base = [], [], 0
        for g in self.groups:
            self.base.append(base)
            rows //= g.size
            base = base + g.place * rows
            self.rows.append(rows)
        self.mine = base
        self.sem = 0
        self.pending = []

    @staticmethod
    def scratch(names, rows, lanes):
        received, sums, copies = [], [], 0
        total, sizes = rows, group_sizes()
        for size in (sizes[n] for n in names):
            rows = rows // size
            received.append(pltpu.VMEM((max(size - 1, 1), rows, lanes), BF16))
            sums.append(pltpu.VMEM((rows, lanes), BF16))
            copies += 2 * (size - 1)
        copies = max(copies + sizes["outer"] - 1, 1)
        return (
            received
            + sums
            + [
                pltpu.VMEM((max(sizes["outer"] - 1, 1), rows, lanes), BF16),
                pltpu.VMEM((total, lanes), BF16),
                pltpu.SemaphoreType.DMA((copies,)),
                pltpu.SemaphoreType.DMA((copies,)),
            ]
        )

    def copy(self, ends):
        at = self.sem
        self.sem += 1

        def form():
            source, target, device = ends()
            return pltpu.make_async_remote_copy(
                src_ref=source,
                dst_ref=target,
                send_sem=self.send.at[at],
                recv_sem=self.arrive.at[at],
                device_id=device,
                device_id_type=MESH,
            )

        form().start()
        self.pending.append(form)

    def scatter(self, k):
        g, rows = self.groups[k], self.rows[k]
        source = self.source if k == 0 else self.sums[k - 1]

        def ends(step):
            other = g.other(step)
            there = pl.ds(pl.multiple_of(other * rows, 16), rows)
            return source.at[there], self.received[k].at[step - 1], g.device(other)

        for step in range(1, g.size):
            self.copy(partial(ends, step))

    def wait(self):
        for form in self.pending:
            form().wait()
        self.pending = []

    def add(self, k):
        self.wait()
        g, rows = self.groups[k], self.rows[k]
        source = self.source if k == 0 else self.sums[k - 1]
        total = source[pl.ds(pl.multiple_of(g.place * rows, 16), rows), :].astype(F32)
        for step in range(1, g.size):
            total = total + self.received[k][step - 1].astype(F32)
        total = total.astype(BF16)
        if k < len(self.groups) - 1 or self.outer.size > 1:
            self.sums[k][...] = total
        if k == len(self.groups) - 1:
            if self.outer.size > 1:
                total = self.exchange(total)
            self.whole[pl.ds(pl.multiple_of(self.mine, 16), rows), :] = total

    def exchange(self, total):
        g = self.outer

        def ends(step):
            return self.sums[-1], self.around.at[step - 1], g.device(g.other(step))

        for step in range(1, g.size):
            self.copy(partial(ends, step))
        self.wait()
        total = total.astype(F32)
        for step in range(1, g.size):
            total = total + self.around[step - 1].astype(F32)
        return total.astype(BF16)

    def gather(self, k):
        g, rows = self.groups[k], self.rows[k]

        def ends(step):
            here = self.whole.at[pl.ds(pl.multiple_of(self.base[k] + g.place * rows, 16), rows)]
            return here, here, g.device(g.other(step))

        for step in range(1, g.size):
            self.copy(partial(ends, step))

    def advance(self, stage):
        count = len(self.groups)
        if 0 < stage <= count:
            self.add(stage - 1)
        else:
            self.wait()
        if stage < count:
            self.scatter(stage)
        elif stage < 2 * count:
            self.gather(2 * count - 1 - stage)


CHAINS = ((0, 896, ("core", "batch", "chain")), (896, 1280, ("core", "chain", "batch")))
LATE = ("core", "batch", "chain")


def back_kernel(
    windows,
    sq_ref,
    skv_ref,
    dctx_ref,
    e_ref,
    g_ref,
    rows_ref,
    pack_ref,
    xs_ref,
    dres_ref,
    wq_ref,
    wk_ref,
    wv_ref,
    dx_ref,
    early_ref,
    late_ref,
    dq_ref,
    dkv_ref,
    give_ref,
    take_ref,
    qkv_ref,
    halo_send,
    halo_arrive,
    out_sem,
    *scratch,
):
    step = pl.program_id(0)
    w = (windows - step) % windows
    slots = windows * WIN
    width_s = xs_ref.shape[0]
    batch, seq = lax.axis_index("batch"), lax.axis_index("seq")
    peers = lax.axis_size("seq")
    chains, used = [], 0
    for first, last, names in CHAINS:
        size = 2 * len(names) + 4
        chains.append(Chain(names, pack_ref.at[:, first:last], scratch[used : used + size]))
        used += size
    late = Chain(LATE, qkv_ref, scratch[used:])
    first_seq, last_seq = seq == 0, seq == peers - 1

    def halo(side):
        return pltpu.make_async_remote_copy(
            src_ref=give_ref.at[side],
            dst_ref=take_ref.at[1 - side],
            send_sem=halo_send.at[side],
            recv_sem=halo_arrive.at[1 - side],
            device_id=(batch, seq - 1 + 2 * side),
            device_id_type=MESH,
        )

    @pl.when(step == 0)
    def _():
        dkv_ref[...] = jnp.zeros_like(dkv_ref)
        take_ref[...] = jnp.zeros_like(take_ref)
        qkv_ref[...] = jnp.zeros_like(qkv_ref)
        barrier = pltpu.get_barrier_semaphore()
        count = 0
        for g in (Group(n) for n in LATE + ("outer",)):
            for k in range(1, g.size):
                pl.semaphore_signal(barrier, inc=1, device_id=g.device(g.other(k)), device_id_type=MESH)
                count += 1

        for move in (1, peers - 1):
            pl.semaphore_signal(
                barrier, inc=1, device_id=(batch, (seq + move) % peers), device_id_type=MESH
            )
        pl.semaphore_wait(barrier, count + 2)

        for c in chains:
            c.advance(0)

    at = pl.multiple_of(w * WIN, WIN)
    left = pl.ds(at, WIN)
    own = pl.ds(pl.multiple_of(at + WIN, WIN), WIN)
    right = pl.ds(pl.multiple_of(at + 2 * WIN, WIN), WIN)
    early_row, late_row = rows_ref[0:1, left], rows_ref[1:2, left]
    early_low, late_low = early_row.astype(BF16), late_row.astype(BF16)

    def one_head(head):
        rows = pl.ds(pl.multiple_of(head * PAD, PAD), PAD)
        query, grad = sq_ref[rows, left], dctx_ref[rows, left]
        stacked = lambda a: jnp.concatenate([a * early_low, a * late_low], axis=0)
        query_fold, grad_fold = stacked(query), stacked(grad)
        beside = lambda k: jnp.concatenate([skv_ref[k, rows, left], skv_ref[k, rows, right]], axis=0)
        keys_fold, values_fold = beside(0), beside(1)
        keys, values = skv_ref[0, rows, own], skv_ref[1, rows, own]
        e_own, e_side = e_ref[0, head, :WIN, :], e_ref[0, head, WIN:, :]
        d_own = (e_own.astype(F32) * (tn(values, grad) + g_ref[0, head, :WIN, :].astype(F32))).astype(BF16)
        d_side = (
            e_side.astype(F32) * (tn(values_fold, grad_fold) + g_ref[0, head, WIN:, :].astype(F32))
        ).astype(BF16)
        side = nn(keys_fold, d_side)
        d_query = nn(keys, d_own) + early_row * side[:PAD] + late_row * side[PAD:]
        dq_ref[rows, left] = (d_query * HD_S**-0.5).astype(BF16)
        for k, (a, a_fold, b, b_fold, scale) in enumerate(
            ((query, query_fold, d_own, d_side, 1.0 / LOG2E), (grad, grad_fold, e_own, e_side, None))
        ):
            fix = (lambda v: v * scale) if scale else (lambda v: v)
            side = fix(nt(a_fold, b_fold))
            dkv_ref[k, rows, own] += fix(nt(a, b))
            dkv_ref[k, rows, left] += side[:PAD]
            dkv_ref[k, rows, right] += side[PAD:]

    def body(pair, carry):
        one_head(2 * pair)
        one_head(2 * pair + 1)
        return carry

    def send_halo():
        for side, lanes in ((0, slice(0, WIN)), (1, slice(WIN + slots, 2 * WIN + slots))):
            give_ref[side] = dkv_ref[:, :, lanes].astype(BF16)

        @pl.when(jnp.logical_not(first_seq))
        def _():
            halo(0).start()

        @pl.when(jnp.logical_not(last_seq))
        def _():
            halo(1).start()

    def advance(stage):
        def run():
            for c in chains:
                c.advance(stage)

        return run

    half = PAIRS // 2
    plan = {(0, 0): [advance(1)], (1, 1): [advance(2), send_halo], (2, 1): [advance(3)], (3, 1): [advance(4)]}
    for part in range(2):
        lax.fori_loop(part * half, (part + 1) * half, body, 0)
        for k in range(windows):
            for action in plan.get((k, part), []):
                pl.when(step == k)(action)

    @pl.when(step == windows - 1)
    def _():
        @pl.when(jnp.logical_not(first_seq))
        def _():
            halo(0).wait_send()
            halo(1).wait_recv()

        @pl.when(jnp.logical_not(last_seq))
        def _():
            halo(1).wait_send()
            halo(0).wait_recv()

        spot = pad_heads()
        plains = []
        for k in range(3):
            if k == 0:
                grad = dq_ref[...]
            else:
                mine = dkv_ref[k - 1, :, WIN : WIN + slots]
                first = mine[:, :WIN] + take_ref[0, k - 1].astype(F32)
                last = mine[:, slots - WIN :] + take_ref[1, k - 1].astype(F32)
                grad = jnp.concatenate([first, mine[:, WIN : slots - WIN], last], axis=1).astype(BF16)
            plain = tn(spot, grad).astype(BF16)
            plains.append(plain)
            qkv_ref[k * BLOCK : k * BLOCK + width_s, :width_s] = nt(xs_ref[...], plain).astype(BF16)
        late.advance(0)
        total = dres_ref[...]
        for w_ref, plain in zip((wq_ref, wk_ref, wv_ref), plains):
            total = total + nn(w_ref[...], plain)
        dx_ref[...] = total.astype(BF16)
        late.advance(1)
        for c in chains:
            c.advance(5)
        late.advance(2)
        late.advance(3)
        for c in chains:
            c.advance(6)
        copies = [
            pltpu.make_async_copy(c.whole, early_ref.at[:, first:last], out_sem.at[n])
            for n, (c, (first, last, _)) in enumerate(zip(chains, CHAINS))
        ]
        for c in copies:
            c.start()
        late.advance(4)
        late.advance(5)
        late.advance(6)
        copies.append(pltpu.make_async_copy(late.whole, late_ref, out_sem.at[len(chains)]))
        copies[-1].start()
        for c in copies:
            c.wait()


def back(sq, skv, dctx, e, g, rows, pack, xs, dres, wq, wk, wv):
    padded, slots = sq.shape
    windows = slots // WIN
    width_s = xs.shape[0]
    packed_rows = pack.shape[0]
    whole = lambda a: pl.BlockSpec(a.shape, lambda i: (0,) * a.ndim, pipeline_mode=pl.Buffered(1))
    saved = pl.BlockSpec((1, HEADS, 2 * WIN, WIN), lambda i: ((windows - i) % windows, 0, 0, 0))
    anywhere = pl.BlockSpec(memory_space=pl.ANY)
    scratch = [
        pltpu.VMEM((padded, slots), BF16),
        pltpu.VMEM((2, padded, slots + 2 * WIN), F32),
        pltpu.VMEM((2, 2, padded, WIN), BF16),
        pltpu.VMEM((2, 2, padded, WIN), BF16),
        pltpu.VMEM((packed_rows, QKV_LANES), BF16),
        pltpu.SemaphoreType.DMA((2,)),
        pltpu.SemaphoreType.DMA((2,)),
        pltpu.SemaphoreType.DMA((len(CHAINS) + 1,)),
    ]
    for first, last, names in CHAINS:
        scratch += Chain.scratch(names, packed_rows, last - first)
    scratch += Chain.scratch(LATE, packed_rows, QKV_LANES)
    return pl.pallas_call(
        partial(back_kernel, windows),
        grid=(windows,),
        out_shape=[
            jax.ShapeDtypeStruct((width_s, slots), BF16),
            jax.ShapeDtypeStruct(pack.shape, BF16),
            jax.ShapeDtypeStruct((packed_rows, QKV_LANES), BF16),
        ],
        in_specs=[whole(sq), whole(skv), whole(dctx), saved, saved]
        + [whole(a) for a in (rows, pack, xs, dres, wq, wk, wv)],
        out_specs=[pl.BlockSpec((width_s, slots), lambda i: (0, 0)), anywhere, anywhere],
        scratch_shapes=scratch,
        compiler_params=pltpu.CompilerParams(
            vmem_limit_bytes=BIG,
            dimension_semantics=("arbitrary",),
            collective_id=0,
            has_side_effects=True,
        ),
    )(sq, skv, dctx, e, g, rows, pack, xs, dres, wq, wk, wv)


def unpack_kernel(
    every,
    width_t,
    early_ref,
    late_ref,
    dx_in_ref,
    dx_ref,
    loss_ref,
    gq_ref,
    gk_ref,
    gv_ref,
    gwo_ref,
    ginner_ref,
    gouter_ref,
    ghid_ref,
    rows_ref,
    binner_ref,
):
    width_s = gq_ref.shape[0]
    units = binner_ref.shape[1]
    scale = 1.0 / every
    full = lambda v: v.astype(F32) * scale
    dx_ref[...] = dx_in_ref[...]
    for k, ref in enumerate((gq_ref, gk_ref, gv_ref)):
        ref[...] = full(late_ref[k * BLOCK : k * BLOCK + width_s, :width_s])
    gouter_ref[...] = full(early_ref[:width_s, :units])
    ginner_ref[...] = full(early_ref[BLOCK : BLOCK + width_s, :units])
    third = slice(2 * BLOCK, 2 * BLOCK + width_s)
    ghid_ref[...] = full(early_ref[third, :width_t])
    gwo_ref[...] = full(early_ref[third, width_t : width_t + width_s])
    binner_ref[...] = full(early_ref[BLOCK + width_s : BLOCK + width_s + 8, :units])[0:1]
    last = units // 128 * 128
    lane = lax.broadcasted_iota(jnp.int32, (width_s, 128), 1)
    columns = jnp.where(
        lane < 4,
        full(early_ref[third, SUMS_AT : SUMS_AT + 128]),
        full(early_ref[:width_s, last : last + 128]),
    )
    rows_ref[...] = jnp.transpose(columns)
    part = early_ref[2 * BLOCK + width_s : 2 * BLOCK + width_s + 8, :128].astype(F32)
    total = jnp.sum(jnp.sum(part, axis=0, keepdims=True), axis=1, keepdims=True)
    loss_ref[...] = total * (scale / width_t)


def unpack(every, width_t, units, early, late, dx):
    width_s = dx.shape[0]
    sds = lambda *shape: jax.ShapeDtypeStruct(shape, F32)
    shapes = [
        jax.ShapeDtypeStruct(dx.shape, BF16),
        sds(1, 1),
        sds(width_s, width_s),
        sds(width_s, width_s),
        sds(width_s, width_s),
        sds(width_s, width_s),
        sds(width_s, units),
        sds(width_s, units),
        sds(width_s, width_t),
        sds(128, width_s),
        sds(1, units),
    ]
    return pl.pallas_call(
        partial(unpack_kernel, every, width_t),
        out_shape=shapes,
        in_specs=[VMEM] * 3,
        out_specs=[VMEM] * len(shapes),
        compiler_params=pltpu.CompilerParams(vmem_limit_bytes=BIG),
    )(early, late, dx)


def local(
    inputs,
    teacher_input,
    filled_slot_mask,
    seg_lengths,
    query_weight,
    key_weight,
    value_weight,
    w_output,
    gain_one,
    shift_one,
    w_inner,
    b_inner,
    w_outer,
    b_outer,
    gain_two,
    shift_two,
    w_hidden,
    teacher_query_weight,
    teacher_key_weight,
    teacher_value_weight,
    teacher_output,
    teacher_gain_one,
    teacher_shift_one,
    teacher_inner,
    teacher_outer,
    teacher_gain_two,
    teacher_shift_two,
):
    xs = jnp.transpose(inputs[0])
    xt = teacher_input[0]
    slots, width_t = xt.shape
    width_s = xs.shape[0]
    units_s = w_inner.shape[1]
    stats, loss_rows, rows, tctx, sctx, sq, skv, e, g = attend(
        filled_slot_mask,
        seg_lengths,
        xt,
        xs,
        teacher_query_weight,
        teacher_key_weight,
        teacher_value_weight,
        query_weight,
        key_weight,
        value_weight,
    )
    fill = lambda n, *rows: jnp.concatenate([jnp.stack(rows), jnp.zeros((8 - len(rows), n), F32)])
    vec_t = fill(width_t, teacher_gain_one, teacher_shift_one, teacher_gain_two, teacher_shift_two)
    vec_s = fill(width_s, gain_one, shift_one, b_outer, gain_two, shift_two)
    vec_b = fill(units_s, b_inner)
    devices = lax.axis_size("seq") * lax.axis_size("batch")
    sizes = group_sizes()
    unit = 16 * sizes["core"] * sizes["batch"] * sizes["chain"]
    packed_rows = -(-3 * BLOCK // unit) * unit
    out, dctx, dres, pack = dense(
        packed_rows,
        xt,
        tctx,
        xs,
        sctx,
        stats,
        rows,
        loss_rows,
        vec_t,
        vec_s,
        vec_b,
        teacher_output,
        teacher_inner,
        teacher_outer,
        w_output,
        w_inner,
        jnp.transpose(w_outer),
        w_hidden,
    )
    dx, early, late = back(sq, skv, dctx, e, g, rows, pack, xs, dres, query_weight, key_weight, value_weight)
    dx, loss, gq, gk, gv, gwo, ginner, gouter, ghid, vectors, binner = unpack(
        slots * devices, width_t, units_s, early, late, dx
    )
    return (
        jnp.transpose(out)[None],
        jnp.transpose(dx)[None],
        loss[0, 0],
        gq,
        gk,
        gv,
        gwo,
        vectors[0],
        vectors[1],
        ginner,
        binner[0],
        jnp.transpose(gouter),
        vectors[units_s % 128],
        vectors[2],
        vectors[3],
        ghid,
    )


def solution(mesh):
    row_split = P("batch", "seq", None)
    return jax.shard_map(
        local,
        mesh=mesh,
        in_specs=(row_split, row_split, P("batch", None), P("batch", None)) + (P(),) * 23,
        out_specs=(row_split, row_split) + (P(),) * 14,
        check_vma=False,
    )
```

```python
from functools import partial

import jax
import jax.numpy as jnp
from jax import lax
from jax.experimental import pallas as pl
from jax.experimental.pallas import tpu as pltpu
from jax.sharding import PartitionSpec as P

HEADS = 12
HD_S = 26
HD_T = 64
WIN = 256
PAD = 32
SLOT_ONE = 26
PAIRS = HEADS // 2
CHUNK = 64
TAIL = 16
SLOTS = 4
BLOCK = 320
SUMS_AT = 1152
QKV_LANES = 384
MESH = pl.DeviceIdType.MESH
EPSILON = 1e-05
NEGATIVE = -1e30
LOG2E = 1.4426950408889634
F32 = jnp.float32
BF16 = jnp.bfloat16
VMEM = pl.BlockSpec(memory_space=pltpu.VMEM)
BIG = 60 << 20


def mm(left, right, dims):
    return lax.dot_general(left, right, ((dims[:1], dims[1:]), ((), ())), preferred_element_type=F32)


def nn(left, right):
    return mm(left, right, (1, 0))


def tn(left, right):
    return mm(left, right, (0, 0))


def nt(left, right):
    return mm(left, right, (1, 1))


def tt(left, right):
    return mm(left, right, (0, 1))


def pad_heads():
    row = lax.broadcasted_iota(jnp.int32, (HEADS * PAD, HEADS * HD_S), 0)
    col = lax.broadcasted_iota(jnp.int32, (HEADS * PAD, HEADS * HD_S), 1)
    spot = jnp.zeros((HEADS * PAD, HEADS * HD_S), F32)
    for head in range(HEADS):
        here = (row - head * PAD == col - head * HD_S) & (col >= head * HD_S) & (col < (head + 1) * HD_S)
        spot = jnp.where(here, 1.0, spot)
    return spot.astype(BF16)


def window_rows(mask_ref, lengths_ref, seq_index, windows, row_windows):
    lengths = lengths_ref[...].astype(F32)
    order = lax.broadcasted_iota(jnp.int32, lengths.shape, 1)
    lane = lax.broadcasted_iota(jnp.int32, (1, WIN), 1).astype(F32)
    out = []
    for j in range(windows + 2):
        number = seq_index * windows + (j - 1)
        inside = (number >= 0) & (number < row_windows)
        safe = jnp.clip(number, 0, row_windows - 1)
        start = jnp.sum(jnp.where(order < safe, lengths, 0.0), axis=1, keepdims=True)
        offset = start - (safe * WIN).astype(F32)
        late = (lane >= offset).astype(F32)
        filled = mask_ref[:, pl.ds(pl.multiple_of(safe * WIN, WIN), WIN)]
        filled = jnp.where(inside, filled.astype(F32), 0.0)
        out.append((late, filled))
    return out


def stack_rows(*rows):
    n = rows[0].shape[1]
    index = lax.broadcasted_iota(jnp.int32, (8, n), 0)
    block = jnp.zeros((8, n), F32)
    for k, row in enumerate(rows):
        block = jnp.where(index == k, row, block)
    return block.astype(BF16)


def attend_kernel(
    windows,
    row_windows,
    mask_ref,
    lengths_ref,
    xt_hbm,
    xs_ref,
    wtq_hbm,
    wtk_hbm,
    wtv_hbm,
    wq_ref,
    wk_ref,
    wv_ref,
    stats_ref,
    loss_ref,
    rows_ref,
    tctx_hbm,
    sctx_hbm,
    sq_hbm,
    skv_hbm,
    saved_e_hbm,
    saved_g_hbm,
    x_ref,
    xs_side_ref,
    wt_ref,
    bias_ref,
    wst_ref,
    tq_ref,
    tk_ref,
    tv_ref,
    sq_ref,
    skv_ref,
    tctx_ref,
    sctx_ref,
    e_ref,
    g_ref,
    work_ref,
    low_ref,
    in_sem,
    halo_send,
    halo_arrive,
    kv_sem,
    out_sem,
):
    slots = windows * WIN
    batch, seq = lax.axis_index("batch"), lax.axis_index("seq")
    peers = lax.axis_size("seq")
    has_left, has_right = seq > 0, seq < peers - 1
    width_t = x_ref.shape[1]
    extended = slots + 2 * WIN

    barrier = pltpu.get_barrier_semaphore()
    for move in (1, peers - 1):
        pl.semaphore_signal(barrier, inc=1, device_id=(batch, (seq + move) % peers), device_id_type=MESH)
    loads = [pltpu.make_async_copy(xt_hbm, x_ref.at[pl.ds(WIN, slots)], in_sem.at[0])]
    for k, w_hbm in enumerate((wtq_hbm, wtk_hbm, wtv_hbm)):
        loads.append(pltpu.make_async_copy(w_hbm, wt_ref.at[k], in_sem.at[1 + k]))
    for c in loads:
        c.start()
    pl.semaphore_wait(barrier, 2)

    def halo(side):
        device = (batch, seq - 1 + 2 * side)
        first = side * (slots - WIN)
        return [
            pltpu.make_async_remote_copy(
                src_ref=xt_hbm.at[pl.ds(first, WIN)],
                dst_ref=x_ref.at[pl.ds((1 - side) * (WIN + slots), WIN)],
                send_sem=halo_send.at[0, side],
                recv_sem=halo_arrive.at[0, 1 - side],
                device_id=device,
                device_id_type=MESH,
            ),
            pltpu.make_async_remote_copy(
                src_ref=xs_ref.at[:, pl.ds(first, WIN)],
                dst_ref=xs_side_ref.at[1 - side],
                send_sem=halo_send.at[1, side],
                recv_sem=halo_arrive.at[1, 1 - side],
                device_id=device,
                device_id_type=MESH,
            ),
        ]

    for side, present in ((0, has_left), (1, has_right)):

        @pl.when(present)
        def _():
            for c in halo(side):
                c.start()

        @pl.when(jnp.logical_not(present))
        def _():
            x_ref[side * (WIN + slots) : side * (WIN + slots) + WIN, :] = jnp.zeros((WIN, width_t), BF16)
            xs_side_ref[side] = jnp.zeros(xs_side_ref.shape[1:], BF16)

    info = window_rows(mask_ref, lengths_ref, seq, windows, row_windows)
    eye = lax.broadcasted_iota(jnp.int32, (WIN, WIN), 0) == lax.broadcasted_iota(jnp.int32, (WIN, WIN), 1)
    rows_ref[...] = jnp.zeros_like(rows_ref)
    for w in range(windows):
        late, filled = info[w + 1]
        late_l, filled_l = info[w]
        late_r, filled_r = info[w + 2]
        early = 1.0 - late
        here = slice(w * WIN, (w + 1) * WIN)
        rows_ref[0:1, here] = early
        rows_ref[1:2, here] = late
        rows_ref[2:3, here] = filled
        query = stack_rows(early, late)
        own = tn(stack_rows(NEGATIVE * (1.0 - early * filled), NEGATIVE * (1.0 - late * filled)), query)
        bias_ref[w, :WIN, :] = jnp.where(eye, 0.0, own)
        bias_ref[w, WIN:, :] = tn(
            stack_rows(
                NEGATIVE * (1.0 - late_l * filled_l), NEGATIVE * (1.0 - (1.0 - late_r) * filled_r)
            ),
            query,
        )
    loss_ref[...] = jnp.zeros_like(loss_ref)
    stats_ref[...] = jnp.zeros_like(stats_ref)
    spot = pad_heads()
    padded = HEADS * PAD
    row = lax.broadcasted_iota(jnp.int32, (padded, 1), 0) % PAD
    ones = (row >= SLOT_ONE) & (row < SLOT_ONE + 3)

    xs = xs_ref[...]
    for k, w_ref in enumerate((wq_ref, wk_ref, wv_ref)):
        wst_ref[k] = nt(spot, w_ref[...]).astype(BF16)
        made = nn(wst_ref[k], xs)
        if k == 0:
            sq_ref[...] = (made * (LOG2E * HD_S**-0.5)).astype(BF16)
        else:
            if k == 2:
                made = jnp.where(ones, 1.0, made)
            skv_ref[k - 1, :, WIN : WIN + slots] = made.astype(BF16)
    tail = (lax.broadcasted_iota(jnp.int32, (TAIL, extended), 0) == 0).astype(BF16)
    for head in range(HEADS):
        tv_ref[head * (HD_T + TAIL) + HD_T : (head + 1) * (HD_T + TAIL), :] = tail

    def put_values(made, first_head, lanes):
        for j in range(made.shape[0] // HD_T):
            at = (first_head + j) * (HD_T + TAIL)
            tv_ref[at : at + HD_T, lanes] = made[j * HD_T : (j + 1) * HD_T]

    part = width_t // 2
    loads[0].wait()
    for k in range(3):
        loads[1 + k].wait()
        for half in range(2):
            made = tt(wt_ref[k, :, half * part : (half + 1) * part], x_ref[WIN : WIN + slots, :])
            if k == 0:
                tq_ref[half * part : (half + 1) * part, :] = (made * (LOG2E * HD_T**-0.5)).astype(BF16)
            elif k == 1:
                tk_ref[half * part : (half + 1) * part, WIN : WIN + slots] = made.astype(BF16)
            else:
                put_values(made.astype(BF16), half * HEADS // 2, slice(WIN, WIN + slots))
    for side, present in ((0, has_left), (1, has_right)):

        @pl.when(present)
        def _():
            for sent, landed in zip(halo(side), halo(1 - side)):
                sent.wait_send()
                landed.wait_recv()

        lanes = slice(side * (WIN + slots), side * (WIN + slots) + WIN)
        for k in (1, 2):
            made = tt(wt_ref[k], x_ref[lanes, :]).astype(BF16)
            if k == 1:
                tk_ref[:, lanes] = made
            else:
                put_values(made, 0, lanes)
            made = nn(wst_ref[k], xs_side_ref[side])
            if k == 2:
                made = jnp.where(ones, 1.0, made)
            skv_ref[k - 1, :, lanes] = made.astype(BF16)
    finals = [
        pltpu.make_async_copy(sq_ref, sq_hbm, kv_sem.at[0]),
        pltpu.make_async_copy(skv_ref, skv_hbm, kv_sem.at[1]),
    ]
    for c in finals:
        c.start()

    def stores(pair, which):
        slot = pair % 2
        t_rows = pl.ds(pl.multiple_of(pair * 2 * HD_T, 2 * HD_T), 2 * HD_T)
        s_rows = pl.ds(pl.multiple_of(pair * 2 * PAD, 2 * PAD), 2 * PAD)
        heads = pl.ds(pair * 2, 2)
        ends = (
            (e_ref.at[slot], saved_e_hbm.at[:, heads]),
            (g_ref.at[slot], saved_g_hbm.at[:, heads]),
            (tctx_ref.at[t_rows], tctx_hbm.at[t_rows]),
            (sctx_ref.at[s_rows], sctx_hbm.at[s_rows]),
        )
        return [pltpu.make_async_copy(*ends[k], out_sem.at[k, pair]) for k in which]

    def one_pair(pair, carry):
        @pl.when(pair >= 2)
        def _():
            for c in stores(pair - 2, (0, 1)):
                c.wait()

        attend_pair(pair)
        for c in stores(pair, range(4)):
            c.start()
        return carry

    def attend_pair(pair):
        e_out, g_out = e_ref.at[pair % 2], g_ref.at[pair % 2]
        def rows_of(w):
            left = slice(w * WIN, (w + 1) * WIN)
            own = slice((w + 1) * WIN, (w + 2) * WIN)
            right = slice((w + 2) * WIN, (w + 3) * WIN)
            return left, own, right, rows_ref[0:1, left], rows_ref[1:2, left], rows_ref[2:3, left]

        def first_pass(w, q_ref, k_ref, rows, work_ref):
            left, own, right, early, late, _ = rows_of(w)
            query = q_ref[rows, left]
            query_fold = jnp.concatenate([query * early.astype(BF16), query * late.astype(BF16)], axis=0)
            keys = k_ref[rows, own]
            keys_fold = jnp.concatenate([k_ref[rows, left], k_ref[rows, right]], axis=0)
            top = None
            for part, (a, b) in enumerate(((keys, query), (keys_fold, query_fold))):
                raw = tn(a, b)
                for c in range(0, WIN, CHUNK):
                    block = raw[c : c + CHUNK] + bias_ref[w, part * WIN + c : part * WIN + c + CHUNK, :]
                    work_ref[part * WIN + c : part * WIN + c + CHUNK, :] = block
                    for r in range(0, CHUNK, 8):
                        piece = block[r : r + 8]
                        top = piece if top is None else jnp.maximum(top, piece)
            return jnp.max(top, axis=0, keepdims=True)

        def second_pass(work_ref, top, low_ref):
            for c in range(0, 2 * WIN, CHUNK):
                e = jnp.exp2(work_ref[c : c + CHUNK, :] - top)
                work_ref[c : c + CHUNK, :] = e
                low_ref[c : c + CHUNK, :] = e.astype(BF16)

        def mix(w, v_ref, rows, low_ref, head_width):
            left, own, right, early, late, _ = rows_of(w)
            values = v_ref[rows, own]
            values_fold = jnp.concatenate([v_ref[rows, left], v_ref[rows, right]], axis=0)
            mixed = nn(values, low_ref[:WIN, :])
            side = nn(values_fold, low_ref[WIN:, :])
            n = values.shape[0]
            mixed = mixed + early * side[:n] + late * side[n:]
            inverse = 1.0 / mixed[head_width : head_width + 1]
            return mixed[: -TAIL if head_width == HD_T else n] * inverse, inverse

        units = [(w, h) for w in range(windows) for h in range(2)]
        state = {}

        def refs(u):
            w, h = units[u]
            head = 2 * pair + h
            t_rows = pl.ds(pl.multiple_of(head * HD_T, HD_T), HD_T)
            s_rows = pl.ds(pl.multiple_of(head * PAD, PAD), PAD)
            v_rows = pl.ds(pl.multiple_of(head * (HD_T + TAIL), TAIL), HD_T + TAIL)
            slot = u % SLOTS
            return w, h, t_rows, s_rows, v_rows, work_ref.at[2 * slot], work_ref.at[2 * slot + 1], low_ref.at[slot]

        def score_stage(u):
            w, h, t_rows, s_rows, _, work_t, work_s, _ = refs(u)
            state[u] = [
                first_pass(w, tq_ref, tk_ref, t_rows, work_t),
                first_pass(w, sq_ref, skv_ref.at[0], s_rows, work_s),
            ]

        def power_stage(u):
            w, h, _, _, _, work_t, work_s, low_t = refs(u)
            second_pass(work_t, state[u][0], low_t)
            second_pass(work_s, state[u][1], e_out.at[w, h])

        def mix_stage(u):
            w, h, t_rows, s_rows, v_rows, _, _, low_t = refs(u)
            left = rows_of(w)[0]
            t_mixed, t_inv = mix(w, tv_ref, v_rows, low_t, HD_T)
            s_mixed, s_inv = mix(w, skv_ref.at[1], s_rows, e_out.at[w, h], SLOT_ONE)
            tctx_ref[t_rows, left] = t_mixed.astype(BF16)
            sctx_ref[s_rows, left] = s_mixed
            state[u] = [t_inv, s_inv]

        def gap_stage(u):
            w, h, _, _, _, work_t, work_s, _ = refs(u)
            left, _, _, _, _, filled = rows_of(w)
            t_inv, s_inv = state.pop(u)
            width = 2.0 * HEADS * HD_T
            scale_s = (width * filled) * s_inv * s_inv
            scale_t = (width * filled) * s_inv * t_inv
            square = jnp.zeros((8, WIN), F32)
            cross = jnp.zeros((8, WIN), F32)
            for c in range(0, 2 * WIN, CHUNK):
                s = work_s[c : c + CHUNK, :]
                gap = s * scale_s - work_t[c : c + CHUNK, :] * scale_t
                g_out[w, h, c : c + CHUNK, :] = gap.astype(BF16)
                for r in range(0, CHUNK, 8):
                    piece = gap[r : r + 8]
                    square += piece * piece
                    cross += piece * s[r : r + 8]
            square = jnp.sum(square, axis=0, keepdims=True)
            cross = jnp.sum(cross, axis=0, keepdims=True)
            back = 1.0 / (s_inv * width)
            stats_ref[pair, h : h + 1, left] = s_inv
            stats_ref[pair, 2 + h : 3 + h, left] = cross
            loss_ref[0:1, left] += square * back * back

        last = len(units)
        for u in range(last + 2):
            if u < last:
                score_stage(u)
            if 0 <= u - 1 < last:
                power_stage(u - 1)
            if 0 <= u - 2 < last:
                mix_stage(u - 2)
                gap_stage(u - 2)


    lax.fori_loop(0, PAIRS, one_pair, 0)
    for pair in range(PAIRS):
        for c in stores(pair, range(0 if pair >= PAIRS - 2 else 2, 4)):
            c.wait()
    for c in finals:
        c.wait()


def attend(mask, lengths, xt, xs, wtq, wtk, wtv, wq, wk, wv):
    slots, width_t = xt.shape
    width_s = xs.shape[0]
    windows = slots // WIN
    row_windows = mask.shape[1] // WIN
    padded = HEADS * PAD
    extended = slots + 2 * WIN
    sds = jax.ShapeDtypeStruct
    anywhere = pl.BlockSpec(memory_space=pl.ANY)
    saved = (windows, HEADS, 2 * WIN, WIN)
    return pl.pallas_call(
        partial(attend_kernel, windows, row_windows),
        out_shape=(
            sds((PAIRS, 8, slots), F32),
            sds((8, slots), F32),
            sds((8, slots), F32),
            sds((width_t, slots), BF16),
            sds((padded, slots), F32),
            sds((padded, slots), BF16),
            sds((2, padded, extended), BF16),
            sds(saved, BF16),
            sds(saved, BF16),
        ),
        in_specs=[VMEM, VMEM, anywhere, VMEM] + [anywhere] * 3 + [VMEM] * 3,
        out_specs=[VMEM] * 3 + [anywhere] * 6,
        scratch_shapes=[
            pltpu.VMEM((extended, width_t), BF16),
            pltpu.VMEM((2, width_s, WIN), BF16),
            pltpu.VMEM((3, width_t, width_t), BF16),
            pltpu.VMEM((windows, 2 * WIN, WIN), F32),
            pltpu.VMEM((3, padded, width_s), BF16),
            pltpu.VMEM((width_t, slots), BF16),
            pltpu.VMEM((width_t, extended), BF16),
            pltpu.VMEM((HEADS * (HD_T + TAIL), extended), BF16),
            pltpu.VMEM((padded, slots), BF16),
            pltpu.VMEM((2, padded, extended), BF16),
            pltpu.VMEM((width_t, slots), BF16),
            pltpu.VMEM((padded, slots), F32),
            pltpu.VMEM((2, windows, 2, 2 * WIN, WIN), BF16),
            pltpu.VMEM((2, windows, 2, 2 * WIN, WIN), BF16),
            pltpu.VMEM((2 * SLOTS, 2 * WIN, WIN), F32),
            pltpu.VMEM((SLOTS, 2 * WIN, WIN), BF16),
            pltpu.SemaphoreType.DMA((4,)),
            pltpu.SemaphoreType.DMA((2, 2)),
            pltpu.SemaphoreType.DMA((2, 2)),
            pltpu.SemaphoreType.DMA((2,)),
            pltpu.SemaphoreType.DMA((4, PAIRS)),
        ],
        compiler_params=pltpu.CompilerParams(
            vmem_limit_bytes=BIG, collective_id=1, has_side_effects=True
        ),
    )(mask, lengths, xt, xs, wtq, wtk, wtv, wq, wk, wv)


def normalize(values, gain, shift):
    n = values.shape[0]
    center = values - jnp.sum(values, axis=0, keepdims=True) * (1.0 / n)
    rscale = lax.rsqrt(jnp.sum(center * center, axis=0, keepdims=True) * (1.0 / n) + EPSILON)
    unit = center * rscale
    return unit * gain + shift, unit, rscale


def normalize_back(grad, unit, rscale, gain):
    n = grad.shape[0]
    scaled = grad * gain
    first = jnp.sum(scaled, axis=0, keepdims=True) * (1.0 / n)
    second = jnp.sum(scaled * unit, axis=0, keepdims=True) * (1.0 / n)
    return rscale * (scaled - first - unit * second)


def fold_lanes(values):
    total = values[:, :128]
    for at in range(128, values.shape[1], 128):
        total = total + values[:, at : at + 128]
    return total


ROOT_HALF = 0.7071067811865476
ROOT_PI = 0.3989422804014327


DENSE_IN = ("xt", "tctx", "two", "xs", "sctx", "tin", "tout", "wo", "w1", "w2", "wh")


def dense_kernel(
    xt_hbm,
    tctx_hbm,
    two_hbm,
    xs_hbm,
    sctx_hbm,
    tin_hbm,
    tout_hbm,
    wo_hbm,
    w1_hbm,
    w2_hbm,
    wh_hbm,
    stats_ref,
    rows_ref,
    loss_ref,
    t_gain_one_ref,
    t_shift_one_ref,
    t_gain_two_ref,
    t_shift_two_ref,
    gain_one_ref,
    shift_one_ref,
    b_outer_ref,
    gain_two_ref,
    shift_two_ref,
    b_inner_ref,
    out_hbm,
    dctx_hbm,
    dres_hbm,
    pack_hbm,
    xt_ref,
    tctx_ref,
    two_ref,
    xs_ref,
    sctx_ref,
    tin_ref,
    tout_ref,
    wo_ref,
    w1_ref,
    w2_ref,
    wh_ref,
    out_ref,
    dctx_ref,
    dres_ref,
    pack_ref,
    act_ref,
    slope_ref,
    in_sem,
    out_sem,
):
    sources = (
        xt_hbm, tctx_hbm, two_hbm, xs_hbm, sctx_hbm, tin_hbm, tout_hbm, wo_hbm, w1_hbm, w2_hbm, wh_hbm
    )
    targets = (xt_ref, tctx_ref, two_ref, xs_ref, sctx_ref, tin_ref, tout_ref, wo_ref, w1_ref, w2_ref, wh_ref)
    loads = {
        name: pltpu.make_async_copy(source, target, in_sem.at[k])
        for k, (name, source, target) in enumerate(zip(DENSE_IN, sources, targets))
    }
    for c in loads.values():
        c.start()
    width_s, units_s = w1_ref.shape
    width_t, units_t = tin_ref.shape
    slots = xt_ref.shape[0]
    low = lambda v: v.astype(BF16)
    stores = []

    def store(source, target):
        stores.append(pltpu.make_async_copy(source, target, out_sem.at[len(stores)]))
        stores[-1].start()

    def columns(*refs):
        n = refs[0].shape[0]
        index = lax.broadcasted_iota(jnp.int32, (8, n), 0)
        block = jnp.zeros((8, n), F32)
        for k, ref in enumerate(refs):
            block = jnp.where(index == k, ref[...].reshape(1, n), block)
        turned = jnp.transpose(block)
        return [turned[:, k : k + 1] for k in range(len(refs))]

    t_gain_one, t_shift_one, t_gain_two, t_shift_two = columns(
        t_gain_one_ref, t_shift_one_ref, t_gain_two_ref, t_shift_two_ref
    )
    gain_one, shift_one, b_outer, gain_two, shift_two = columns(
        gain_one_ref, shift_one_ref, b_outer_ref, gain_two_ref, shift_two_ref
    )
    (b_inner,) = columns(b_inner_ref)
    spot = pad_heads()
    pack_ref[...] = jnp.zeros_like(pack_ref)
    act_ref[units_s:, :] = jnp.ones((act_ref.shape[0] - units_s, slots), BF16)
    for name in ("xt", "tctx", "two"):
        loads[name].wait()
    start = jnp.transpose(xt_ref[...]).astype(F32) + tn(two_ref[...], tctx_ref[...])
    t_normed = normalize(start, t_gain_one, t_shift_one)[0]
    t_low = low(t_normed)
    t_sum = t_normed
    for name in ("xs", "sctx", "tin", "tout"):
        loads[name].wait()
    for at in range(0, units_t, width_t):
        pre = tn(tin_ref[:, at : at + width_t], t_low)
        active = low(0.5 * pre * (1.0 + lax.erf(pre * ROOT_HALF)))
        t_sum = t_sum + tn(tout_ref[at : at + width_t, :], active)
    target = normalize(t_sum, t_gain_two, t_shift_two)[0]
    for name in ("wo", "w1", "w2", "wh"):
        loads[name].wait()
    wop = low(nn(spot, wo_ref[...]))
    context = sctx_ref[...]
    context_low = low(context)
    normed, unit_one, rscale_one = normalize(
        xs_ref[...].astype(F32) + tn(wop, context_low), gain_one, shift_one
    )
    normed_low = low(normed)
    pre = tn(w1_ref[...], normed_low) + b_inner
    half = 0.5 * (1.0 + lax.erf(pre * ROOT_HALF))
    slope_ref[...] = half + pre * (ROOT_PI * jnp.exp(-0.5 * pre * pre))
    act_ref[:units_s, :] = low(pre * half)
    student, unit_two, rscale_two = normalize(
        normed + nn(w2_ref[...], act_ref[:units_s, :]) + b_outer, gain_two, shift_two
    )
    student_low = low(student)
    out_ref[...] = student_low
    store(out_ref, out_hbm)
    gap = tn(wh_ref[...], student_low) - target
    filled = rows_ref[2:3, :]
    masked = filled * gap
    d_proj = low(2.0 * masked)
    third = slice(2 * BLOCK, 2 * BLOCK + width_s)
    pack_ref[third, :width_t] = low(nt(student_low, d_proj))
    d_student = nn(wh_ref[...], d_proj)
    d_two = normalize_back(d_student, unit_two, rscale_two, gain_two)
    d_outer = low(d_two)
    pack_ref[:width_s, :] = low(nt(d_outer, act_ref[...]))
    store(pack_ref.at[:BLOCK], pack_hbm.at[:BLOCK])
    d_inner = low(tn(w2_ref[...], d_outer) * slope_ref[...])
    pack_ref[BLOCK : BLOCK + width_s, :units_s] = low(nt(normed_low, d_inner))
    pack_ref[BLOCK + width_s : BLOCK + width_s + 8, :units_s] = low(nt(jnp.ones((8, slots), BF16), d_inner))
    store(pack_ref.at[BLOCK : 2 * BLOCK], pack_hbm.at[BLOCK : 2 * BLOCK])
    d_normed = nn(w1_ref[...], d_inner) + d_two
    d_one = normalize_back(d_normed, unit_one, rscale_one, gain_one)
    dres_ref[...] = d_one
    store(dres_ref, dres_hbm)
    d_att = low(d_one)
    gwo = low(nt(context_low, d_att))
    pack_ref[third, width_t : width_t + width_s] = low(tn(spot, gwo))
    d_context = nn(wop, d_att)
    row = lax.broadcasted_iota(jnp.int32, (PAD, slots), 0)
    for head in range(HEADS):
        pair, h = head // 2, head % 2
        inverse = stats_ref[pair, h : h + 1, :]
        cross = stats_ref[pair, 2 + h : 3 + h, :]
        rows = slice(head * PAD, (head + 1) * PAD)
        part = low(d_context[rows] * inverse).astype(F32)
        delta = -jnp.sum(part * context[rows], axis=0, keepdims=True) - inverse * cross
        high = low(delta).astype(F32)
        rest = delta - high
        middle = low(rest).astype(F32)
        part = jnp.where(row == SLOT_ONE, high, part)
        part = jnp.where(row == SLOT_ONE + 1, middle, part)
        part = jnp.where(row == SLOT_ONE + 2, rest - middle, part)
        dctx_ref[rows, :] = low(part)
    store(dctx_ref, dctx_hbm)
    lane = lax.broadcasted_iota(jnp.int32, (width_s, 128), 1)
    sums = jnp.zeros((width_s, 128), F32)
    for k, values in enumerate((d_normed * unit_one, d_normed, d_student * unit_two, d_student)):
        sums = jnp.where(lane == k, jnp.sum(fold_lanes(values), axis=1, keepdims=True), sums)
    pack_ref[third, SUMS_AT : SUMS_AT + 128] = low(sums)
    square = jnp.sum(fold_lanes(masked * gap).reshape(-1, 8, 128), axis=0)
    row = lax.broadcasted_iota(jnp.int32, (8, 128), 0)
    for c in range(slots // 128):
        square += jnp.where(row == c % 8, width_t * loss_ref[0:1, c * 128 : (c + 1) * 128], 0.0)
    pack_ref[2 * BLOCK + width_s : 2 * BLOCK + width_s + 8, :128] = low(square)
    store(pack_ref.at[2 * BLOCK :], pack_hbm.at[2 * BLOCK :])
    for c in stores:
        c.wait()


def dense(packed_rows, big, small):
    xt, tctx, two, xs, sctx, tin, tout, wo, w1, w2, wh = big
    slots, width_t = xt.shape
    width_s, units_s = w1.shape
    padded = HEADS * PAD
    inner_pad = -(-units_s // 128) * 128
    sds = jax.ShapeDtypeStruct
    outs = [
        sds((width_s, slots), BF16),
        sds((padded, slots), BF16),
        sds((width_s, slots), F32),
        sds((packed_rows, inner_pad), BF16),
    ]
    anywhere = pl.BlockSpec(memory_space=pl.ANY)
    return pl.pallas_call(
        dense_kernel,
        out_shape=outs,
        in_specs=[anywhere] * len(big) + [VMEM] * len(small),
        out_specs=[anywhere] * len(outs),
        scratch_shapes=[pltpu.VMEM(a.shape, a.dtype) for a in big]
        + [pltpu.VMEM(a.shape, a.dtype) for a in outs]
        + [
            pltpu.VMEM((inner_pad, slots), BF16),
            pltpu.VMEM((units_s, slots), F32),
            pltpu.SemaphoreType.DMA((len(big),)),
            pltpu.SemaphoreType.DMA((6,)),
        ],
        compiler_params=pltpu.CompilerParams(vmem_limit_bytes=BIG),
    )(*big, *small)


def group_sizes():
    seq = lax.axis_size("seq")
    core = 2 if seq % 2 == 0 else 1
    chain = 4 if seq // core % 4 == 0 else 1
    return {"core": core, "batch": lax.axis_size("batch"), "chain": chain, "outer": seq // core // chain}


class Group:
    def __init__(self, name):
        batch, seq = lax.axis_index("batch"), lax.axis_index("seq")
        sizes = group_sizes()
        self.size = sizes[name]
        if name == "batch":
            self.place = batch
            self.device = lambda j: (j, seq)
        else:
            stride = {"core": 1, "chain": sizes["core"], "outer": sizes["core"] * sizes["chain"]}[name]
            self.place = seq // stride % self.size
            self.device = lambda j: (batch, seq + (j - self.place) * stride)

    def other(self, k):
        return (self.place + k) % self.size


class Chain:
    def __init__(self, names, source, scratch):
        self.names, self.source = names, source
        self.groups = [Group(n) for n in names]
        count = len(names)
        self.outer = Group("outer")
        self.received, self.sums = scratch[:count], scratch[count : 2 * count]
        self.around, self.whole, self.send, self.arrive = scratch[2 * count :]
        rows = self.whole.shape[0]
        self.rows, self.base, base = [], [], 0
        for g in self.groups:
            self.base.append(base)
            rows //= g.size
            base = base + g.place * rows
            self.rows.append(rows)
        self.mine = base
        self.sem = 0
        self.pending = []

    @staticmethod
    def scratch(names, rows, lanes):
        received, sums, copies = [], [], 0
        total, sizes = rows, group_sizes()
        for size in (sizes[n] for n in names):
            rows = rows // size
            received.append(pltpu.VMEM((max(size - 1, 1), rows, lanes), BF16))
            sums.append(pltpu.VMEM((rows, lanes), BF16))
            copies += 2 * (size - 1)
        copies = max(copies + sizes["outer"] - 1, 1)
        return (
            received
            + sums
            + [
                pltpu.VMEM((max(sizes["outer"] - 1, 1), rows, lanes), BF16),
                pltpu.VMEM((total, lanes), BF16),
                pltpu.SemaphoreType.DMA((copies,)),
                pltpu.SemaphoreType.DMA((copies,)),
            ]
        )

    def copy(self, ends):
        at = self.sem
        self.sem += 1

        def form():
            source, target, device = ends()
            return pltpu.make_async_remote_copy(
                src_ref=source,
                dst_ref=target,
                send_sem=self.send.at[at],
                recv_sem=self.arrive.at[at],
                device_id=device,
                device_id_type=MESH,
            )

        form().start()
        self.pending.append(form)

    def scatter(self, k):
        g, rows = self.groups[k], self.rows[k]
        source = self.source if k == 0 else self.sums[k - 1]

        def ends(step):
            other = g.other(step)
            there = pl.ds(pl.multiple_of(other * rows, 16), rows)
            return source.at[there], self.received[k].at[step - 1], g.device(other)

        for step in range(1, g.size):
            self.copy(partial(ends, step))

    def wait(self):
        for form in self.pending:
            form().wait()
        self.pending = []

    def add(self, k):
        self.wait()
        g, rows = self.groups[k], self.rows[k]
        source = self.source if k == 0 else self.sums[k - 1]
        total = source[pl.ds(pl.multiple_of(g.place * rows, 16), rows), :].astype(F32)
        for step in range(1, g.size):
            total = total + self.received[k][step - 1].astype(F32)
        total = total.astype(BF16)
        if k < len(self.groups) - 1 or self.outer.size > 1:
            self.sums[k][...] = total
        if k == len(self.groups) - 1:
            if self.outer.size > 1:
                total = self.exchange(total)
            self.whole[pl.ds(pl.multiple_of(self.mine, 16), rows), :] = total

    def exchange(self, total):
        g = self.outer

        def ends(step):
            return self.sums[-1], self.around.at[step - 1], g.device(g.other(step))

        for step in range(1, g.size):
            self.copy(partial(ends, step))
        self.wait()
        total = total.astype(F32)
        for step in range(1, g.size):
            total = total + self.around[step - 1].astype(F32)
        return total.astype(BF16)

    def gather(self, k):
        g, rows = self.groups[k], self.rows[k]

        def ends(step):
            here = self.whole.at[pl.ds(pl.multiple_of(self.base[k] + g.place * rows, 16), rows)]
            return here, here, g.device(g.other(step))

        for step in range(1, g.size):
            self.copy(partial(ends, step))

    def advance(self, stage):
        count = len(self.groups)
        if 0 < stage <= count:
            self.add(stage - 1)
        else:
            self.wait()
        if stage < count:
            self.scatter(stage)
        elif stage < 2 * count:
            self.gather(2 * count - 1 - stage)


EARLY = ((0, 768, ("core", "batch", "chain")), (768, 1280, ("core", "chain", "batch")))
LATE = ((0, 256, ("core", "batch", "chain")), (256, 384, ("core", "chain", "batch")))


def back_kernel(
    windows,
    sq_ref,
    skv_ref,
    dctx_ref,
    e_ref,
    g_ref,
    rows_ref,
    pack_ref,
    xs_ref,
    dres_ref,
    wq_ref,
    wk_ref,
    wv_ref,
    dx_ref,
    early_ref,
    late_ref,
    dq_ref,
    dkv_ref,
    give_ref,
    take_ref,
    qkv_ref,
    halo_send,
    halo_arrive,
    out_sem,
    *scratch,
):
    step = pl.program_id(0)
    w = (windows - step) % windows
    slots = windows * WIN
    width_s = xs_ref.shape[0]
    batch, seq = lax.axis_index("batch"), lax.axis_index("seq")
    peers = lax.axis_size("seq")
    chains, used = [], 0
    for source, cuts in ((pack_ref, EARLY), (qkv_ref, LATE)):
        for first, last, names in cuts:
            size = 2 * len(names) + 4
            chains.append(Chain(names, source.at[:, first:last], scratch[used : used + size]))
            used += size
    soon, late = chains[: len(EARLY)], chains[len(EARLY) :]
    first_seq, last_seq = seq == 0, seq == peers - 1

    def halo(side):
        return pltpu.make_async_remote_copy(
            src_ref=give_ref.at[side],
            dst_ref=take_ref.at[1 - side],
            send_sem=halo_send.at[side],
            recv_sem=halo_arrive.at[1 - side],
            device_id=(batch, seq - 1 + 2 * side),
            device_id_type=MESH,
        )

    @pl.when(step == 0)
    def _():
        dkv_ref[...] = jnp.zeros_like(dkv_ref)
        take_ref[...] = jnp.zeros_like(take_ref)
        qkv_ref[...] = jnp.zeros_like(qkv_ref)
        barrier = pltpu.get_barrier_semaphore()
        count = 0
        for g in (Group(n) for n in ("core", "batch", "chain", "outer")):
            for k in range(1, g.size):
                pl.semaphore_signal(barrier, inc=1, device_id=g.device(g.other(k)), device_id_type=MESH)
                count += 1

        for move in (1, peers - 1):
            pl.semaphore_signal(
                barrier, inc=1, device_id=(batch, (seq + move) % peers), device_id_type=MESH
            )
        pl.semaphore_wait(barrier, count + 2)

        for c in soon:
            c.advance(0)

    at = pl.multiple_of(w * WIN, WIN)
    left = pl.ds(at, WIN)
    own = pl.ds(pl.multiple_of(at + WIN, WIN), WIN)
    right = pl.ds(pl.multiple_of(at + 2 * WIN, WIN), WIN)
    early_row, late_row = rows_ref[0:1, left], rows_ref[1:2, left]
    early_low, late_low = early_row.astype(BF16), late_row.astype(BF16)

    def one_head(head):
        rows = pl.ds(pl.multiple_of(head * PAD, PAD), PAD)
        query, grad = sq_ref[rows, left], dctx_ref[rows, left]
        stacked = lambda a: jnp.concatenate([a * early_low, a * late_low], axis=0)
        query_fold, grad_fold = stacked(query), stacked(grad)
        beside = lambda k: jnp.concatenate([skv_ref[k, rows, left], skv_ref[k, rows, right]], axis=0)
        keys_fold, values_fold = beside(0), beside(1)
        keys, values = skv_ref[0, rows, own], skv_ref[1, rows, own]
        e_own, e_side = e_ref[0, head, :WIN, :], e_ref[0, head, WIN:, :]
        d_own = (e_own.astype(F32) * (tn(values, grad) + g_ref[0, head, :WIN, :].astype(F32))).astype(BF16)
        d_side = (
            e_side.astype(F32) * (tn(values_fold, grad_fold) + g_ref[0, head, WIN:, :].astype(F32))
        ).astype(BF16)
        side = nn(keys_fold, d_side)
        d_query = nn(keys, d_own) + early_row * side[:PAD] + late_row * side[PAD:]
        dq_ref[rows, left] = (d_query * HD_S**-0.5).astype(BF16)
        for k, (a, a_fold, b, b_fold, scale) in enumerate(
            ((query, query_fold, d_own, d_side, 1.0 / LOG2E), (grad, grad_fold, e_own, e_side, None))
        ):
            fix = (lambda v: v * scale) if scale else (lambda v: v)
            side = fix(nt(a_fold, b_fold))
            dkv_ref[k, rows, own] += fix(nt(a, b))
            dkv_ref[k, rows, left] += side[:PAD]
            dkv_ref[k, rows, right] += side[PAD:]

    def body(pair, carry):
        one_head(2 * pair)
        one_head(2 * pair + 1)
        return carry

    def send_halo():
        for side, lanes in ((0, slice(0, WIN)), (1, slice(WIN + slots, 2 * WIN + slots))):
            give_ref[side] = dkv_ref[:, :, lanes].astype(BF16)

        @pl.when(jnp.logical_not(first_seq))
        def _():
            halo(0).start()

        @pl.when(jnp.logical_not(last_seq))
        def _():
            halo(1).start()

    def advance(which, stage):
        for c in which:
            c.advance(stage)

    half = PAIRS // 2
    plan = {
        (0, 0): [partial(advance, soon, 1)],
        (1, 1): [send_halo],
        (2, 0): [partial(advance, soon, 2)],
        (3, 0): [partial(advance, soon, 3)],
    }
    for part in range(2):
        lax.fori_loop(part * half, (part + 1) * half, body, 0, unroll=half)
        for k in range(windows):
            for action in plan.get((k, part), []):
                pl.when(step == k)(action)

    @pl.when(step == windows - 1)
    def _():
        @pl.when(jnp.logical_not(first_seq))
        def _():
            halo(0).wait_send()
            halo(1).wait_recv()

        @pl.when(jnp.logical_not(last_seq))
        def _():
            halo(1).wait_send()
            halo(0).wait_recv()

        spot = pad_heads()
        plains = []
        for k in range(3):
            if k == 0:
                grad = dq_ref[...]
            else:
                mine = dkv_ref[k - 1, :, WIN : WIN + slots]
                first = mine[:, :WIN] + take_ref[0, k - 1].astype(F32)
                last = mine[:, slots - WIN :] + take_ref[1, k - 1].astype(F32)
                grad = jnp.concatenate([first, mine[:, WIN : slots - WIN], last], axis=1).astype(BF16)
            plain = tn(spot, grad).astype(BF16)
            plains.append(plain)
            qkv_ref[k * BLOCK : k * BLOCK + width_s, :width_s] = nt(xs_ref[...], plain).astype(BF16)
        advance(soon, 4)
        advance(late, 0)
        total = dres_ref[...]
        for w_ref, plain in zip((wq_ref, wk_ref, wv_ref), plains):
            total = total + nn(w_ref[...], plain)
        dx_ref[...] = total.astype(BF16)
        advance(late, 1)
        advance(late, 2)
        advance(soon, 5)
        advance(late, 3)
        advance(soon, 6)

        def put(group, cuts, target, first_sem):
            made = []
            for n, (c, (first, last, _)) in enumerate(zip(group, cuts)):
                made.append(pltpu.make_async_copy(c.whole, target.at[:, first:last], out_sem.at[first_sem + n]))
                made[-1].start()
            return made

        copies = put(soon, EARLY, early_ref, 0)
        advance(late, 4)
        advance(late, 5)
        advance(late, 6)
        copies += put(late, LATE, late_ref, len(EARLY))
        for c in copies:
            c.wait()


def back(sq, skv, dctx, e, g, rows, pack, xs, dres, wq, wk, wv):
    padded, slots = sq.shape
    windows = slots // WIN
    width_s = xs.shape[0]
    packed_rows = pack.shape[0]
    whole = lambda a: pl.BlockSpec(a.shape, lambda i: (0,) * a.ndim, pipeline_mode=pl.Buffered(1))
    saved = pl.BlockSpec((1, HEADS, 2 * WIN, WIN), lambda i: ((windows - i) % windows, 0, 0, 0))
    anywhere = pl.BlockSpec(memory_space=pl.ANY)
    scratch = [
        pltpu.VMEM((padded, slots), BF16),
        pltpu.VMEM((2, padded, slots + 2 * WIN), F32),
        pltpu.VMEM((2, 2, padded, WIN), BF16),
        pltpu.VMEM((2, 2, padded, WIN), BF16),
        pltpu.VMEM((packed_rows, QKV_LANES), BF16),
        pltpu.SemaphoreType.DMA((2,)),
        pltpu.SemaphoreType.DMA((2,)),
        pltpu.SemaphoreType.DMA((len(EARLY) + len(LATE),)),
    ]
    for first, last, names in EARLY + LATE:
        scratch += Chain.scratch(names, packed_rows, last - first)
    return pl.pallas_call(
        partial(back_kernel, windows),
        grid=(windows,),
        out_shape=[
            jax.ShapeDtypeStruct((width_s, slots), BF16),
            jax.ShapeDtypeStruct(pack.shape, BF16),
            jax.ShapeDtypeStruct((packed_rows, QKV_LANES), BF16),
        ],
        in_specs=[whole(sq), whole(skv), whole(dctx), saved, saved]
        + [whole(a) for a in (rows, pack, xs, dres, wq, wk, wv)],
        out_specs=[pl.BlockSpec((width_s, slots), lambda i: (0, 0)), anywhere, anywhere],
        scratch_shapes=scratch,
        compiler_params=pltpu.CompilerParams(
            vmem_limit_bytes=BIG,
            dimension_semantics=("arbitrary",),
            collective_id=0,
            has_side_effects=True,
        ),
    )(sq, skv, dctx, e, g, rows, pack, xs, dres, wq, wk, wv)


def unpack_kernel(
    every,
    width_t,
    early_hbm,
    late_hbm,
    dx_in_ref,
    dx_ref,
    loss_ref,
    gq_hbm,
    gk_hbm,
    gv_hbm,
    gwo_hbm,
    ginner_hbm,
    gouter_hbm,
    ghid_hbm,
    bouter_ref,
    binner_ref,
    gain_one_ref,
    shift_one_ref,
    gain_two_ref,
    shift_two_ref,
    early_ref,
    late_ref,
    gq_ref,
    gk_ref,
    gv_ref,
    gwo_ref,
    ginner_ref,
    gouter_ref,
    ghid_ref,
    in_sem,
    out_sem,
):
    width_s = gq_ref.shape[0]
    units = ginner_ref.shape[1]
    scale = 1.0 / every
    full = lambda v: v.astype(F32) * scale
    loads = [
        pltpu.make_async_copy(
            early_hbm.at[k * BLOCK : (k + 1) * BLOCK], early_ref.at[k * BLOCK : (k + 1) * BLOCK], in_sem.at[k]
        )
        for k in range(3)
    ]
    loads.append(pltpu.make_async_copy(late_hbm, late_ref, in_sem.at[3]))
    for c in loads:
        c.start()
    stores = []

    def store(source, target):
        stores.append(pltpu.make_async_copy(source, target, out_sem.at[len(stores)]))
        stores[-1].start()

    dx_ref[...] = dx_in_ref[...]
    loads[0].wait()
    gouter_ref[...] = full(early_ref[:width_s, :units])
    store(gouter_ref, gouter_hbm)
    loads[1].wait()
    ginner_ref[...] = full(early_ref[BLOCK : BLOCK + width_s, :units])
    store(ginner_ref, ginner_hbm)
    binner_ref[...] = full(early_ref[BLOCK + width_s : BLOCK + width_s + 8, :units])[0]
    loads[2].wait()
    third = slice(2 * BLOCK, 2 * BLOCK + width_s)
    ghid_ref[...] = full(early_ref[third, :width_t])
    store(ghid_ref, ghid_hbm)
    gwo_ref[...] = full(early_ref[third, width_t : width_t + width_s])
    store(gwo_ref, gwo_hbm)
    loads[3].wait()
    for k, (ref, hbm) in enumerate(((gq_ref, gq_hbm), (gk_ref, gk_hbm), (gv_ref, gv_hbm))):
        ref[...] = full(late_ref[k * BLOCK : k * BLOCK + width_s, :width_s])
        store(ref, hbm)
    last = units // 128 * 128
    lane = lax.broadcasted_iota(jnp.int32, (width_s, 128), 1)
    columns = jnp.where(
        lane < 4,
        full(early_ref[third, SUMS_AT : SUMS_AT + 128]),
        full(early_ref[:width_s, last : last + 128]),
    )
    turned = jnp.transpose(columns)
    for k, ref in enumerate((gain_one_ref, shift_one_ref, gain_two_ref, shift_two_ref)):
        ref[...] = turned[k]
    bouter_ref[...] = turned[units - last]
    part = early_ref[2 * BLOCK + width_s : 2 * BLOCK + width_s + 8, :128].astype(F32)
    total = jnp.sum(jnp.sum(part, axis=0, keepdims=True), axis=1, keepdims=True)
    loss_ref[...] = total * (scale / width_t)
    for c in stores:
        c.wait()


def unpack(every, width_t, units, early, late, dx):
    width_s = dx.shape[0]
    sds = lambda *shape: jax.ShapeDtypeStruct(shape, F32)
    square = sds(width_s, width_s)
    large = [square, square, square, square, sds(width_s, units), sds(width_s, units), sds(width_s, width_t)]
    vectors = [sds(width_s), sds(units)] + [sds(width_s)] * 4
    anywhere = pl.BlockSpec(memory_space=pl.ANY)
    return pl.pallas_call(
        partial(unpack_kernel, every, width_t),
        out_shape=[jax.ShapeDtypeStruct(dx.shape, BF16), sds(1, 1)] + large + vectors,
        in_specs=[anywhere, anywhere, VMEM],
        out_specs=[VMEM] * 2 + [anywhere] * len(large) + [VMEM] * len(vectors),
        scratch_shapes=[pltpu.VMEM(early.shape, BF16), pltpu.VMEM(late.shape, BF16)]
        + [pltpu.VMEM(a.shape, F32) for a in large]
        + [pltpu.SemaphoreType.DMA((4,)), pltpu.SemaphoreType.DMA((len(large),))],
        compiler_params=pltpu.CompilerParams(vmem_limit_bytes=BIG),
    )(early, late, dx)


def local(
    inputs,
    teacher_input,
    filled_slot_mask,
    seg_lengths,
    query_weight,
    key_weight,
    value_weight,
    w_output,
    gain_one,
    shift_one,
    w_inner,
    b_inner,
    w_outer,
    b_outer,
    gain_two,
    shift_two,
    w_hidden,
    teacher_query_weight,
    teacher_key_weight,
    teacher_value_weight,
    teacher_output,
    teacher_gain_one,
    teacher_shift_one,
    teacher_inner,
    teacher_outer,
    teacher_gain_two,
    teacher_shift_two,
):
    xs = jnp.transpose(inputs[0])
    xt = teacher_input[0]
    slots, width_t = xt.shape
    width_s = xs.shape[0]
    stats, loss_rows, rows, tctx, sctx, sq, skv, e, g = attend(
        filled_slot_mask,
        seg_lengths,
        xt,
        xs,
        teacher_query_weight,
        teacher_key_weight,
        teacher_value_weight,
        query_weight,
        key_weight,
        value_weight,
    )
    devices = lax.axis_size("seq") * lax.axis_size("batch")
    sizes = group_sizes()
    unit = 16 * sizes["core"] * sizes["batch"] * sizes["chain"]
    packed_rows = -(-3 * BLOCK // unit) * unit
    out, dctx, dres, pack = dense(
        packed_rows,
        (
            xt,
            tctx,
            teacher_output,
            xs,
            sctx,
            teacher_inner,
            teacher_outer,
            w_output,
            w_inner,
            jnp.transpose(w_outer),
            w_hidden,
        ),
        (stats, rows, loss_rows)
        + (
            teacher_gain_one,
            teacher_shift_one,
            teacher_gain_two,
            teacher_shift_two,
            gain_one,
            shift_one,
            b_outer,
            gain_two,
            shift_two,
            b_inner,
        ),
    )
    dx, early, late = back(sq, skv, dctx, e, g, rows, pack, xs, dres, query_weight, key_weight, value_weight)
    dx, loss, gq, gk, gv, gwo, ginner, gouter, ghid, *vectors = unpack(
        slots * devices, width_t, w_inner.shape[1], early, late, dx
    )
    g_b_outer, g_b_inner, g_gain_one, g_shift_one, g_gain_two, g_shift_two = vectors
    return (
        jnp.transpose(out)[None],
        jnp.transpose(dx)[None],
        loss[0, 0],
        gq,
        gk,
        gv,
        gwo,
        g_gain_one,
        g_shift_one,
        ginner,
        g_b_inner,
        jnp.transpose(gouter),
        g_b_outer,
        g_gain_two,
        g_shift_two,
        ghid,
    )


def solution(mesh):
    row_split = P("batch", "seq", None)
    return jax.shard_map(
        local,
        mesh=mesh,
        in_specs=(row_split, row_split, P("batch", None), P("batch", None)) + (P(),) * 23,
        out_specs=(row_split, row_split) + (P(),) * 14,
        check_vma=False,
    )
```

```python
from functools import partial

import jax
import jax.numpy as jnp
from jax import lax
from jax.experimental import pallas as pl
from jax.experimental.pallas import tpu as pltpu
from jax.sharding import PartitionSpec as P

HEADS = 12
HD_S = 26
HD_T = 64
WIN = 256
PAD = 32
SLOT_ONE = 26
PAIRS = HEADS // 2
CHUNK = 64
TAIL = 16
SLOTS = 4
BLOCK = 320
SUMS_AT = 1152
QKV_LANES = 384
MESH = pl.DeviceIdType.MESH
EPSILON = 1e-05
NEGATIVE = -1e30
LOG2E = 1.4426950408889634
F32 = jnp.float32
BF16 = jnp.bfloat16
VMEM = pl.BlockSpec(memory_space=pltpu.VMEM)
BIG = 60 << 20


def mm(left, right, dims):
    return lax.dot_general(left, right, ((dims[:1], dims[1:]), ((), ())), preferred_element_type=F32)


def nn(left, right):
    return mm(left, right, (1, 0))


def tn(left, right):
    return mm(left, right, (0, 0))


def nt(left, right):
    return mm(left, right, (1, 1))


def tt(left, right):
    return mm(left, right, (0, 1))


def pad_heads():
    row = lax.broadcasted_iota(jnp.int32, (HEADS * PAD, HEADS * HD_S), 0)
    col = lax.broadcasted_iota(jnp.int32, (HEADS * PAD, HEADS * HD_S), 1)
    spot = jnp.zeros((HEADS * PAD, HEADS * HD_S), F32)
    for head in range(HEADS):
        here = (row - head * PAD == col - head * HD_S) & (col >= head * HD_S) & (col < (head + 1) * HD_S)
        spot = jnp.where(here, 1.0, spot)
    return spot.astype(BF16)


def window_rows(mask_ref, lengths_ref, seq_index, windows, row_windows):
    lengths = lengths_ref[...].astype(F32)
    order = lax.broadcasted_iota(jnp.int32, lengths.shape, 1)
    lane = lax.broadcasted_iota(jnp.int32, (1, WIN), 1).astype(F32)
    out = []
    for j in range(windows + 2):
        number = seq_index * windows + (j - 1)
        inside = (number >= 0) & (number < row_windows)
        safe = jnp.clip(number, 0, row_windows - 1)
        start = jnp.sum(jnp.where(order < safe, lengths, 0.0), axis=1, keepdims=True)
        offset = start - (safe * WIN).astype(F32)
        late = (lane >= offset).astype(F32)
        filled = mask_ref[:, pl.ds(pl.multiple_of(safe * WIN, WIN), WIN)]
        filled = jnp.where(inside, filled.astype(F32), 0.0)
        out.append((late, filled))
    return out


def stack_rows(*rows):
    n = rows[0].shape[1]
    index = lax.broadcasted_iota(jnp.int32, (8, n), 0)
    block = jnp.zeros((8, n), F32)
    for k, row in enumerate(rows):
        block = jnp.where(index == k, row, block)
    return block.astype(BF16)


def attend_kernel(
    windows,
    row_windows,
    mask_ref,
    lengths_ref,
    xt_hbm,
    xs_ref,
    wtq_hbm,
    wtk_hbm,
    wtv_hbm,
    wq_ref,
    wk_ref,
    wv_ref,
    stats_ref,
    loss_ref,
    rows_ref,
    tctx_hbm,
    sctx_hbm,
    sq_hbm,
    skv_hbm,
    saved_e_hbm,
    saved_g_hbm,
    x_ref,
    xs_side_ref,
    wt_ref,
    bias_ref,
    wst_ref,
    tq_ref,
    tk_ref,
    tv_ref,
    sq_ref,
    skv_ref,
    tctx_ref,
    sctx_ref,
    e_ref,
    g_ref,
    work_ref,
    low_ref,
    in_sem,
    halo_send,
    halo_arrive,
    kv_sem,
    out_sem,
):
    slots = windows * WIN
    batch, seq = lax.axis_index("batch"), lax.axis_index("seq")
    peers = lax.axis_size("seq")
    has_left, has_right = seq > 0, seq < peers - 1
    width_t = x_ref.shape[1]
    extended = slots + 2 * WIN

    barrier = pltpu.get_barrier_semaphore()
    for move in (1, peers - 1):
        pl.semaphore_signal(barrier, inc=1, device_id=(batch, (seq + move) % peers), device_id_type=MESH)
    loads = [pltpu.make_async_copy(xt_hbm, x_ref.at[pl.ds(WIN, slots)], in_sem.at[0])]
    for k, w_hbm in enumerate((wtq_hbm, wtk_hbm, wtv_hbm)):
        loads.append(pltpu.make_async_copy(w_hbm, wt_ref.at[k], in_sem.at[1 + k]))
    for c in loads:
        c.start()
    pl.semaphore_wait(barrier, 2)

    def halo(side):
        device = (batch, seq - 1 + 2 * side)
        first = side * (slots - WIN)
        return [
            pltpu.make_async_remote_copy(
                src_ref=xt_hbm.at[pl.ds(first, WIN)],
                dst_ref=x_ref.at[pl.ds((1 - side) * (WIN + slots), WIN)],
                send_sem=halo_send.at[0, side],
                recv_sem=halo_arrive.at[0, 1 - side],
                device_id=device,
                device_id_type=MESH,
            ),
            pltpu.make_async_remote_copy(
                src_ref=xs_ref.at[:, pl.ds(first, WIN)],
                dst_ref=xs_side_ref.at[1 - side],
                send_sem=halo_send.at[1, side],
                recv_sem=halo_arrive.at[1, 1 - side],
                device_id=device,
                device_id_type=MESH,
            ),
        ]

    for side, present in ((0, has_left), (1, has_right)):

        @pl.when(present)
        def _():
            for c in halo(side):
                c.start()

        @pl.when(jnp.logical_not(present))
        def _():
            x_ref[side * (WIN + slots) : side * (WIN + slots) + WIN, :] = jnp.zeros((WIN, width_t), BF16)
            xs_side_ref[side] = jnp.zeros(xs_side_ref.shape[1:], BF16)

    info = window_rows(mask_ref, lengths_ref, seq, windows, row_windows)
    eye = lax.broadcasted_iota(jnp.int32, (WIN, WIN), 0) == lax.broadcasted_iota(jnp.int32, (WIN, WIN), 1)
    rows_ref[...] = jnp.zeros_like(rows_ref)
    for w in range(windows):
        late, filled = info[w + 1]
        late_l, filled_l = info[w]
        late_r, filled_r = info[w + 2]
        early = 1.0 - late
        here = slice(w * WIN, (w + 1) * WIN)
        rows_ref[0:1, here] = early
        rows_ref[1:2, here] = late
        rows_ref[2:3, here] = filled
        query = stack_rows(early, late)
        own = tn(stack_rows(NEGATIVE * (1.0 - early * filled), NEGATIVE * (1.0 - late * filled)), query)
        bias_ref[w, :WIN, :] = jnp.where(eye, 0.0, own)
        bias_ref[w, WIN:, :] = tn(
            stack_rows(
                NEGATIVE * (1.0 - late_l * filled_l), NEGATIVE * (1.0 - (1.0 - late_r) * filled_r)
            ),
            query,
        )
    loss_ref[...] = jnp.zeros_like(loss_ref)
    stats_ref[...] = jnp.zeros_like(stats_ref)
    spot = pad_heads()
    padded = HEADS * PAD
    row = lax.broadcasted_iota(jnp.int32, (padded, 1), 0) % PAD
    ones = (row >= SLOT_ONE) & (row < SLOT_ONE + 3)

    xs = xs_ref[...]
    for k, w_ref in enumerate((wq_ref, wk_ref, wv_ref)):
        wst_ref[k] = nt(spot, w_ref[...]).astype(BF16)
        made = nn(wst_ref[k], xs)
        if k == 0:
            sq_ref[...] = (made * (LOG2E * HD_S**-0.5)).astype(BF16)
        else:
            if k == 2:
                made = jnp.where(ones, 1.0, made)
            skv_ref[k - 1, :, WIN : WIN + slots] = made.astype(BF16)
    tail = (lax.broadcasted_iota(jnp.int32, (TAIL, extended), 0) == 0).astype(BF16)
    for head in range(HEADS):
        tv_ref[head * (HD_T + TAIL) + HD_T : (head + 1) * (HD_T + TAIL), :] = tail

    def put_values(made, first_head, lanes):
        for j in range(made.shape[0] // HD_T):
            at = (first_head + j) * (HD_T + TAIL)
            tv_ref[at : at + HD_T, lanes] = made[j * HD_T : (j + 1) * HD_T]

    part = width_t // 2
    loads[0].wait()
    for k in range(3):
        loads[1 + k].wait()
        for half in range(2):
            made = tt(wt_ref[k, :, half * part : (half + 1) * part], x_ref[WIN : WIN + slots, :])
            if k == 0:
                tq_ref[half * part : (half + 1) * part, :] = (made * (LOG2E * HD_T**-0.5)).astype(BF16)
            elif k == 1:
                tk_ref[half * part : (half + 1) * part, WIN : WIN + slots] = made.astype(BF16)
            else:
                put_values(made.astype(BF16), half * HEADS // 2, slice(WIN, WIN + slots))
    for side, present in ((0, has_left), (1, has_right)):

        @pl.when(present)
        def _():
            for sent, landed in zip(halo(side), halo(1 - side)):
                sent.wait_send()
                landed.wait_recv()

        lanes = slice(side * (WIN + slots), side * (WIN + slots) + WIN)
        for k in (1, 2):
            made = tt(wt_ref[k], x_ref[lanes, :]).astype(BF16)
            if k == 1:
                tk_ref[:, lanes] = made
            else:
                put_values(made, 0, lanes)
            made = nn(wst_ref[k], xs_side_ref[side])
            if k == 2:
                made = jnp.where(ones, 1.0, made)
            skv_ref[k - 1, :, lanes] = made.astype(BF16)
    finals = [
        pltpu.make_async_copy(sq_ref, sq_hbm, kv_sem.at[0]),
        pltpu.make_async_copy(skv_ref, skv_hbm, kv_sem.at[1]),
    ]
    for c in finals:
        c.start()

    def stores(pair, which):
        slot = pair % 2
        t_rows = pl.ds(pl.multiple_of(pair * 2 * HD_T, 2 * HD_T), 2 * HD_T)
        s_rows = pl.ds(pl.multiple_of(pair * 2 * PAD, 2 * PAD), 2 * PAD)
        heads = pl.ds(pair * 2, 2)
        ends = (
            (e_ref.at[slot], saved_e_hbm.at[:, heads]),
            (g_ref.at[slot], saved_g_hbm.at[:, heads]),
            (tctx_ref.at[t_rows], tctx_hbm.at[t_rows]),
            (sctx_ref.at[s_rows], sctx_hbm.at[s_rows]),
        )
        return [pltpu.make_async_copy(*ends[k], out_sem.at[k, pair]) for k in which]

    def one_pair(pair, carry):
        @pl.when(pair >= 2)
        def _():
            for c in stores(pair - 2, (0, 1)):
                c.wait()

        attend_pair(pair)
        for c in stores(pair, range(4)):
            c.start()
        return carry

    def attend_pair(pair):
        e_out, g_out = e_ref.at[pair % 2], g_ref.at[pair % 2]
        def rows_of(w):
            left = slice(w * WIN, (w + 1) * WIN)
            own = slice((w + 1) * WIN, (w + 2) * WIN)
            right = slice((w + 2) * WIN, (w + 3) * WIN)
            return left, own, right, rows_ref[0:1, left], rows_ref[1:2, left], rows_ref[2:3, left]

        def first_pass(w, q_ref, k_ref, rows, work_ref):
            left, own, right, early, late, _ = rows_of(w)
            query = q_ref[rows, left]
            query_fold = jnp.concatenate([query * early.astype(BF16), query * late.astype(BF16)], axis=0)
            keys = k_ref[rows, own]
            keys_fold = jnp.concatenate([k_ref[rows, left], k_ref[rows, right]], axis=0)
            top = None
            for part, (a, b) in enumerate(((keys, query), (keys_fold, query_fold))):
                raw = tn(a, b)
                for c in range(0, WIN, CHUNK):
                    block = raw[c : c + CHUNK] + bias_ref[w, part * WIN + c : part * WIN + c + CHUNK, :]
                    work_ref[part * WIN + c : part * WIN + c + CHUNK, :] = block
                    for r in range(0, CHUNK, 8):
                        piece = block[r : r + 8]
                        top = piece if top is None else jnp.maximum(top, piece)
            return jnp.max(top, axis=0, keepdims=True)

        def second_pass(work_ref, top, low_ref):
            for c in range(0, 2 * WIN, CHUNK):
                e = jnp.exp2(work_ref[c : c + CHUNK, :] - top)
                work_ref[c : c + CHUNK, :] = e
                low_ref[c : c + CHUNK, :] = e.astype(BF16)

        def mix(w, v_ref, rows, low_ref, head_width):
            left, own, right, early, late, _ = rows_of(w)
            values = v_ref[rows, own]
            values_fold = jnp.concatenate([v_ref[rows, left], v_ref[rows, right]], axis=0)
            mixed = nn(values, low_ref[:WIN, :])
            side = nn(values_fold, low_ref[WIN:, :])
            n = values.shape[0]
            mixed = mixed + early * side[:n] + late * side[n:]
            inverse = 1.0 / mixed[head_width : head_width + 1]
            return mixed[: -TAIL if head_width == HD_T else n] * inverse, inverse

        units = [(w, h) for w in range(windows) for h in range(2)]
        state = {}

        def refs(u):
            w, h = units[u]
            head = 2 * pair + h
            t_rows = pl.ds(pl.multiple_of(head * HD_T, HD_T), HD_T)
            s_rows = pl.ds(pl.multiple_of(head * PAD, PAD), PAD)
            v_rows = pl.ds(pl.multiple_of(head * (HD_T + TAIL), TAIL), HD_T + TAIL)
            slot = u % SLOTS
            return w, h, t_rows, s_rows, v_rows, work_ref.at[2 * slot], work_ref.at[2 * slot + 1], low_ref.at[slot]

        def score_stage(u):
            w, h, t_rows, s_rows, _, work_t, work_s, _ = refs(u)
            state[u] = [
                first_pass(w, tq_ref, tk_ref, t_rows, work_t),
                first_pass(w, sq_ref, skv_ref.at[0], s_rows, work_s),
            ]

        def power_stage(u):
            w, h, _, _, _, work_t, work_s, low_t = refs(u)
            second_pass(work_t, state[u][0], low_t)
            second_pass(work_s, state[u][1], e_out.at[w, h])

        def mix_stage(u):
            w, h, t_rows, s_rows, v_rows, _, _, low_t = refs(u)
            left = rows_of(w)[0]
            t_mixed, t_inv = mix(w, tv_ref, v_rows, low_t, HD_T)
            s_mixed, s_inv = mix(w, skv_ref.at[1], s_rows, e_out.at[w, h], SLOT_ONE)
            tctx_ref[t_rows, left] = t_mixed.astype(BF16)
            sctx_ref[s_rows, left] = s_mixed
            state[u] = [t_inv, s_inv]

        def gap_stage(u):
            w, h, _, _, _, work_t, work_s, _ = refs(u)
            left, _, _, _, _, filled = rows_of(w)
            t_inv, s_inv = state.pop(u)
            width = 2.0 * HEADS * HD_T
            scale_s = (width * filled) * s_inv * s_inv
            scale_t = (width * filled) * s_inv * t_inv
            square = jnp.zeros((8, WIN), F32)
            cross = jnp.zeros((8, WIN), F32)
            for c in range(0, 2 * WIN, CHUNK):
                s = work_s[c : c + CHUNK, :]
                gap = s * scale_s - work_t[c : c + CHUNK, :] * scale_t
                g_out[w, h, c : c + CHUNK, :] = gap.astype(BF16)
                for r in range(0, CHUNK, 8):
                    piece = gap[r : r + 8]
                    square += piece * piece
                    cross += piece * s[r : r + 8]
            square = jnp.sum(square, axis=0, keepdims=True)
            cross = jnp.sum(cross, axis=0, keepdims=True)
            back = 1.0 / (s_inv * width)
            stats_ref[pair, h : h + 1, left] = s_inv
            stats_ref[pair, 2 + h : 3 + h, left] = cross
            loss_ref[0:1, left] += square * back * back

        last = len(units)
        for u in range(last + 2):
            if u < last:
                score_stage(u)
            if 0 <= u - 1 < last:
                power_stage(u - 1)
            if 0 <= u - 2 < last:
                mix_stage(u - 2)
                gap_stage(u - 2)


    lax.fori_loop(0, PAIRS, one_pair, 0)
    for pair in range(PAIRS):
        for c in stores(pair, range(0 if pair >= PAIRS - 2 else 2, 4)):
            c.wait()
    for c in finals:
        c.wait()


def attend(mask, lengths, xt, xs, wtq, wtk, wtv, wq, wk, wv):
    slots, width_t = xt.shape
    width_s = xs.shape[0]
    windows = slots // WIN
    row_windows = mask.shape[1] // WIN
    padded = HEADS * PAD
    extended = slots + 2 * WIN
    sds = jax.ShapeDtypeStruct
    anywhere = pl.BlockSpec(memory_space=pl.ANY)
    saved = (windows, HEADS, 2 * WIN, WIN)
    return pl.pallas_call(
        partial(attend_kernel, windows, row_windows),
        out_shape=(
            sds((PAIRS, 8, slots), F32),
            sds((8, slots), F32),
            sds((8, slots), F32),
            sds((width_t, slots), BF16),
            sds((padded, slots), F32),
            sds((padded, slots), BF16),
            sds((2, padded, extended), BF16),
            sds(saved, BF16),
            sds(saved, BF16),
        ),
        in_specs=[VMEM, VMEM, anywhere, VMEM] + [anywhere] * 3 + [VMEM] * 3,
        out_specs=[VMEM] * 3 + [anywhere] * 6,
        scratch_shapes=[
            pltpu.VMEM((extended, width_t), BF16),
            pltpu.VMEM((2, width_s, WIN), BF16),
            pltpu.VMEM((3, width_t, width_t), BF16),
            pltpu.VMEM((windows, 2 * WIN, WIN), F32),
            pltpu.VMEM((3, padded, width_s), BF16),
            pltpu.VMEM((width_t, slots), BF16),
            pltpu.VMEM((width_t, extended), BF16),
            pltpu.VMEM((HEADS * (HD_T + TAIL), extended), BF16),
            pltpu.VMEM((padded, slots), BF16),
            pltpu.VMEM((2, padded, extended), BF16),
            pltpu.VMEM((width_t, slots), BF16),
            pltpu.VMEM((padded, slots), F32),
            pltpu.VMEM((2, windows, 2, 2 * WIN, WIN), BF16),
            pltpu.VMEM((2, windows, 2, 2 * WIN, WIN), BF16),
            pltpu.VMEM((2 * SLOTS, 2 * WIN, WIN), F32),
            pltpu.VMEM((SLOTS, 2 * WIN, WIN), BF16),
            pltpu.SemaphoreType.DMA((4,)),
            pltpu.SemaphoreType.DMA((2, 2)),
            pltpu.SemaphoreType.DMA((2, 2)),
            pltpu.SemaphoreType.DMA((2,)),
            pltpu.SemaphoreType.DMA((4, PAIRS)),
        ],
        compiler_params=pltpu.CompilerParams(
            vmem_limit_bytes=BIG, collective_id=1, has_side_effects=True
        ),
    )(mask, lengths, xt, xs, wtq, wtk, wtv, wq, wk, wv)


def normalize(values, gain, shift):
    n = values.shape[0]
    center = values - jnp.sum(values, axis=0, keepdims=True) * (1.0 / n)
    rscale = lax.rsqrt(jnp.sum(center * center, axis=0, keepdims=True) * (1.0 / n) + EPSILON)
    unit = center * rscale
    return unit * gain + shift, unit, rscale


def normalize_back(grad, unit, rscale, gain):
    n = grad.shape[0]
    scaled = grad * gain
    first = jnp.sum(scaled, axis=0, keepdims=True) * (1.0 / n)
    second = jnp.sum(scaled * unit, axis=0, keepdims=True) * (1.0 / n)
    return rscale * (scaled - first - unit * second)


def fold_lanes(values):
    total = values[:, :128]
    for at in range(128, values.shape[1], 128):
        total = total + values[:, at : at + 128]
    return total


ROOT_HALF = 0.7071067811865476
ROOT_PI = 0.3989422804014327


DENSE_IN = ("xt", "tctx", "two", "xs", "sctx", "tin", "tout", "wo", "w1", "w2", "wh")


def dense_kernel(
    xt_hbm,
    tctx_hbm,
    two_hbm,
    xs_hbm,
    sctx_hbm,
    tin_hbm,
    tout_hbm,
    wo_hbm,
    w1_hbm,
    w2_hbm,
    wh_hbm,
    stats_ref,
    rows_ref,
    loss_ref,
    t_gain_one_ref,
    t_shift_one_ref,
    t_gain_two_ref,
    t_shift_two_ref,
    gain_one_ref,
    shift_one_ref,
    b_outer_ref,
    gain_two_ref,
    shift_two_ref,
    b_inner_ref,
    out_hbm,
    dctx_hbm,
    dres_hbm,
    pack_hbm,
    xt_ref,
    tctx_ref,
    two_ref,
    xs_ref,
    sctx_ref,
    tin_ref,
    tout_ref,
    wo_ref,
    w1_ref,
    w2_ref,
    wh_ref,
    out_ref,
    dctx_ref,
    dres_ref,
    pack_ref,
    act_ref,
    slope_ref,
    in_sem,
    out_sem,
):
    sources = (
        xt_hbm, tctx_hbm, two_hbm, xs_hbm, sctx_hbm, tin_hbm, tout_hbm, wo_hbm, w1_hbm, w2_hbm, wh_hbm
    )
    targets = (xt_ref, tctx_ref, two_ref, xs_ref, sctx_ref, tin_ref, tout_ref, wo_ref, w1_ref, w2_ref, wh_ref)
    loads = {
        name: pltpu.make_async_copy(source, target, in_sem.at[k])
        for k, (name, source, target) in enumerate(zip(DENSE_IN, sources, targets))
    }
    for c in loads.values():
        c.start()
    width_s, units_s = w1_ref.shape
    width_t, units_t = tin_ref.shape
    slots = xt_ref.shape[0]
    low = lambda v: v.astype(BF16)
    stores = []

    def store(source, target):
        stores.append(pltpu.make_async_copy(source, target, out_sem.at[len(stores)]))
        stores[-1].start()

    def columns(*refs):
        n = refs[0].shape[0]
        index = lax.broadcasted_iota(jnp.int32, (8, n), 0)
        block = jnp.zeros((8, n), F32)
        for k, ref in enumerate(refs):
            block = jnp.where(index == k, ref[...].reshape(1, n), block)
        turned = jnp.transpose(block)
        return [turned[:, k : k + 1] for k in range(len(refs))]

    t_gain_one, t_shift_one, t_gain_two, t_shift_two = columns(
        t_gain_one_ref, t_shift_one_ref, t_gain_two_ref, t_shift_two_ref
    )
    gain_one, shift_one, b_outer, gain_two, shift_two = columns(
        gain_one_ref, shift_one_ref, b_outer_ref, gain_two_ref, shift_two_ref
    )
    (b_inner,) = columns(b_inner_ref)
    spot = pad_heads()
    pack_ref[...] = jnp.zeros_like(pack_ref)
    act_ref[units_s:, :] = jnp.ones((act_ref.shape[0] - units_s, slots), BF16)
    for name in ("xt", "tctx", "two"):
        loads[name].wait()
    start = jnp.transpose(xt_ref[...]).astype(F32) + tn(two_ref[...], tctx_ref[...])
    t_normed = normalize(start, t_gain_one, t_shift_one)[0]
    t_low = low(t_normed)
    t_sum = t_normed
    for name in ("xs", "sctx", "tin", "tout"):
        loads[name].wait()
    for at in range(0, units_t, width_t):
        pre = tn(tin_ref[:, at : at + width_t], t_low)
        active = low(0.5 * pre * (1.0 + lax.erf(pre * ROOT_HALF)))
        t_sum = t_sum + tn(tout_ref[at : at + width_t, :], active)
    target = normalize(t_sum, t_gain_two, t_shift_two)[0]
    for name in ("wo", "w1", "w2", "wh"):
        loads[name].wait()
    wop = low(nn(spot, wo_ref[...]))
    context = sctx_ref[...]
    context_low = low(context)
    normed, unit_one, rscale_one = normalize(
        xs_ref[...].astype(F32) + tn(wop, context_low), gain_one, shift_one
    )
    normed_low = low(normed)
    pre = tn(w1_ref[...], normed_low) + b_inner
    half = 0.5 * (1.0 + lax.erf(pre * ROOT_HALF))
    slope_ref[...] = half + pre * (ROOT_PI * jnp.exp(-0.5 * pre * pre))
    act_ref[:units_s, :] = low(pre * half)
    student, unit_two, rscale_two = normalize(
        normed + nn(w2_ref[...], act_ref[:units_s, :]) + b_outer, gain_two, shift_two
    )
    student_low = low(student)
    out_ref[...] = student_low
    store(out_ref, out_hbm)
    gap = tn(wh_ref[...], student_low) - target
    filled = rows_ref[2:3, :]
    masked = filled * gap
    d_proj = low(2.0 * masked)
    third = slice(2 * BLOCK, 2 * BLOCK + width_s)
    pack_ref[third, :width_t] = low(nt(student_low, d_proj))
    d_student = nn(wh_ref[...], d_proj)
    d_two = normalize_back(d_student, unit_two, rscale_two, gain_two)
    d_outer = low(d_two)
    pack_ref[:width_s, :] = low(nt(d_outer, act_ref[...]))
    store(pack_ref.at[:BLOCK], pack_hbm.at[:BLOCK])
    d_inner = low(tn(w2_ref[...], d_outer) * slope_ref[...])
    pack_ref[BLOCK : BLOCK + width_s, :units_s] = low(nt(normed_low, d_inner))
    pack_ref[BLOCK + width_s : BLOCK + width_s + 8, :units_s] = low(nt(jnp.ones((8, slots), BF16), d_inner))
    store(pack_ref.at[BLOCK : 2 * BLOCK], pack_hbm.at[BLOCK : 2 * BLOCK])
    d_normed = nn(w1_ref[...], d_inner) + d_two
    d_one = normalize_back(d_normed, unit_one, rscale_one, gain_one)
    dres_ref[...] = d_one
    store(dres_ref, dres_hbm)
    d_att = low(d_one)
    gwo = low(nt(context_low, d_att))
    pack_ref[third, width_t : width_t + width_s] = low(tn(spot, gwo))
    d_context = nn(wop, d_att)
    row = lax.broadcasted_iota(jnp.int32, (PAD, slots), 0)
    for head in range(HEADS):
        pair, h = head // 2, head % 2
        inverse = stats_ref[pair, h : h + 1, :]
        cross = stats_ref[pair, 2 + h : 3 + h, :]
        rows = slice(head * PAD, (head + 1) * PAD)
        part = low(d_context[rows] * inverse).astype(F32)
        delta = -jnp.sum(part * context[rows], axis=0, keepdims=True) - inverse * cross
        high = low(delta).astype(F32)
        rest = delta - high
        middle = low(rest).astype(F32)
        part = jnp.where(row == SLOT_ONE, high, part)
        part = jnp.where(row == SLOT_ONE + 1, middle, part)
        part = jnp.where(row == SLOT_ONE + 2, rest - middle, part)
        dctx_ref[rows, :] = low(part)
    store(dctx_ref, dctx_hbm)
    lane = lax.broadcasted_iota(jnp.int32, (width_s, 128), 1)
    sums = jnp.zeros((width_s, 128), F32)
    for k, values in enumerate((d_normed * unit_one, d_normed, d_student * unit_two, d_student)):
        sums = jnp.where(lane == k, jnp.sum(fold_lanes(values), axis=1, keepdims=True), sums)
    pack_ref[third, SUMS_AT : SUMS_AT + 128] = low(sums)
    square = jnp.sum(fold_lanes(masked * gap).reshape(-1, 8, 128), axis=0)
    row = lax.broadcasted_iota(jnp.int32, (8, 128), 0)
    for c in range(slots // 128):
        square += jnp.where(row == c % 8, width_t * loss_ref[0:1, c * 128 : (c + 1) * 128], 0.0)
    pack_ref[2 * BLOCK + width_s : 2 * BLOCK + width_s + 8, :128] = low(square)
    store(pack_ref.at[2 * BLOCK :], pack_hbm.at[2 * BLOCK :])
    for c in stores:
        c.wait()


def dense(packed_rows, big, small):
    xt, tctx, two, xs, sctx, tin, tout, wo, w1, w2, wh = big
    slots, width_t = xt.shape
    width_s, units_s = w1.shape
    padded = HEADS * PAD
    inner_pad = -(-units_s // 128) * 128
    sds = jax.ShapeDtypeStruct
    outs = [
        sds((width_s, slots), BF16),
        sds((padded, slots), BF16),
        sds((width_s, slots), F32),
        sds((packed_rows, inner_pad), BF16),
    ]
    anywhere = pl.BlockSpec(memory_space=pl.ANY)
    return pl.pallas_call(
        dense_kernel,
        out_shape=outs,
        in_specs=[anywhere] * len(big) + [VMEM] * len(small),
        out_specs=[anywhere] * len(outs),
        scratch_shapes=[pltpu.VMEM(a.shape, a.dtype) for a in big]
        + [pltpu.VMEM(a.shape, a.dtype) for a in outs]
        + [
            pltpu.VMEM((inner_pad, slots), BF16),
            pltpu.VMEM((units_s, slots), F32),
            pltpu.SemaphoreType.DMA((len(big),)),
            pltpu.SemaphoreType.DMA((6,)),
        ],
        compiler_params=pltpu.CompilerParams(vmem_limit_bytes=BIG),
    )(*big, *small)


def group_sizes():
    seq = lax.axis_size("seq")
    core = 2 if seq % 2 == 0 else 1
    chain = 4 if seq // core % 4 == 0 else 1
    return {"core": core, "batch": lax.axis_size("batch"), "chain": chain, "outer": seq // core // chain}


class Group:
    def __init__(self, name):
        batch, seq = lax.axis_index("batch"), lax.axis_index("seq")
        sizes = group_sizes()
        self.size = sizes[name]
        if name == "batch":
            self.place = batch
            self.device = lambda j: (j, seq)
        else:
            stride = {"core": 1, "chain": sizes["core"], "outer": sizes["core"] * sizes["chain"]}[name]
            self.place = seq // stride % self.size
            self.device = lambda j: (batch, seq + (j - self.place) * stride)

    def other(self, k):
        return (self.place + k) % self.size


class Chain:
    def __init__(self, names, source, scratch, local=None):
        self.names, self.source, self.local = names, source, local
        self.groups = [Group(n) for n in names]
        count = len(names)
        self.outer = Group("outer")
        self.received, self.sums = scratch[:count], scratch[count : 2 * count]
        self.around, self.whole, self.send, self.arrive = scratch[2 * count :]
        rows = self.whole.shape[0]
        self.rows, self.base, base = [], [], 0
        for g in self.groups:
            self.base.append(base)
            rows //= g.size
            base = base + g.place * rows
            self.rows.append(rows)
        self.mine = base
        self.sem = 0
        self.pending = []

    @staticmethod
    def scratch(names, rows, lanes):
        received, sums, copies = [], [], 0
        total, sizes = rows, group_sizes()
        for size in (sizes[n] for n in names):
            rows = rows // size
            received.append(pltpu.VMEM((max(size - 1, 1), rows, lanes), BF16))
            sums.append(pltpu.VMEM((rows, lanes), BF16))
            copies += 2 * (size - 1)
        copies = max(copies + sizes["outer"] - 1, 1)
        return (
            received
            + sums
            + [
                pltpu.VMEM((max(sizes["outer"] - 1, 1), rows, lanes), BF16),
                pltpu.VMEM((total, lanes), BF16),
                pltpu.SemaphoreType.DMA((copies,)),
                pltpu.SemaphoreType.DMA((copies,)),
            ]
        )

    def copy(self, ends):
        at = self.sem
        self.sem += 1

        def form():
            source, target, device = ends()
            return pltpu.make_async_remote_copy(
                src_ref=source,
                dst_ref=target,
                send_sem=self.send.at[at],
                recv_sem=self.arrive.at[at],
                device_id=device,
                device_id_type=MESH,
            )

        form().start()
        self.pending.append(form)

    def scatter(self, k):
        g, rows = self.groups[k], self.rows[k]
        source = self.source if k == 0 else self.sums[k - 1]

        def ends(step):
            other = g.other(step)
            there = pl.ds(pl.multiple_of(other * rows, 16), rows)
            return source.at[there], self.received[k].at[step - 1], g.device(other)

        for step in range(1, g.size):
            self.copy(partial(ends, step))

    def wait(self):
        for form in self.pending:
            form().wait()
        self.pending = []

    def add(self, k):
        self.wait()
        g, rows = self.groups[k], self.rows[k]
        source = self.source if k == 0 else self.sums[k - 1]
        if k == 0 and self.local is not None:
            total = self.local[...].astype(F32)
        else:
            total = source[pl.ds(pl.multiple_of(g.place * rows, 16), rows), :].astype(F32)
        for step in range(1, g.size):
            total = total + self.received[k][step - 1].astype(F32)
        total = total.astype(BF16)
        if k < len(self.groups) - 1 or self.outer.size > 1:
            self.sums[k][...] = total
        if k == len(self.groups) - 1:
            if self.outer.size > 1:
                total = self.exchange(total)
            self.whole[pl.ds(pl.multiple_of(self.mine, 16), rows), :] = total

    def exchange(self, total):
        g = self.outer

        def ends(step):
            return self.sums[-1], self.around.at[step - 1], g.device(g.other(step))

        for step in range(1, g.size):
            self.copy(partial(ends, step))
        self.wait()
        total = total.astype(F32)
        for step in range(1, g.size):
            total = total + self.around[step - 1].astype(F32)
        return total.astype(BF16)

    def gather(self, k):
        g, rows = self.groups[k], self.rows[k]

        def ends(step):
            here = self.whole.at[pl.ds(pl.multiple_of(self.base[k] + g.place * rows, 16), rows)]
            return here, here, g.device(g.other(step))

        for step in range(1, g.size):
            self.copy(partial(ends, step))

    def advance(self, stage):
        count = len(self.groups)
        if 0 < stage <= count:
            self.add(stage - 1)
        else:
            self.wait()
        if stage < count:
            self.scatter(stage)
        elif stage < 2 * count:
            self.gather(2 * count - 1 - stage)


EARLY = (
    (0, 384, ("core", "batch", "chain")),
    (384, 896, ("core", "batch", "chain")),
    (896, 1280, ("core", "chain", "batch")),
)
LATE = ((0, 256, ("core", "batch", "chain")), (256, 384, ("core", "chain", "batch")))


def back_kernel(
    windows,
    sq_hbm,
    skv_hbm,
    dctx_hbm,
    e_hbm,
    g_hbm,
    pack_hbm,
    xs_hbm,
    dres_hbm,
    wq_hbm,
    wk_hbm,
    wv_hbm,
    rows_ref,
    dx_ref,
    early_ref,
    late_ref,
    sq_ref,
    skv_ref,
    dctx_ref,
    e_ref,
    g_ref,
    half_ref,
    xs_ref,
    dres_ref,
    wq_ref,
    wk_ref,
    wv_ref,
    in_sem,
    block_sem,
    dq_ref,
    dkv_ref,
    give_ref,
    take_ref,
    qkv_ref,
    halo_send,
    halo_arrive,
    out_sem,
    *scratch,
):
    step = pl.program_id(0)
    w = (windows - step) % windows
    slots = windows * WIN
    width_s = xs_ref.shape[0]
    batch, seq = lax.axis_index("batch"), lax.axis_index("seq")
    peers = lax.axis_size("seq")
    chains, used = [], 0
    for source, local, cuts in ((pack_hbm, half_ref, EARLY), (qkv_ref, None, LATE)):
        for first, last, names in cuts:
            size = 2 * len(names) + 4
            mine = local.at[:, first:last] if local is not None else None
            chains.append(Chain(names, source.at[:, first:last], scratch[used : used + size], mine))
            used += size
    soon, late = chains[: len(EARLY)], chains[len(EARLY) :]
    first_seq, last_seq = seq == 0, seq == peers - 1

    def halo(side):
        return pltpu.make_async_remote_copy(
            src_ref=give_ref.at[side],
            dst_ref=take_ref.at[1 - side],
            send_sem=halo_send.at[side],
            recv_sem=halo_arrive.at[1 - side],
            device_id=(batch, seq - 1 + 2 * side),
            device_id_type=MESH,
        )

    half_rows = half_ref.shape[0]
    ends = {
        "half": (pack_hbm.at[pl.ds(pl.multiple_of(seq % group_sizes()["core"] * half_rows, 16), half_rows)], half_ref),
        "sq": (sq_hbm, sq_ref),
        "skv": (skv_hbm, skv_ref),
        "dctx": (dctx_hbm, dctx_ref),
        "xs": (xs_hbm, xs_ref),
        "dres": (dres_hbm, dres_ref),
        "wq": (wq_hbm, wq_ref),
        "wk": (wk_hbm, wk_ref),
        "wv": (wv_hbm, wv_ref),
    }
    load = lambda name: pltpu.make_async_copy(*ends[name], in_sem.at[list(ends).index(name)])

    def blocks(number):
        slot, window = number % 2, (windows - number) % windows
        return [
            pltpu.make_async_copy(source.at[window], target.at[slot], block_sem.at[k, slot])
            for k, (source, target) in enumerate(((e_hbm, e_ref), (g_hbm, g_ref)))
        ]

    @pl.when(step == 0)
    def _():
        load("half").start()
        dkv_ref[...] = jnp.zeros_like(dkv_ref)
        take_ref[...] = jnp.zeros_like(take_ref)
        qkv_ref[...] = jnp.zeros_like(qkv_ref)
        barrier = pltpu.get_barrier_semaphore()
        count = 0
        for g in (Group(n) for n in ("core", "batch", "chain", "outer")):
            for k in range(1, g.size):
                pl.semaphore_signal(barrier, inc=1, device_id=g.device(g.other(k)), device_id_type=MESH)
                count += 1

        for move in (1, peers - 1):
            pl.semaphore_signal(
                barrier, inc=1, device_id=(batch, (seq + move) % peers), device_id_type=MESH
            )
        pl.semaphore_wait(barrier, count + 2)

        for c in soon:
            c.advance(0)
        for c in blocks(0):
            c.start()
        for name in ("sq", "skv", "dctx"):
            load(name).start()
        for c in blocks(1):
            c.start()
        for name in ("xs", "dres", "wq", "wk", "wv"):
            load(name).start()
        for name in ("sq", "skv", "dctx", "half"):
            load(name).wait()

    for c in blocks(step):
        c.wait()
    slot = step % 2
    at = pl.multiple_of(w * WIN, WIN)
    left = pl.ds(at, WIN)
    own = pl.ds(pl.multiple_of(at + WIN, WIN), WIN)
    right = pl.ds(pl.multiple_of(at + 2 * WIN, WIN), WIN)
    early_row, late_row = rows_ref[0:1, left], rows_ref[1:2, left]
    early_low, late_low = early_row.astype(BF16), late_row.astype(BF16)

    def one_head(head):
        rows = pl.ds(pl.multiple_of(head * PAD, PAD), PAD)
        query, grad = sq_ref[rows, left], dctx_ref[rows, left]
        stacked = lambda a: jnp.concatenate([a * early_low, a * late_low], axis=0)
        query_fold, grad_fold = stacked(query), stacked(grad)
        beside = lambda k: jnp.concatenate([skv_ref[k, rows, left], skv_ref[k, rows, right]], axis=0)
        keys_fold, values_fold = beside(0), beside(1)
        keys, values = skv_ref[0, rows, own], skv_ref[1, rows, own]
        e_own, e_side = e_ref[slot, head, :WIN, :], e_ref[slot, head, WIN:, :]
        d_own = (e_own.astype(F32) * (tn(values, grad) + g_ref[slot, head, :WIN, :].astype(F32))).astype(BF16)
        d_side = (
            e_side.astype(F32) * (tn(values_fold, grad_fold) + g_ref[slot, head, WIN:, :].astype(F32))
        ).astype(BF16)
        side = nn(keys_fold, d_side)
        d_query = nn(keys, d_own) + early_row * side[:PAD] + late_row * side[PAD:]
        dq_ref[rows, left] = (d_query * HD_S**-0.5).astype(BF16)
        for k, (a, a_fold, b, b_fold, scale) in enumerate(
            ((query, query_fold, d_own, d_side, 1.0 / LOG2E), (grad, grad_fold, e_own, e_side, None))
        ):
            fix = (lambda v: v * scale) if scale else (lambda v: v)
            side = fix(nt(a_fold, b_fold))
            dkv_ref[k, rows, own] += fix(nt(a, b))
            dkv_ref[k, rows, left] += side[:PAD]
            dkv_ref[k, rows, right] += side[PAD:]

    def body(pair, carry):
        one_head(2 * pair)
        one_head(2 * pair + 1)
        return carry

    def send_halo():
        for side, lanes in ((0, slice(0, WIN)), (1, slice(WIN + slots, 2 * WIN + slots))):
            give_ref[side] = dkv_ref[:, :, lanes].astype(BF16)

        @pl.when(jnp.logical_not(first_seq))
        def _():
            halo(0).start()

        @pl.when(jnp.logical_not(last_seq))
        def _():
            halo(1).start()

    def advance(which, stage):
        for c in which:
            c.advance(stage)

    half = PAIRS // 2
    plan = {
        (0, 0): [partial(advance, soon, 1)],
        (1, 1): [send_halo],
        (2, 0): [partial(advance, soon, 2)],
        (3, 0): [partial(advance, soon, 3)],
    }
    for part in range(2):
        lax.fori_loop(part * half, (part + 1) * half, body, 0, unroll=half)
        for k in range(windows):
            for action in plan.get((k, part), []):
                pl.when(step == k)(action)

    @pl.when(step < windows - 2)
    def _():
        for c in blocks(step + 2):
            c.start()

    @pl.when(step == windows - 1)
    def _():
        for name in ("xs", "dres", "wq", "wk", "wv"):
            load(name).wait()

        @pl.when(jnp.logical_not(first_seq))
        def _():
            halo(0).wait_send()
            halo(1).wait_recv()

        @pl.when(jnp.logical_not(last_seq))
        def _():
            halo(1).wait_send()
            halo(0).wait_recv()

        spot = pad_heads()
        plains = []
        for k in range(3):
            if k == 0:
                grad = dq_ref[...]
            else:
                mine = dkv_ref[k - 1, :, WIN : WIN + slots]
                first = mine[:, :WIN] + take_ref[0, k - 1].astype(F32)
                last = mine[:, slots - WIN :] + take_ref[1, k - 1].astype(F32)
                grad = jnp.concatenate([first, mine[:, WIN : slots - WIN], last], axis=1).astype(BF16)
            plain = tn(spot, grad).astype(BF16)
            plains.append(plain)
            qkv_ref[k * BLOCK : k * BLOCK + width_s, :width_s] = nt(xs_ref[...], plain).astype(BF16)
        advance(soon, 4)
        advance(late, 0)
        total = dres_ref[...]
        for w_ref, plain in zip((wq_ref, wk_ref, wv_ref), plains):
            total = total + nn(w_ref[...], plain)
        dx_ref[...] = total.astype(BF16)
        advance(late, 1)
        advance(late, 2)
        advance(soon, 5)
        advance(late, 3)
        advance(soon, 6)

        def put(group, cuts, target, first_sem):
            made = []
            for n, (c, (first, last, _)) in enumerate(zip(group, cuts)):
                made.append(pltpu.make_async_copy(c.whole, target.at[:, first:last], out_sem.at[first_sem + n]))
                made[-1].start()
            return made

        copies = put(soon, EARLY, early_ref, 0)
        advance(late, 4)
        advance(late, 5)
        advance(late, 6)
        copies += put(late, LATE, late_ref, len(EARLY))
        for c in copies:
            c.wait()


def back(sq, skv, dctx, e, g, rows, pack, xs, dres, wq, wk, wv):
    padded, slots = sq.shape
    windows = slots // WIN
    width_s = xs.shape[0]
    packed_rows = pack.shape[0]
    anywhere = pl.BlockSpec(memory_space=pl.ANY)
    held = lambda a: pltpu.VMEM(a.shape, a.dtype)
    scratch = [held(sq), held(skv), held(dctx)]
    scratch += [pltpu.VMEM((2,) + a.shape[1:], a.dtype) for a in (e, g)]
    scratch += [pltpu.VMEM((packed_rows // group_sizes()["core"], pack.shape[1]), BF16)]
    scratch += [held(a) for a in (xs, dres, wq, wk, wv)]
    scratch += [
        pltpu.SemaphoreType.DMA((9,)),
        pltpu.SemaphoreType.DMA((2, 2)),
        pltpu.VMEM((padded, slots), BF16),
        pltpu.VMEM((2, padded, slots + 2 * WIN), F32),
        pltpu.VMEM((2, 2, padded, WIN), BF16),
        pltpu.VMEM((2, 2, padded, WIN), BF16),
        pltpu.VMEM((packed_rows, QKV_LANES), BF16),
        pltpu.SemaphoreType.DMA((2,)),
        pltpu.SemaphoreType.DMA((2,)),
        pltpu.SemaphoreType.DMA((len(EARLY) + len(LATE),)),
    ]
    for first, last, names in EARLY + LATE:
        scratch += Chain.scratch(names, packed_rows, last - first)
    return pl.pallas_call(
        partial(back_kernel, windows),
        grid=(windows,),
        out_shape=[
            jax.ShapeDtypeStruct((width_s, slots), BF16),
            jax.ShapeDtypeStruct(pack.shape, BF16),
            jax.ShapeDtypeStruct((packed_rows, QKV_LANES), BF16),
        ],
        in_specs=[anywhere] * 11 + [VMEM],
        out_specs=[pl.BlockSpec((width_s, slots), lambda i: (0, 0)), anywhere, anywhere],
        scratch_shapes=scratch,
        compiler_params=pltpu.CompilerParams(
            vmem_limit_bytes=BIG,
            dimension_semantics=("arbitrary",),
            collective_id=0,
            has_side_effects=True,
        ),
    )(sq, skv, dctx, e, g, pack, xs, dres, wq, wk, wv, rows)


def unpack_kernel(
    every,
    width_t,
    early_hbm,
    late_hbm,
    dx_in_ref,
    dx_ref,
    loss_ref,
    gq_hbm,
    gk_hbm,
    gv_hbm,
    gwo_hbm,
    ginner_hbm,
    gouter_hbm,
    ghid_hbm,
    bouter_ref,
    binner_ref,
    gain_one_ref,
    shift_one_ref,
    gain_two_ref,
    shift_two_ref,
    early_ref,
    late_ref,
    gq_ref,
    gk_ref,
    gv_ref,
    gwo_ref,
    ginner_ref,
    gouter_ref,
    ghid_ref,
    in_sem,
    out_sem,
):
    width_s = gq_ref.shape[0]
    units = ginner_ref.shape[1]
    scale = 1.0 / every
    full = lambda v: v.astype(F32) * scale
    loads = [
        pltpu.make_async_copy(
            early_hbm.at[k * BLOCK : (k + 1) * BLOCK], early_ref.at[k * BLOCK : (k + 1) * BLOCK], in_sem.at[k]
        )
        for k in range(3)
    ]
    loads.append(pltpu.make_async_copy(late_hbm, late_ref, in_sem.at[3]))
    for c in loads:
        c.start()
    stores = []

    def store(source, target):
        stores.append(pltpu.make_async_copy(source, target, out_sem.at[len(stores)]))
        stores[-1].start()

    dx_ref[...] = dx_in_ref[...]
    loads[0].wait()
    gouter_ref[...] = full(early_ref[:width_s, :units])
    store(gouter_ref, gouter_hbm)
    loads[1].wait()
    ginner_ref[...] = full(early_ref[BLOCK : BLOCK + width_s, :units])
    store(ginner_ref, ginner_hbm)
    binner_ref[...] = full(early_ref[BLOCK + width_s : BLOCK + width_s + 8, :units])[0]
    loads[2].wait()
    third = slice(2 * BLOCK, 2 * BLOCK + width_s)
    ghid_ref[...] = full(early_ref[third, :width_t])
    store(ghid_ref, ghid_hbm)
    gwo_ref[...] = full(early_ref[third, width_t : width_t + width_s])
    store(gwo_ref, gwo_hbm)
    loads[3].wait()
    for k, (ref, hbm) in enumerate(((gq_ref, gq_hbm), (gk_ref, gk_hbm), (gv_ref, gv_hbm))):
        ref[...] = full(late_ref[k * BLOCK : k * BLOCK + width_s, :width_s])
        store(ref, hbm)
    last = units // 128 * 128
    lane = lax.broadcasted_iota(jnp.int32, (width_s, 128), 1)
    columns = jnp.where(
        lane < 4,
        full(early_ref[third, SUMS_AT : SUMS_AT + 128]),
        full(early_ref[:width_s, last : last + 128]),
    )
    turned = jnp.transpose(columns)
    for k, ref in enumerate((gain_one_ref, shift_one_ref, gain_two_ref, shift_two_ref)):
        ref[...] = turned[k]
    bouter_ref[...] = turned[units - last]
    part = early_ref[2 * BLOCK + width_s : 2 * BLOCK + width_s + 8, :128].astype(F32)
    total = jnp.sum(jnp.sum(part, axis=0, keepdims=True), axis=1, keepdims=True)
    loss_ref[...] = total
    for c in stores:
        c.wait()


def unpack(every, width_t, units, early, late, dx):
    width_s = dx.shape[0]
    sds = lambda *shape: jax.ShapeDtypeStruct(shape, F32)
    square = sds(width_s, width_s)
    large = [square, square, square, square, sds(width_s, units), sds(width_s, units), sds(width_s, width_t)]
    vectors = [sds(width_s), sds(units)] + [sds(width_s)] * 4
    anywhere = pl.BlockSpec(memory_space=pl.ANY)
    return pl.pallas_call(
        partial(unpack_kernel, every, width_t),
        out_shape=[jax.ShapeDtypeStruct(dx.shape, BF16), sds(1, 1)] + large + vectors,
        in_specs=[anywhere, anywhere, VMEM],
        out_specs=[VMEM] * 2 + [anywhere] * len(large) + [VMEM] * len(vectors),
        scratch_shapes=[pltpu.VMEM(early.shape, BF16), pltpu.VMEM(late.shape, BF16)]
        + [pltpu.VMEM(a.shape, F32) for a in large]
        + [pltpu.SemaphoreType.DMA((4,)), pltpu.SemaphoreType.DMA((len(large),))],
        compiler_params=pltpu.CompilerParams(vmem_limit_bytes=BIG),
    )(early, late, dx)


def local(
    inputs,
    teacher_input,
    filled_slot_mask,
    seg_lengths,
    query_weight,
    key_weight,
    value_weight,
    w_output,
    gain_one,
    shift_one,
    w_inner,
    b_inner,
    w_outer,
    b_outer,
    gain_two,
    shift_two,
    w_hidden,
    teacher_query_weight,
    teacher_key_weight,
    teacher_value_weight,
    teacher_output,
    teacher_gain_one,
    teacher_shift_one,
    teacher_inner,
    teacher_outer,
    teacher_gain_two,
    teacher_shift_two,
):
    xs = jnp.transpose(inputs[0])
    xt = teacher_input[0]
    slots, width_t = xt.shape
    width_s = xs.shape[0]
    stats, loss_rows, rows, tctx, sctx, sq, skv, e, g = attend(
        filled_slot_mask,
        seg_lengths,
        xt,
        xs,
        teacher_query_weight,
        teacher_key_weight,
        teacher_value_weight,
        query_weight,
        key_weight,
        value_weight,
    )
    devices = lax.axis_size("seq") * lax.axis_size("batch")
    sizes = group_sizes()
    unit = 16 * sizes["core"] * sizes["batch"] * sizes["chain"]
    packed_rows = -(-3 * BLOCK // unit) * unit
    out, dctx, dres, pack = dense(
        packed_rows,
        (
            xt,
            tctx,
            teacher_output,
            xs,
            sctx,
            teacher_inner,
            teacher_outer,
            w_output,
            w_inner,
            jnp.transpose(w_outer),
            w_hidden,
        ),
        (stats, rows, loss_rows)
        + (
            teacher_gain_one,
            teacher_shift_one,
            teacher_gain_two,
            teacher_shift_two,
            gain_one,
            shift_one,
            b_outer,
            gain_two,
            shift_two,
            b_inner,
        ),
    )
    dx, early, late = back(sq, skv, dctx, e, g, rows, pack, xs, dres, query_weight, key_weight, value_weight)
    dx, loss, gq, gk, gv, gwo, ginner, gouter, ghid, *vectors = unpack(
        slots * devices, width_t, w_inner.shape[1], early, late, dx
    )
    g_b_outer, g_b_inner, g_gain_one, g_shift_one, g_gain_two, g_shift_two = vectors
    return (
        jnp.transpose(out)[None],
        jnp.transpose(dx)[None],
        loss[0, 0] / (slots * devices * width_t),
        gq,
        gk,
        gv,
        gwo,
        g_gain_one,
        g_shift_one,
        ginner,
        g_b_inner,
        jnp.transpose(gouter),
        g_b_outer,
        g_gain_two,
        g_shift_two,
        ghid,
    )


def solution(mesh):
    row_split = P("batch", "seq", None)
    return jax.shard_map(
        local,
        mesh=mesh,
        in_specs=(row_split, row_split, P("batch", None), P("batch", None)) + (P(),) * 23,
        out_specs=(row_split, row_split) + (P(),) * 14,
        check_vma=False,
    )
```

```python
from functools import partial

import jax
import jax.numpy as jnp
from jax import lax
from jax.experimental import pallas as pl
from jax.experimental.pallas import tpu as pltpu
from jax.sharding import PartitionSpec as P

HEADS = 12
HD_S = 26
HD_T = 64
WIN = 256
PAD = 32
SLOT_ONE = 26
PAIRS = HEADS // 2
CHUNK = 64
TAIL = 16
SLOTS = 4
BLOCK = 320
SUMS_AT = 1152
QKV_LANES = 384
MESH = pl.DeviceIdType.MESH
EPSILON = 1e-05
NEGATIVE = -1e30
LOG2E = 1.4426950408889634
F32 = jnp.float32
BF16 = jnp.bfloat16
VMEM = pl.BlockSpec(memory_space=pltpu.VMEM)
BIG = 60 << 20


def mm(left, right, dims):
    return lax.dot_general(left, right, ((dims[:1], dims[1:]), ((), ())), preferred_element_type=F32)


def nn(left, right):
    return mm(left, right, (1, 0))


def tn(left, right):
    return mm(left, right, (0, 0))


def nt(left, right):
    return mm(left, right, (1, 1))


def tt(left, right):
    return mm(left, right, (0, 1))


def pad_heads():
    row = lax.broadcasted_iota(jnp.int32, (HEADS * PAD, HEADS * HD_S), 0)
    col = lax.broadcasted_iota(jnp.int32, (HEADS * PAD, HEADS * HD_S), 1)
    spot = jnp.zeros((HEADS * PAD, HEADS * HD_S), F32)
    for head in range(HEADS):
        here = (row - head * PAD == col - head * HD_S) & (col >= head * HD_S) & (col < (head + 1) * HD_S)
        spot = jnp.where(here, 1.0, spot)
    return spot.astype(BF16)


def window_rows(mask_ref, lengths_ref, seq_index, windows, row_windows):
    lengths = lengths_ref[...].astype(F32)
    order = lax.broadcasted_iota(jnp.int32, lengths.shape, 1)
    lane = lax.broadcasted_iota(jnp.int32, (1, WIN), 1).astype(F32)
    out = []
    for j in range(windows + 2):
        number = seq_index * windows + (j - 1)
        inside = (number >= 0) & (number < row_windows)
        safe = jnp.clip(number, 0, row_windows - 1)
        start = jnp.sum(jnp.where(order < safe, lengths, 0.0), axis=1, keepdims=True)
        offset = start - (safe * WIN).astype(F32)
        late = (lane >= offset).astype(F32)
        filled = mask_ref[:, pl.ds(pl.multiple_of(safe * WIN, WIN), WIN)]
        filled = jnp.where(inside, filled.astype(F32), 0.0)
        out.append((late, filled))
    return out


def stack_rows(*rows):
    n = rows[0].shape[1]
    index = lax.broadcasted_iota(jnp.int32, (8, n), 0)
    block = jnp.zeros((8, n), F32)
    for k, row in enumerate(rows):
        block = jnp.where(index == k, row, block)
    return block.astype(BF16)


def attend_kernel(
    windows,
    row_windows,
    mask_ref,
    lengths_ref,
    xt_hbm,
    xs_ref,
    wtq_hbm,
    wtk_hbm,
    wtv_hbm,
    wq_ref,
    wk_ref,
    wv_ref,
    stats_ref,
    loss_ref,
    rows_ref,
    tctx_hbm,
    sctx_hbm,
    sq_hbm,
    skv_hbm,
    saved_e_hbm,
    saved_g_hbm,
    x_ref,
    xs_side_ref,
    wt_ref,
    bias_ref,
    wst_ref,
    tq_ref,
    tk_ref,
    tv_ref,
    sq_ref,
    skv_ref,
    tctx_ref,
    sctx_ref,
    e_ref,
    g_ref,
    work_ref,
    low_ref,
    in_sem,
    halo_send,
    halo_arrive,
    kv_sem,
    out_sem,
):
    slots = windows * WIN
    batch, seq = lax.axis_index("batch"), lax.axis_index("seq")
    peers = lax.axis_size("seq")
    has_left, has_right = seq > 0, seq < peers - 1
    width_t = x_ref.shape[1]
    extended = slots + 2 * WIN

    barrier = pltpu.get_barrier_semaphore()
    for move in (1, peers - 1):
        pl.semaphore_signal(barrier, inc=1, device_id=(batch, (seq + move) % peers), device_id_type=MESH)
    loads = [pltpu.make_async_copy(xt_hbm, x_ref.at[pl.ds(WIN, slots)], in_sem.at[0])]
    for k, w_hbm in enumerate((wtq_hbm, wtk_hbm, wtv_hbm)):
        loads.append(pltpu.make_async_copy(w_hbm, wt_ref.at[k], in_sem.at[1 + k]))
    for c in loads:
        c.start()
    pl.semaphore_wait(barrier, 2)

    def halo(side):
        device = (batch, seq - 1 + 2 * side)
        first = side * (slots - WIN)
        return [
            pltpu.make_async_remote_copy(
                src_ref=xt_hbm.at[pl.ds(first, WIN)],
                dst_ref=x_ref.at[pl.ds((1 - side) * (WIN + slots), WIN)],
                send_sem=halo_send.at[0, side],
                recv_sem=halo_arrive.at[0, 1 - side],
                device_id=device,
                device_id_type=MESH,
            ),
            pltpu.make_async_remote_copy(
                src_ref=xs_ref.at[:, pl.ds(first, WIN)],
                dst_ref=xs_side_ref.at[1 - side],
                send_sem=halo_send.at[1, side],
                recv_sem=halo_arrive.at[1, 1 - side],
                device_id=device,
                device_id_type=MESH,
            ),
        ]

    for side, present in ((0, has_left), (1, has_right)):

        @pl.when(present)
        def _():
            for c in halo(side):
                c.start()

        @pl.when(jnp.logical_not(present))
        def _():
            x_ref[side * (WIN + slots) : side * (WIN + slots) + WIN, :] = jnp.zeros((WIN, width_t), BF16)
            xs_side_ref[side] = jnp.zeros(xs_side_ref.shape[1:], BF16)

    info = window_rows(mask_ref, lengths_ref, seq, windows, row_windows)
    eye = lax.broadcasted_iota(jnp.int32, (WIN, WIN), 0) == lax.broadcasted_iota(jnp.int32, (WIN, WIN), 1)
    rows_ref[...] = jnp.zeros_like(rows_ref)
    for w in range(windows):
        late, filled = info[w + 1]
        late_l, filled_l = info[w]
        late_r, filled_r = info[w + 2]
        early = 1.0 - late
        here = slice(w * WIN, (w + 1) * WIN)
        rows_ref[0:1, here] = early
        rows_ref[1:2, here] = late
        rows_ref[2:3, here] = filled
        query = stack_rows(early, late)
        own = tn(stack_rows(NEGATIVE * (1.0 - early * filled), NEGATIVE * (1.0 - late * filled)), query)
        bias_ref[w, :WIN, :] = jnp.where(eye, 0.0, own)
        bias_ref[w, WIN:, :] = tn(
            stack_rows(
                NEGATIVE * (1.0 - late_l * filled_l), NEGATIVE * (1.0 - (1.0 - late_r) * filled_r)
            ),
            query,
        )
    loss_ref[...] = jnp.zeros_like(loss_ref)
    stats_ref[...] = jnp.zeros_like(stats_ref)
    spot = pad_heads()
    padded = HEADS * PAD
    row = lax.broadcasted_iota(jnp.int32, (padded, 1), 0) % PAD
    ones = (row >= SLOT_ONE) & (row < SLOT_ONE + 3)

    xs = xs_ref[...]
    for k, w_ref in enumerate((wq_ref, wk_ref, wv_ref)):
        wst_ref[k] = nt(spot, w_ref[...]).astype(BF16)
        made = nn(wst_ref[k], xs)
        if k == 0:
            sq_ref[...] = (made * (LOG2E * HD_S**-0.5)).astype(BF16)
        else:
            if k == 2:
                made = jnp.where(ones, 1.0, made)
            skv_ref[k - 1, :, WIN : WIN + slots] = made.astype(BF16)
    tail = (lax.broadcasted_iota(jnp.int32, (TAIL, extended), 0) == 0).astype(BF16)
    for head in range(HEADS):
        tv_ref[head * (HD_T + TAIL) + HD_T : (head + 1) * (HD_T + TAIL), :] = tail

    def put_values(made, first_head, lanes):
        for j in range(made.shape[0] // HD_T):
            at = (first_head + j) * (HD_T + TAIL)
            tv_ref[at : at + HD_T, lanes] = made[j * HD_T : (j + 1) * HD_T]

    part = width_t // 2
    loads[0].wait()
    for k in range(3):
        loads[1 + k].wait()
        for half in range(2):
            made = tt(wt_ref[k, :, half * part : (half + 1) * part], x_ref[WIN : WIN + slots, :])
            if k == 0:
                tq_ref[half * part : (half + 1) * part, :] = (made * (LOG2E * HD_T**-0.5)).astype(BF16)
            elif k == 1:
                tk_ref[half * part : (half + 1) * part, WIN : WIN + slots] = made.astype(BF16)
            else:
                put_values(made.astype(BF16), half * HEADS // 2, slice(WIN, WIN + slots))
    for side, present in ((0, has_left), (1, has_right)):

        @pl.when(present)
        def _():
            for sent, landed in zip(halo(side), halo(1 - side)):
                sent.wait_send()
                landed.wait_recv()

        lanes = slice(side * (WIN + slots), side * (WIN + slots) + WIN)
        for k in (1, 2):
            made = tt(wt_ref[k], x_ref[lanes, :]).astype(BF16)
            if k == 1:
                tk_ref[:, lanes] = made
            else:
                put_values(made, 0, lanes)
            made = nn(wst_ref[k], xs_side_ref[side])
            if k == 2:
                made = jnp.where(ones, 1.0, made)
            skv_ref[k - 1, :, lanes] = made.astype(BF16)
    finals = [
        pltpu.make_async_copy(sq_ref, sq_hbm, kv_sem.at[0]),
        pltpu.make_async_copy(skv_ref, skv_hbm, kv_sem.at[1]),
    ]
    for c in finals:
        c.start()

    def stores(pair, which):
        slot = pair % 2
        t_rows = pl.ds(pl.multiple_of(pair * 2 * HD_T, 2 * HD_T), 2 * HD_T)
        s_rows = pl.ds(pl.multiple_of(pair * 2 * PAD, 2 * PAD), 2 * PAD)
        heads = pl.ds(pair * 2, 2)
        ends = (
            (e_ref.at[slot], saved_e_hbm.at[:, heads]),
            (g_ref.at[slot], saved_g_hbm.at[:, heads]),
            (tctx_ref.at[t_rows], tctx_hbm.at[t_rows]),
            (sctx_ref.at[s_rows], sctx_hbm.at[s_rows]),
        )
        return [pltpu.make_async_copy(*ends[k], out_sem.at[k, pair]) for k in which]

    def one_pair(pair, carry):
        @pl.when(pair >= 2)
        def _():
            for c in stores(pair - 2, (0, 1)):
                c.wait()

        attend_pair(pair)
        for c in stores(pair, range(4)):
            c.start()
        return carry

    def attend_pair(pair):
        e_out, g_out = e_ref.at[pair % 2], g_ref.at[pair % 2]
        def rows_of(w):
            left = slice(w * WIN, (w + 1) * WIN)
            own = slice((w + 1) * WIN, (w + 2) * WIN)
            right = slice((w + 2) * WIN, (w + 3) * WIN)
            return left, own, right, rows_ref[0:1, left], rows_ref[1:2, left], rows_ref[2:3, left]

        def first_pass(w, q_ref, k_ref, rows, work_ref):
            left, own, right, early, late, _ = rows_of(w)
            query = q_ref[rows, left]
            query_fold = jnp.concatenate([query * early.astype(BF16), query * late.astype(BF16)], axis=0)
            keys = k_ref[rows, own]
            keys_fold = jnp.concatenate([k_ref[rows, left], k_ref[rows, right]], axis=0)
            top = None
            for part, (a, b) in enumerate(((keys, query), (keys_fold, query_fold))):
                raw = tn(a, b)
                for c in range(0, WIN, CHUNK):
                    block = raw[c : c + CHUNK] + bias_ref[w, part * WIN + c : part * WIN + c + CHUNK, :]
                    work_ref[part * WIN + c : part * WIN + c + CHUNK, :] = block
                    for r in range(0, CHUNK, 8):
                        piece = block[r : r + 8]
                        top = piece if top is None else jnp.maximum(top, piece)
            return jnp.max(top, axis=0, keepdims=True)

        def second_pass(work_ref, top, low_ref):
            for c in range(0, 2 * WIN, CHUNK):
                e = jnp.exp2(work_ref[c : c + CHUNK, :] - top)
                work_ref[c : c + CHUNK, :] = e
                low_ref[c : c + CHUNK, :] = e.astype(BF16)

        def mix(w, v_ref, rows, low_ref, head_width):
            left, own, right, early, late, _ = rows_of(w)
            values = v_ref[rows, own]
            values_fold = jnp.concatenate([v_ref[rows, left], v_ref[rows, right]], axis=0)
            mixed = nn(values, low_ref[:WIN, :])
            side = nn(values_fold, low_ref[WIN:, :])
            n = values.shape[0]
            mixed = mixed + early * side[:n] + late * side[n:]
            inverse = 1.0 / mixed[head_width : head_width + 1]
            return mixed[: -TAIL if head_width == HD_T else n] * inverse, inverse

        units = [(w, h) for w in range(windows) for h in range(2)]
        state = {}

        def refs(u):
            w, h = units[u]
            head = 2 * pair + h
            t_rows = pl.ds(pl.multiple_of(head * HD_T, HD_T), HD_T)
            s_rows = pl.ds(pl.multiple_of(head * PAD, PAD), PAD)
            v_rows = pl.ds(pl.multiple_of(head * (HD_T + TAIL), TAIL), HD_T + TAIL)
            slot = u % SLOTS
            return w, h, t_rows, s_rows, v_rows, work_ref.at[2 * slot], work_ref.at[2 * slot + 1], low_ref.at[slot]

        def score_stage(u):
            w, h, t_rows, s_rows, _, work_t, work_s, _ = refs(u)
            state[u] = [
                first_pass(w, tq_ref, tk_ref, t_rows, work_t),
                first_pass(w, sq_ref, skv_ref.at[0], s_rows, work_s),
            ]

        def power_stage(u):
            w, h, _, _, _, work_t, work_s, low_t = refs(u)
            second_pass(work_t, state[u][0], low_t)
            second_pass(work_s, state[u][1], e_out.at[w, h])

        def mix_stage(u):
            w, h, t_rows, s_rows, v_rows, _, _, low_t = refs(u)
            left = rows_of(w)[0]
            t_mixed, t_inv = mix(w, tv_ref, v_rows, low_t, HD_T)
            s_mixed, s_inv = mix(w, skv_ref.at[1], s_rows, e_out.at[w, h], SLOT_ONE)
            tctx_ref[t_rows, left] = t_mixed.astype(BF16)
            sctx_ref[s_rows, left] = s_mixed
            state[u] = [t_inv, s_inv]

        def gap_stage(u):
            w, h, _, _, _, work_t, work_s, _ = refs(u)
            left, _, _, _, _, filled = rows_of(w)
            t_inv, s_inv = state.pop(u)
            width = 2.0 * HEADS * HD_T
            scale_s = (width * filled) * s_inv * s_inv
            scale_t = (width * filled) * s_inv * t_inv
            square = jnp.zeros((8, WIN), F32)
            cross = jnp.zeros((8, WIN), F32)
            for c in range(0, 2 * WIN, CHUNK):
                s = work_s[c : c + CHUNK, :]
                gap = s * scale_s - work_t[c : c + CHUNK, :] * scale_t
                g_out[w, h, c : c + CHUNK, :] = gap.astype(BF16)
                for r in range(0, CHUNK, 8):
                    piece = gap[r : r + 8]
                    square += piece * piece
                    cross += piece * s[r : r + 8]
            square = jnp.sum(square, axis=0, keepdims=True)
            cross = jnp.sum(cross, axis=0, keepdims=True)
            back = 1.0 / (s_inv * width)
            stats_ref[pair, h : h + 1, left] = s_inv
            stats_ref[pair, 2 + h : 3 + h, left] = cross
            loss_ref[0:1, left] += square * back * back

        last = len(units)
        for u in range(last + 2):
            if u < last:
                score_stage(u)
            if 0 <= u - 1 < last:
                power_stage(u - 1)
            if 0 <= u - 2 < last:
                mix_stage(u - 2)
                gap_stage(u - 2)


    lax.fori_loop(0, PAIRS, one_pair, 0)
    for pair in range(PAIRS):
        for c in stores(pair, range(0 if pair >= PAIRS - 2 else 2, 4)):
            c.wait()
    for c in finals:
        c.wait()


def attend(mask, lengths, xt, xs, wtq, wtk, wtv, wq, wk, wv):
    slots, width_t = xt.shape
    width_s = xs.shape[0]
    windows = slots // WIN
    row_windows = mask.shape[1] // WIN
    padded = HEADS * PAD
    extended = slots + 2 * WIN
    sds = jax.ShapeDtypeStruct
    anywhere = pl.BlockSpec(memory_space=pl.ANY)
    saved = (windows, HEADS, 2 * WIN, WIN)
    return pl.pallas_call(
        partial(attend_kernel, windows, row_windows),
        out_shape=(
            sds((PAIRS, 8, slots), F32),
            sds((8, slots), F32),
            sds((8, slots), F32),
            sds((width_t, slots), BF16),
            sds((padded, slots), F32),
            sds((padded, slots), BF16),
            sds((2, padded, extended), BF16),
            sds(saved, BF16),
            sds(saved, BF16),
        ),
        in_specs=[VMEM, VMEM, anywhere, VMEM] + [anywhere] * 3 + [VMEM] * 3,
        out_specs=[VMEM] * 3 + [anywhere] * 6,
        scratch_shapes=[
            pltpu.VMEM((extended, width_t), BF16),
            pltpu.VMEM((2, width_s, WIN), BF16),
            pltpu.VMEM((3, width_t, width_t), BF16),
            pltpu.VMEM((windows, 2 * WIN, WIN), F32),
            pltpu.VMEM((3, padded, width_s), BF16),
            pltpu.VMEM((width_t, slots), BF16),
            pltpu.VMEM((width_t, extended), BF16),
            pltpu.VMEM((HEADS * (HD_T + TAIL), extended), BF16),
            pltpu.VMEM((padded, slots), BF16),
            pltpu.VMEM((2, padded, extended), BF16),
            pltpu.VMEM((width_t, slots), BF16),
            pltpu.VMEM((padded, slots), F32),
            pltpu.VMEM((2, windows, 2, 2 * WIN, WIN), BF16),
            pltpu.VMEM((2, windows, 2, 2 * WIN, WIN), BF16),
            pltpu.VMEM((2 * SLOTS, 2 * WIN, WIN), F32),
            pltpu.VMEM((SLOTS, 2 * WIN, WIN), BF16),
            pltpu.SemaphoreType.DMA((4,)),
            pltpu.SemaphoreType.DMA((2, 2)),
            pltpu.SemaphoreType.DMA((2, 2)),
            pltpu.SemaphoreType.DMA((2,)),
            pltpu.SemaphoreType.DMA((4, PAIRS)),
        ],
        compiler_params=pltpu.CompilerParams(
            vmem_limit_bytes=BIG, collective_id=1, has_side_effects=True
        ),
    )(mask, lengths, xt, xs, wtq, wtk, wtv, wq, wk, wv)


def normalize(values, gain, shift):
    n = values.shape[0]
    center = values - jnp.sum(values, axis=0, keepdims=True) * (1.0 / n)
    rscale = lax.rsqrt(jnp.sum(center * center, axis=0, keepdims=True) * (1.0 / n) + EPSILON)
    unit = center * rscale
    return unit * gain + shift, unit, rscale


def normalize_back(grad, unit, rscale, gain):
    n = grad.shape[0]
    scaled = grad * gain
    first = jnp.sum(scaled, axis=0, keepdims=True) * (1.0 / n)
    second = jnp.sum(scaled * unit, axis=0, keepdims=True) * (1.0 / n)
    return rscale * (scaled - first - unit * second)


def fold_lanes(values):
    total = values[:, :128]
    for at in range(128, values.shape[1], 128):
        total = total + values[:, at : at + 128]
    return total


ROOT_HALF = 0.7071067811865476
ROOT_PI = 0.3989422804014327


DENSE_IN = ("xt", "tctx", "two", "xs", "sctx", "tin", "tout", "wo", "w1", "w2", "wh")


def dense_kernel(
    xt_hbm,
    tctx_hbm,
    two_hbm,
    xs_hbm,
    sctx_hbm,
    tin_hbm,
    tout_hbm,
    wo_hbm,
    w1_hbm,
    w2_hbm,
    wh_hbm,
    stats_ref,
    rows_ref,
    loss_ref,
    t_gain_one_ref,
    t_shift_one_ref,
    t_gain_two_ref,
    t_shift_two_ref,
    gain_one_ref,
    shift_one_ref,
    b_outer_ref,
    gain_two_ref,
    shift_two_ref,
    b_inner_ref,
    out_hbm,
    dctx_hbm,
    dres_hbm,
    pack_hbm,
    xt_ref,
    tctx_ref,
    two_ref,
    xs_ref,
    sctx_ref,
    tin_ref,
    tout_ref,
    wo_ref,
    w1_ref,
    w2_ref,
    wh_ref,
    out_ref,
    dctx_ref,
    dres_ref,
    pack_ref,
    act_ref,
    slope_ref,
    in_sem,
    out_sem,
):
    sources = (
        xt_hbm, tctx_hbm, two_hbm, xs_hbm, sctx_hbm, tin_hbm, tout_hbm, wo_hbm, w1_hbm, w2_hbm, wh_hbm
    )
    targets = (xt_ref, tctx_ref, two_ref, xs_ref, sctx_ref, tin_ref, tout_ref, wo_ref, w1_ref, w2_ref, wh_ref)
    loads = {
        name: pltpu.make_async_copy(source, target, in_sem.at[k])
        for k, (name, source, target) in enumerate(zip(DENSE_IN, sources, targets))
    }
    for c in loads.values():
        c.start()
    width_s, units_s = w1_ref.shape
    width_t, units_t = tin_ref.shape
    slots = xt_ref.shape[0]
    low = lambda v: v.astype(BF16)
    stores = []

    def store(source, target):
        stores.append(pltpu.make_async_copy(source, target, out_sem.at[len(stores)]))
        stores[-1].start()

    def columns(*refs):
        n = refs[0].shape[0]
        index = lax.broadcasted_iota(jnp.int32, (8, n), 0)
        block = jnp.zeros((8, n), F32)
        for k, ref in enumerate(refs):
            block = jnp.where(index == k, ref[...].reshape(1, n), block)
        turned = jnp.transpose(block)
        return [turned[:, k : k + 1] for k in range(len(refs))]

    t_gain_one, t_shift_one, t_gain_two, t_shift_two = columns(
        t_gain_one_ref, t_shift_one_ref, t_gain_two_ref, t_shift_two_ref
    )
    gain_one, shift_one, b_outer, gain_two, shift_two = columns(
        gain_one_ref, shift_one_ref, b_outer_ref, gain_two_ref, shift_two_ref
    )
    (b_inner,) = columns(b_inner_ref)
    spot = pad_heads()
    pack_ref[...] = jnp.zeros_like(pack_ref)
    act_ref[units_s:, :] = jnp.ones((act_ref.shape[0] - units_s, slots), BF16)
    for name in ("xt", "tctx", "two"):
        loads[name].wait()
    start = jnp.transpose(xt_ref[...]).astype(F32) + tn(two_ref[...], tctx_ref[...])
    t_normed = normalize(start, t_gain_one, t_shift_one)[0]
    t_low = low(t_normed)
    t_sum = t_normed
    for name in ("xs", "sctx", "tin", "tout"):
        loads[name].wait()
    for at in range(0, units_t, width_t):
        pre = tn(tin_ref[:, at : at + width_t], t_low)
        active = low(0.5 * pre * (1.0 + lax.erf(pre * ROOT_HALF)))
        t_sum = t_sum + tn(tout_ref[at : at + width_t, :], active)
    target = normalize(t_sum, t_gain_two, t_shift_two)[0]
    for name in ("wo", "w1", "w2", "wh"):
        loads[name].wait()
    wop = low(nn(spot, wo_ref[...]))
    context = sctx_ref[...]
    context_low = low(context)
    normed, unit_one, rscale_one = normalize(
        xs_ref[...].astype(F32) + tn(wop, context_low), gain_one, shift_one
    )
    normed_low = low(normed)
    pre = tn(w1_ref[...], normed_low) + b_inner
    half = 0.5 * (1.0 + lax.erf(pre * ROOT_HALF))
    slope_ref[...] = half + pre * (ROOT_PI * jnp.exp(-0.5 * pre * pre))
    act_ref[:units_s, :] = low(pre * half)
    student, unit_two, rscale_two = normalize(
        normed + nn(w2_ref[...], act_ref[:units_s, :]) + b_outer, gain_two, shift_two
    )
    student_low = low(student)
    out_ref[...] = student_low
    store(out_ref, out_hbm)
    gap = tn(wh_ref[...], student_low) - target
    filled = rows_ref[2:3, :]
    masked = filled * gap
    d_proj = low(2.0 * masked)
    third = slice(2 * BLOCK, 2 * BLOCK + width_s)
    pack_ref[third, :width_t] = low(nt(student_low, d_proj))
    d_student = nn(wh_ref[...], d_proj)
    d_two = normalize_back(d_student, unit_two, rscale_two, gain_two)
    d_outer = low(d_two)
    pack_ref[:width_s, :] = low(nt(d_outer, act_ref[...]))
    store(pack_ref.at[:BLOCK], pack_hbm.at[:BLOCK])
    d_inner = low(tn(w2_ref[...], d_outer) * slope_ref[...])
    pack_ref[BLOCK : BLOCK + width_s, :units_s] = low(nt(normed_low, d_inner))
    pack_ref[BLOCK + width_s : BLOCK + width_s + 8, :units_s] = low(nt(jnp.ones((8, slots), BF16), d_inner))
    store(pack_ref.at[BLOCK : 2 * BLOCK], pack_hbm.at[BLOCK : 2 * BLOCK])
    d_normed = nn(w1_ref[...], d_inner) + d_two
    d_one = normalize_back(d_normed, unit_one, rscale_one, gain_one)
    dres_ref[...] = d_one
    store(dres_ref, dres_hbm)
    d_att = low(d_one)
    gwo = low(nt(context_low, d_att))
    pack_ref[third, width_t : width_t + width_s] = low(tn(spot, gwo))
    d_context = nn(wop, d_att)
    row = lax.broadcasted_iota(jnp.int32, (PAD, slots), 0)
    for head in range(HEADS):
        pair, h = head // 2, head % 2
        inverse = stats_ref[pair, h : h + 1, :]
        cross = stats_ref[pair, 2 + h : 3 + h, :]
        rows = slice(head * PAD, (head + 1) * PAD)
        part = low(d_context[rows] * inverse).astype(F32)
        delta = -jnp.sum(part * context[rows], axis=0, keepdims=True) - inverse * cross
        high = low(delta).astype(F32)
        rest = delta - high
        middle = low(rest).astype(F32)
        part = jnp.where(row == SLOT_ONE, high, part)
        part = jnp.where(row == SLOT_ONE + 1, middle, part)
        part = jnp.where(row == SLOT_ONE + 2, rest - middle, part)
        dctx_ref[rows, :] = low(part)
    store(dctx_ref, dctx_hbm)
    lane = lax.broadcasted_iota(jnp.int32, (width_s, 128), 1)
    sums = jnp.zeros((width_s, 128), F32)
    for k, values in enumerate((d_normed * unit_one, d_normed, d_student * unit_two, d_student)):
        sums = jnp.where(lane == k, jnp.sum(fold_lanes(values), axis=1, keepdims=True), sums)
    pack_ref[third, SUMS_AT : SUMS_AT + 128] = low(sums)
    square = jnp.sum(fold_lanes(masked * gap).reshape(-1, 8, 128), axis=0)
    row = lax.broadcasted_iota(jnp.int32, (8, 128), 0)
    for c in range(slots // 128):
        square += jnp.where(row == c % 8, width_t * loss_ref[0:1, c * 128 : (c + 1) * 128], 0.0)
    pack_ref[2 * BLOCK + width_s : 2 * BLOCK + width_s + 8, :128] = low(square)
    store(pack_ref.at[2 * BLOCK :], pack_hbm.at[2 * BLOCK :])
    for c in stores:
        c.wait()


def dense(packed_rows, big, small):
    xt, tctx, two, xs, sctx, tin, tout, wo, w1, w2, wh = big
    slots, width_t = xt.shape
    width_s, units_s = w1.shape
    padded = HEADS * PAD
    inner_pad = -(-units_s // 128) * 128
    sds = jax.ShapeDtypeStruct
    outs = [
        sds((width_s, slots), BF16),
        sds((padded, slots), BF16),
        sds((width_s, slots), F32),
        sds((packed_rows, inner_pad), BF16),
    ]
    anywhere = pl.BlockSpec(memory_space=pl.ANY)
    return pl.pallas_call(
        dense_kernel,
        out_shape=outs,
        in_specs=[anywhere] * len(big) + [VMEM] * len(small),
        out_specs=[anywhere] * len(outs),
        scratch_shapes=[pltpu.VMEM(a.shape, a.dtype) for a in big]
        + [pltpu.VMEM(a.shape, a.dtype) for a in outs]
        + [
            pltpu.VMEM((inner_pad, slots), BF16),
            pltpu.VMEM((units_s, slots), F32),
            pltpu.SemaphoreType.DMA((len(big),)),
            pltpu.SemaphoreType.DMA((6,)),
        ],
        compiler_params=pltpu.CompilerParams(vmem_limit_bytes=BIG),
    )(*big, *small)


def group_sizes():
    seq = lax.axis_size("seq")
    core = 2 if seq % 2 == 0 else 1
    chain = 4 if seq // core % 4 == 0 else 1
    return {"core": core, "batch": lax.axis_size("batch"), "chain": chain, "outer": seq // core // chain}


class Group:
    def __init__(self, name):
        batch, seq = lax.axis_index("batch"), lax.axis_index("seq")
        sizes = group_sizes()
        self.size = sizes[name]
        if name == "batch":
            self.place = batch
            self.device = lambda j: (j, seq)
        else:
            stride = {"core": 1, "chain": sizes["core"], "outer": sizes["core"] * sizes["chain"]}[name]
            self.place = seq // stride % self.size
            self.device = lambda j: (batch, seq + (j - self.place) * stride)

    def other(self, k):
        return (self.place + k) % self.size


class Chain:
    def __init__(self, names, source, scratch, local=None):
        self.names, self.source, self.local = names, source, local
        self.groups = [Group(n) for n in names]
        count = len(names)
        self.outer = Group("outer")
        self.received, self.sums = scratch[:count], scratch[count : 2 * count]
        self.around, self.whole, self.send, self.arrive = scratch[2 * count :]
        rows = self.whole.shape[0]
        self.rows, self.base, base = [], [], 0
        for g in self.groups:
            self.base.append(base)
            rows //= g.size
            base = base + g.place * rows
            self.rows.append(rows)
        self.mine = base
        self.sem = 0
        self.pending = []

    @staticmethod
    def scratch(names, rows, lanes):
        received, sums, copies = [], [], 0
        total, sizes = rows, group_sizes()
        for size in (sizes[n] for n in names):
            rows = rows // size
            received.append(pltpu.VMEM((max(size - 1, 1), rows, lanes), BF16))
            sums.append(pltpu.VMEM((rows, lanes), BF16))
            copies += 2 * (size - 1)
        copies = max(copies + sizes["outer"] - 1, 1)
        return (
            received
            + sums
            + [
                pltpu.VMEM((max(sizes["outer"] - 1, 1), rows, lanes), BF16),
                pltpu.VMEM((total, lanes), BF16),
                pltpu.SemaphoreType.DMA((copies,)),
                pltpu.SemaphoreType.DMA((copies,)),
            ]
        )

    def copy(self, ends):
        at = self.sem
        self.sem += 1

        def form():
            source, target, device = ends()
            return pltpu.make_async_remote_copy(
                src_ref=source,
                dst_ref=target,
                send_sem=self.send.at[at],
                recv_sem=self.arrive.at[at],
                device_id=device,
                device_id_type=MESH,
            )

        form().start()
        self.pending.append(form)

    def scatter(self, k):
        g, rows = self.groups[k], self.rows[k]
        source = self.source if k == 0 else self.sums[k - 1]

        def ends(step):
            other = g.other(step)
            there = pl.ds(pl.multiple_of(other * rows, 16), rows)
            return source.at[there], self.received[k].at[step - 1], g.device(other)

        for step in range(1, g.size):
            self.copy(partial(ends, step))

    def wait(self):
        for form in self.pending:
            form().wait()
        self.pending = []

    def add(self, k):
        self.wait()
        g, rows = self.groups[k], self.rows[k]
        source = self.source if k == 0 else self.sums[k - 1]
        if k == 0 and self.local is not None:
            total = self.local[...].astype(F32)
        else:
            total = source[pl.ds(pl.multiple_of(g.place * rows, 16), rows), :].astype(F32)
        for step in range(1, g.size):
            total = total + self.received[k][step - 1].astype(F32)
        total = total.astype(BF16)
        if k < len(self.groups) - 1 or self.outer.size > 1:
            self.sums[k][...] = total
        if k == len(self.groups) - 1:
            if self.outer.size > 1:
                total = self.exchange(total)
            self.whole[pl.ds(pl.multiple_of(self.mine, 16), rows), :] = total

    def exchange(self, total):
        g = self.outer

        def ends(step):
            return self.sums[-1], self.around.at[step - 1], g.device(g.other(step))

        for step in range(1, g.size):
            self.copy(partial(ends, step))
        self.wait()
        total = total.astype(F32)
        for step in range(1, g.size):
            total = total + self.around[step - 1].astype(F32)
        return total.astype(BF16)

    def gather(self, k):
        g, rows = self.groups[k], self.rows[k]

        def ends(step):
            here = self.whole.at[pl.ds(pl.multiple_of(self.base[k] + g.place * rows, 16), rows)]
            return here, here, g.device(g.other(step))

        for step in range(1, g.size):
            self.copy(partial(ends, step))

    def advance(self, stage):
        count = len(self.groups)
        if 0 < stage <= count:
            self.add(stage - 1)
        else:
            self.wait()
        if stage < count:
            self.scatter(stage)
        elif stage < 2 * count:
            self.gather(2 * count - 1 - stage)


EARLY = (
    (0, 384, ("core", "batch", "chain")),
    (384, 896, ("core", "batch", "chain")),
    (896, 1280, ("core", "chain", "batch")),
)
LATE = (
    (0, 128, ("core", "batch", "chain")),
    (128, 256, ("core", "batch", "chain")),
    (256, 384, ("core", "chain", "batch")),
)


def back_kernel(
    windows,
    sq_hbm,
    skv_hbm,
    dctx_hbm,
    e_hbm,
    g_hbm,
    pack_hbm,
    xs_hbm,
    dres_hbm,
    wq_hbm,
    wk_hbm,
    wv_hbm,
    rows_ref,
    dx_ref,
    early_ref,
    late_ref,
    sq_ref,
    skv_ref,
    dctx_ref,
    e_ref,
    g_ref,
    half_ref,
    xs_ref,
    dres_ref,
    wq_ref,
    wk_ref,
    wv_ref,
    in_sem,
    block_sem,
    dq_ref,
    dkv_ref,
    give_ref,
    take_ref,
    qkv_ref,
    halo_send,
    halo_arrive,
    out_sem,
    *scratch,
):
    step = pl.program_id(0)
    w = (windows - step) % windows
    slots = windows * WIN
    width_s = xs_ref.shape[0]
    batch, seq = lax.axis_index("batch"), lax.axis_index("seq")
    peers = lax.axis_size("seq")
    chains, used = [], 0
    for source, local, cuts in ((pack_hbm, half_ref, EARLY), (qkv_ref, None, LATE)):
        for first, last, names in cuts:
            size = 2 * len(names) + 4
            mine = local.at[:, first:last] if local is not None else None
            chains.append(Chain(names, source.at[:, first:last], scratch[used : used + size], mine))
            used += size
    soon, late = chains[: len(EARLY)], chains[len(EARLY) :]
    first_seq, last_seq = seq == 0, seq == peers - 1

    def halo(side):
        return pltpu.make_async_remote_copy(
            src_ref=give_ref.at[side],
            dst_ref=take_ref.at[1 - side],
            send_sem=halo_send.at[side],
            recv_sem=halo_arrive.at[1 - side],
            device_id=(batch, seq - 1 + 2 * side),
            device_id_type=MESH,
        )

    half_rows = half_ref.shape[0]
    ends = {
        "half": (pack_hbm.at[pl.ds(pl.multiple_of(seq % group_sizes()["core"] * half_rows, 16), half_rows)], half_ref),
        "sq": (sq_hbm, sq_ref),
        "skv": (skv_hbm, skv_ref),
        "dctx": (dctx_hbm, dctx_ref),
        "xs": (xs_hbm, xs_ref),
        "dres": (dres_hbm, dres_ref),
        "wq": (wq_hbm, wq_ref),
        "wk": (wk_hbm, wk_ref),
        "wv": (wv_hbm, wv_ref),
    }
    load = lambda name: pltpu.make_async_copy(*ends[name], in_sem.at[list(ends).index(name)])

    def blocks(number):
        slot, window = number % 2, (windows - number) % windows
        return [
            pltpu.make_async_copy(source.at[window], target.at[slot], block_sem.at[k, slot])
            for k, (source, target) in enumerate(((e_hbm, e_ref), (g_hbm, g_ref)))
        ]

    @pl.when(step == 0)
    def _():
        load("half").start()
        dkv_ref[...] = jnp.zeros_like(dkv_ref)
        take_ref[...] = jnp.zeros_like(take_ref)
        qkv_ref[...] = jnp.zeros_like(qkv_ref)
        barrier = pltpu.get_barrier_semaphore()
        count = 0
        for g in (Group(n) for n in ("core", "batch", "chain", "outer")):
            for k in range(1, g.size):
                pl.semaphore_signal(barrier, inc=1, device_id=g.device(g.other(k)), device_id_type=MESH)
                count += 1

        for move in (1, peers - 1):
            pl.semaphore_signal(
                barrier, inc=1, device_id=(batch, (seq + move) % peers), device_id_type=MESH
            )
        pl.semaphore_wait(barrier, count + 2)

        for c in soon:
            c.advance(0)
        for c in blocks(0):
            c.start()
        for name in ("sq", "skv", "dctx"):
            load(name).start()
        for c in blocks(1):
            c.start()
        for name in ("xs", "dres", "wq", "wk", "wv"):
            load(name).start()
        for name in ("sq", "skv", "dctx", "half"):
            load(name).wait()

    for c in blocks(step):
        c.wait()
    slot = step % 2
    at = pl.multiple_of(w * WIN, WIN)
    left = pl.ds(at, WIN)
    own = pl.ds(pl.multiple_of(at + WIN, WIN), WIN)
    right = pl.ds(pl.multiple_of(at + 2 * WIN, WIN), WIN)
    early_row, late_row = rows_ref[0:1, left], rows_ref[1:2, left]
    early_low, late_low = early_row.astype(BF16), late_row.astype(BF16)

    def one_head(head):
        rows = pl.ds(pl.multiple_of(head * PAD, PAD), PAD)
        query, grad = sq_ref[rows, left], dctx_ref[rows, left]
        stacked = lambda a: jnp.concatenate([a * early_low, a * late_low], axis=0)
        query_fold, grad_fold = stacked(query), stacked(grad)
        beside = lambda k: jnp.concatenate([skv_ref[k, rows, left], skv_ref[k, rows, right]], axis=0)
        keys_fold, values_fold = beside(0), beside(1)
        keys, values = skv_ref[0, rows, own], skv_ref[1, rows, own]
        e_own, e_side = e_ref[slot, head, :WIN, :], e_ref[slot, head, WIN:, :]
        d_own = (e_own.astype(F32) * (tn(values, grad) + g_ref[slot, head, :WIN, :].astype(F32))).astype(BF16)
        d_side = (
            e_side.astype(F32) * (tn(values_fold, grad_fold) + g_ref[slot, head, WIN:, :].astype(F32))
        ).astype(BF16)
        side = nn(keys_fold, d_side)
        d_query = nn(keys, d_own) + early_row * side[:PAD] + late_row * side[PAD:]
        dq_ref[rows, left] = (d_query * HD_S**-0.5).astype(BF16)
        for k, (a, a_fold, b, b_fold, scale) in enumerate(
            ((query, query_fold, d_own, d_side, 1.0 / LOG2E), (grad, grad_fold, e_own, e_side, None))
        ):
            fix = (lambda v: v * scale) if scale else (lambda v: v)
            side = fix(nt(a_fold, b_fold))
            dkv_ref[k, rows, own] += fix(nt(a, b))
            dkv_ref[k, rows, left] += side[:PAD]
            dkv_ref[k, rows, right] += side[PAD:]

    def body(pair, carry):
        one_head(2 * pair)
        one_head(2 * pair + 1)
        return carry

    def send_halo():
        for side, lanes in ((0, slice(0, WIN)), (1, slice(WIN + slots, 2 * WIN + slots))):
            give_ref[side] = dkv_ref[:, :, lanes].astype(BF16)

        @pl.when(jnp.logical_not(first_seq))
        def _():
            halo(0).start()

        @pl.when(jnp.logical_not(last_seq))
        def _():
            halo(1).start()

    def advance(which, stage):
        for c in which:
            c.advance(stage)

    half = PAIRS // 2
    plan = {
        (0, 0): [partial(advance, soon, 1)],
        (1, 1): [send_halo],
        (2, 0): [partial(advance, soon, 2)],
        (3, 0): [partial(advance, soon, 3)],
    }
    for part in range(2):
        lax.fori_loop(part * half, (part + 1) * half, body, 0)
        for k in range(windows):
            for action in plan.get((k, part), []):
                pl.when(step == k)(action)

    @pl.when(step < windows - 2)
    def _():
        for c in blocks(step + 2):
            c.start()

    @pl.when(step == windows - 1)
    def _():
        for name in ("xs", "dres", "wq", "wk", "wv"):
            load(name).wait()

        @pl.when(jnp.logical_not(first_seq))
        def _():
            halo(0).wait_send()
            halo(1).wait_recv()

        @pl.when(jnp.logical_not(last_seq))
        def _():
            halo(1).wait_send()
            halo(0).wait_recv()

        spot = pad_heads()
        plains = []
        for k in range(3):
            if k == 0:
                grad = dq_ref[...]
            else:
                mine = dkv_ref[k - 1, :, WIN : WIN + slots]
                first = mine[:, :WIN] + take_ref[0, k - 1].astype(F32)
                last = mine[:, slots - WIN :] + take_ref[1, k - 1].astype(F32)
                grad = jnp.concatenate([first, mine[:, WIN : slots - WIN], last], axis=1).astype(BF16)
            plain = tn(spot, grad).astype(BF16)
            plains.append(plain)
            qkv_ref[k * BLOCK : k * BLOCK + width_s, :width_s] = nt(xs_ref[...], plain).astype(BF16)
        advance(soon, 4)
        advance(late, 0)
        total = dres_ref[...]
        for w_ref, plain in zip((wq_ref, wk_ref, wv_ref), plains):
            total = total + nn(w_ref[...], plain)
        dx_ref[...] = total.astype(BF16)
        advance(late, 1)
        advance(late, 2)
        advance(soon, 5)
        advance(late, 3)
        advance(soon, 6)

        def put(group, cuts, target, first_sem):
            made = []
            for n, (c, (first, last, _)) in enumerate(zip(group, cuts)):
                made.append(pltpu.make_async_copy(c.whole, target.at[:, first:last], out_sem.at[first_sem + n]))
                made[-1].start()
            return made

        copies = put(soon, EARLY, early_ref, 0)
        advance(late, 4)
        advance(late, 5)
        advance(late, 6)
        copies += put(late, LATE, late_ref, len(EARLY))
        for c in copies:
            c.wait()


def back(sq, skv, dctx, e, g, rows, pack, xs, dres, wq, wk, wv):
    padded, slots = sq.shape
    windows = slots // WIN
    width_s = xs.shape[0]
    packed_rows = pack.shape[0]
    anywhere = pl.BlockSpec(memory_space=pl.ANY)
    held = lambda a: pltpu.VMEM(a.shape, a.dtype)
    scratch = [held(sq), held(skv), held(dctx)]
    scratch += [pltpu.VMEM((2,) + a.shape[1:], a.dtype) for a in (e, g)]
    scratch += [pltpu.VMEM((packed_rows // group_sizes()["core"], pack.shape[1]), BF16)]
    scratch += [held(a) for a in (xs, dres, wq, wk, wv)]
    scratch += [
        pltpu.SemaphoreType.DMA((9,)),
        pltpu.SemaphoreType.DMA((2, 2)),
        pltpu.VMEM((padded, slots), BF16),
        pltpu.VMEM((2, padded, slots + 2 * WIN), F32),
        pltpu.VMEM((2, 2, padded, WIN), BF16),
        pltpu.VMEM((2, 2, padded, WIN), BF16),
        pltpu.VMEM((packed_rows, QKV_LANES), BF16),
        pltpu.SemaphoreType.DMA((2,)),
        pltpu.SemaphoreType.DMA((2,)),
        pltpu.SemaphoreType.DMA((len(EARLY) + len(LATE),)),
    ]
    for first, last, names in EARLY + LATE:
        scratch += Chain.scratch(names, packed_rows, last - first)
    return pl.pallas_call(
        partial(back_kernel, windows),
        grid=(windows,),
        out_shape=[
            jax.ShapeDtypeStruct((width_s, slots), BF16),
            jax.ShapeDtypeStruct(pack.shape, BF16),
            jax.ShapeDtypeStruct((packed_rows, QKV_LANES), BF16),
        ],
        in_specs=[anywhere] * 11 + [VMEM],
        out_specs=[pl.BlockSpec((width_s, slots), lambda i: (0, 0)), anywhere, anywhere],
        scratch_shapes=scratch,
        compiler_params=pltpu.CompilerParams(
            vmem_limit_bytes=BIG,
            dimension_semantics=("arbitrary",),
            collective_id=0,
            has_side_effects=True,
        ),
    )(sq, skv, dctx, e, g, pack, xs, dres, wq, wk, wv, rows)


def unpack_kernel(
    every,
    width_t,
    early_ref,
    late_ref,
    dx_in_ref,
    dx_ref,
    loss_ref,
    gq_ref,
    gk_ref,
    gv_ref,
    gwo_ref,
    ginner_ref,
    gouter_ref,
    ghid_ref,
    rows_ref,
    binner_ref,
):
    width_s = gq_ref.shape[0]
    units = binner_ref.shape[1]
    scale = 1.0 / every
    full = lambda v: v.astype(F32) * scale
    dx_ref[...] = dx_in_ref[...]
    for k, ref in enumerate((gq_ref, gk_ref, gv_ref)):
        ref[...] = full(late_ref[k * BLOCK : k * BLOCK + width_s, :width_s])
    gouter_ref[...] = full(early_ref[:width_s, :units])
    ginner_ref[...] = full(early_ref[BLOCK : BLOCK + width_s, :units])
    third = slice(2 * BLOCK, 2 * BLOCK + width_s)
    ghid_ref[...] = full(early_ref[third, :width_t])
    gwo_ref[...] = full(early_ref[third, width_t : width_t + width_s])
    binner_ref[...] = full(early_ref[BLOCK + width_s : BLOCK + width_s + 8, :units])[0:1]
    last = units // 128 * 128
    lane = lax.broadcasted_iota(jnp.int32, (width_s, 128), 1)
    columns = jnp.where(
        lane < 4,
        full(early_ref[third, SUMS_AT : SUMS_AT + 128]),
        full(early_ref[:width_s, last : last + 128]),
    )
    rows_ref[...] = jnp.transpose(columns)
    part = early_ref[2 * BLOCK + width_s : 2 * BLOCK + width_s + 8, :128].astype(F32)
    total = jnp.sum(jnp.sum(part, axis=0, keepdims=True), axis=1, keepdims=True)
    loss_ref[...] = total * (scale / width_t)


def unpack(every, width_t, units, early, late, dx):
    width_s = dx.shape[0]
    sds = lambda *shape: jax.ShapeDtypeStruct(shape, F32)
    shapes = [
        jax.ShapeDtypeStruct(dx.shape, BF16),
        sds(1, 1),
        sds(width_s, width_s),
        sds(width_s, width_s),
        sds(width_s, width_s),
        sds(width_s, width_s),
        sds(width_s, units),
        sds(width_s, units),
        sds(width_s, width_t),
        sds(128, width_s),
        sds(1, units),
    ]
    return pl.pallas_call(
        partial(unpack_kernel, every, width_t),
        out_shape=shapes,
        in_specs=[VMEM] * 3,
        out_specs=[VMEM] * len(shapes),
        compiler_params=pltpu.CompilerParams(vmem_limit_bytes=BIG),
    )(early, late, dx)


def local(
    inputs,
    teacher_input,
    filled_slot_mask,
    seg_lengths,
    query_weight,
    key_weight,
    value_weight,
    w_output,
    gain_one,
    shift_one,
    w_inner,
    b_inner,
    w_outer,
    b_outer,
    gain_two,
    shift_two,
    w_hidden,
    teacher_query_weight,
    teacher_key_weight,
    teacher_value_weight,
    teacher_output,
    teacher_gain_one,
    teacher_shift_one,
    teacher_inner,
    teacher_outer,
    teacher_gain_two,
    teacher_shift_two,
):
    xs = jnp.transpose(inputs[0])
    xt = teacher_input[0]
    slots, width_t = xt.shape
    width_s = xs.shape[0]
    stats, loss_rows, rows, tctx, sctx, sq, skv, e, g = attend(
        filled_slot_mask,
        seg_lengths,
        xt,
        xs,
        teacher_query_weight,
        teacher_key_weight,
        teacher_value_weight,
        query_weight,
        key_weight,
        value_weight,
    )
    devices = lax.axis_size("seq") * lax.axis_size("batch")
    sizes = group_sizes()
    unit = 16 * sizes["core"] * sizes["batch"] * sizes["chain"]
    packed_rows = -(-3 * BLOCK // unit) * unit
    out, dctx, dres, pack = dense(
        packed_rows,
        (
            xt,
            tctx,
            teacher_output,
            xs,
            sctx,
            teacher_inner,
            teacher_outer,
            w_output,
            w_inner,
            jnp.transpose(w_outer),
            w_hidden,
        ),
        (stats, rows, loss_rows)
        + (
            teacher_gain_one,
            teacher_shift_one,
            teacher_gain_two,
            teacher_shift_two,
            gain_one,
            shift_one,
            b_outer,
            gain_two,
            shift_two,
            b_inner,
        ),
    )
    dx, early, late = back(sq, skv, dctx, e, g, rows, pack, xs, dres, query_weight, key_weight, value_weight)
    dx, loss, gq, gk, gv, gwo, ginner, gouter, ghid, vectors, binner = unpack(
        slots * devices, width_t, w_inner.shape[1], early, late, dx
    )
    return (
        jnp.transpose(out)[None],
        jnp.transpose(dx)[None],
        loss[0, 0],
        gq,
        gk,
        gv,
        gwo,
        vectors[0],
        vectors[1],
        ginner,
        binner[0],
        jnp.transpose(gouter),
        vectors[w_inner.shape[1] % 128],
        vectors[2],
        vectors[3],
        ghid,
    )


def solution(mesh):
    row_split = P("batch", "seq", None)
    return jax.shard_map(
        local,
        mesh=mesh,
        in_specs=(row_split, row_split, P("batch", None), P("batch", None)) + (P(),) * 23,
        out_specs=(row_split, row_split) + (P(),) * 14,
        check_vma=False,
    )
```

```python
from functools import partial

import jax
import jax.numpy as jnp
from jax import lax
from jax.experimental import pallas as pl
from jax.experimental.pallas import tpu as pltpu
from jax.sharding import PartitionSpec as P

HEADS = 12
HD_S = 26
HD_T = 64
WIN = 256
PAD = 32
SLOT_ONE = 26
PAIRS = HEADS // 2
CHUNK = 64
TAIL = 16
SLOTS = 4
BLOCK = 320
STRIP = 64
STRIP_OUTER = 384
STRIP_BIAS = 768
QKV_LANES = 384
MESH = pl.DeviceIdType.MESH
EPSILON = 1e-05
NEGATIVE = -1e30
LOG2E = 1.4426950408889634
F32 = jnp.float32
BF16 = jnp.bfloat16
VMEM = pl.BlockSpec(memory_space=pltpu.VMEM)
BIG = 60 << 20


def mm(left, right, dims):
    return lax.dot_general(left, right, ((dims[:1], dims[1:]), ((), ())), preferred_element_type=F32)


def nn(left, right):
    return mm(left, right, (1, 0))


def tn(left, right):
    return mm(left, right, (0, 0))


def nt(left, right):
    return mm(left, right, (1, 1))


def tt(left, right):
    return mm(left, right, (0, 1))


def pad_heads():
    row = lax.broadcasted_iota(jnp.int32, (HEADS * PAD, HEADS * HD_S), 0)
    col = lax.broadcasted_iota(jnp.int32, (HEADS * PAD, HEADS * HD_S), 1)
    spot = jnp.zeros((HEADS * PAD, HEADS * HD_S), F32)
    for head in range(HEADS):
        here = (row - head * PAD == col - head * HD_S) & (col >= head * HD_S) & (col < (head + 1) * HD_S)
        spot = jnp.where(here, 1.0, spot)
    return spot.astype(BF16)


def window_rows(mask_ref, lengths_ref, seq_index, windows, row_windows):
    lengths = lengths_ref[...].astype(F32)
    order = lax.broadcasted_iota(jnp.int32, lengths.shape, 1)
    lane = lax.broadcasted_iota(jnp.int32, (1, WIN), 1).astype(F32)
    out = []
    for j in range(windows + 2):
        number = seq_index * windows + (j - 1)
        inside = (number >= 0) & (number < row_windows)
        safe = jnp.clip(number, 0, row_windows - 1)
        start = jnp.sum(jnp.where(order < safe, lengths, 0.0), axis=1, keepdims=True)
        offset = start - (safe * WIN).astype(F32)
        late = (lane >= offset).astype(F32)
        filled = mask_ref[:, pl.ds(pl.multiple_of(safe * WIN, WIN), WIN)]
        filled = jnp.where(inside, filled.astype(F32), 0.0)
        out.append((late, filled))
    return out


def stack_rows(*rows):
    n = rows[0].shape[1]
    index = lax.broadcasted_iota(jnp.int32, (8, n), 0)
    block = jnp.zeros((8, n), F32)
    for k, row in enumerate(rows):
        block = jnp.where(index == k, row, block)
    return block.astype(BF16)


def attend_kernel(
    windows,
    row_windows,
    mask_ref,
    lengths_ref,
    xt_hbm,
    xs_ref,
    wtq_hbm,
    wtk_hbm,
    wtv_hbm,
    wq_ref,
    wk_ref,
    wv_ref,
    stats_ref,
    loss_ref,
    rows_ref,
    tctx_hbm,
    sctx_hbm,
    sq_hbm,
    skv_hbm,
    saved_e_hbm,
    saved_g_hbm,
    x_ref,
    xs_side_ref,
    wt_ref,
    bias_ref,
    wst_ref,
    tq_ref,
    tk_ref,
    tv_ref,
    sq_ref,
    skv_ref,
    tctx_ref,
    sctx_ref,
    e_ref,
    g_ref,
    work_ref,
    low_ref,
    in_sem,
    halo_send,
    halo_arrive,
    kv_sem,
    out_sem,
):
    slots = windows * WIN
    batch, seq = lax.axis_index("batch"), lax.axis_index("seq")
    peers = lax.axis_size("seq")
    has_left, has_right = seq > 0, seq < peers - 1
    width_t = x_ref.shape[1]
    extended = slots + 2 * WIN

    barrier = pltpu.get_barrier_semaphore()
    for move in (1, peers - 1):
        pl.semaphore_signal(barrier, inc=1, device_id=(batch, (seq + move) % peers), device_id_type=MESH)
    loads = [pltpu.make_async_copy(xt_hbm, x_ref.at[pl.ds(WIN, slots)], in_sem.at[0])]
    for k, w_hbm in enumerate((wtq_hbm, wtk_hbm, wtv_hbm)):
        loads.append(pltpu.make_async_copy(w_hbm, wt_ref.at[k], in_sem.at[1 + k]))
    for c in loads:
        c.start()
    pl.semaphore_wait(barrier, 2)

    def halo(side):
        device = (batch, seq - 1 + 2 * side)
        first = pl.multiple_of(side * (slots - WIN), WIN)
        return [
            pltpu.make_async_remote_copy(
                src_ref=xt_hbm.at[pl.ds(first, WIN)],
                dst_ref=x_ref.at[pl.ds(pl.multiple_of((1 - side) * (WIN + slots), WIN), WIN)],
                send_sem=halo_send.at[0, side],
                recv_sem=halo_arrive.at[0, 1 - side],
                device_id=device,
                device_id_type=MESH,
            ),
            pltpu.make_async_remote_copy(
                src_ref=xs_ref.at[:, pl.ds(first, WIN)],
                dst_ref=xs_side_ref.at[1 - side],
                send_sem=halo_send.at[1, side],
                recv_sem=halo_arrive.at[1, 1 - side],
                device_id=device,
                device_id_type=MESH,
            ),
        ]

    for side, present in ((0, has_left), (1, has_right)):

        @pl.when(present)
        def _():
            for c in halo(side):
                c.start()

        @pl.when(jnp.logical_not(present))
        def _():
            x_ref[side * (WIN + slots) : side * (WIN + slots) + WIN, :] = jnp.zeros((WIN, width_t), BF16)
            xs_side_ref[side] = jnp.zeros(xs_side_ref.shape[1:], BF16)

    info = window_rows(mask_ref, lengths_ref, seq, windows, row_windows)
    eye = lax.broadcasted_iota(jnp.int32, (WIN, WIN), 0) == lax.broadcasted_iota(jnp.int32, (WIN, WIN), 1)
    rows_ref[...] = jnp.zeros_like(rows_ref)
    for w in range(windows):
        late, filled = info[w + 1]
        late_l, filled_l = info[w]
        late_r, filled_r = info[w + 2]
        early = 1.0 - late
        here = slice(w * WIN, (w + 1) * WIN)
        rows_ref[0:1, here] = early
        rows_ref[1:2, here] = late
        rows_ref[2:3, here] = filled
        query = stack_rows(early, late)
        own = tn(stack_rows(NEGATIVE * (1.0 - early * filled), NEGATIVE * (1.0 - late * filled)), query)
        bias_ref[w, :WIN, :] = jnp.where(eye, 0.0, own)
        bias_ref[w, WIN:, :] = tn(
            stack_rows(
                NEGATIVE * (1.0 - late_l * filled_l), NEGATIVE * (1.0 - (1.0 - late_r) * filled_r)
            ),
            query,
        )
    loss_ref[...] = jnp.zeros_like(loss_ref)
    stats_ref[...] = jnp.zeros_like(stats_ref)
    spot = pad_heads()
    padded = HEADS * PAD
    row = lax.broadcasted_iota(jnp.int32, (padded, 1), 0) % PAD
    ones = (row >= SLOT_ONE) & (row < SLOT_ONE + 3)

    xs = xs_ref[...]
    for k, w_ref in enumerate((wq_ref, wk_ref, wv_ref)):
        wst_ref[k] = nt(spot, w_ref[...]).astype(BF16)
        made = nn(wst_ref[k], xs)
        if k == 0:
            sq_ref[...] = (made * (LOG2E * HD_S**-0.5)).astype(BF16)
        else:
            if k == 2:
                made = jnp.where(ones, 1.0, made)
            skv_ref[k - 1, :, WIN : WIN + slots] = made.astype(BF16)
    tail = (lax.broadcasted_iota(jnp.int32, (TAIL, extended), 0) == 0).astype(BF16)
    for head in range(HEADS):
        tv_ref[head * (HD_T + TAIL) + HD_T : (head + 1) * (HD_T + TAIL), :] = tail

    def put_values(made, first_head, lanes):
        for j in range(made.shape[0] // HD_T):
            at = pl.multiple_of((first_head + j) * (HD_T + TAIL), TAIL)
            tv_ref[pl.ds(at, HD_T), lanes] = made[j * HD_T : (j + 1) * HD_T]

    part = width_t // 2
    loads[0].wait()
    for k in range(3):
        loads[1 + k].wait()

        def project(half, carry, k=k):
            rows = pl.ds(pl.multiple_of(half * part, 128), part)
            made = tt(wt_ref[k, :, rows], x_ref[WIN : WIN + slots, :])
            if k == 0:
                tq_ref[rows, :] = (made * (LOG2E * HD_T**-0.5)).astype(BF16)
            elif k == 1:
                tk_ref[rows, WIN : WIN + slots] = made.astype(BF16)
            else:
                put_values(made.astype(BF16), half * (HEADS // 2), slice(WIN, WIN + slots))
            return carry

        lax.fori_loop(0, 2, project, 0)

    def project_side(side, carry):
        @pl.when(jnp.where(side == 0, has_left, has_right))
        def _():
            for sent, landed in zip(halo(side), halo(1 - side)):
                sent.wait_send()
                landed.wait_recv()

        lanes = pl.ds(pl.multiple_of(side * (WIN + slots), WIN), WIN)
        for k in (1, 2):
            made = tt(wt_ref[k], x_ref[lanes, :]).astype(BF16)
            if k == 1:
                tk_ref[:, lanes] = made
            else:
                put_values(made, 0, lanes)
            made = nn(wst_ref[k], xs_side_ref[side])
            if k == 2:
                made = jnp.where(ones, 1.0, made)
            skv_ref[k - 1, :, lanes] = made.astype(BF16)
        return carry

    lax.fori_loop(0, 2, project_side, 0)
    finals = [
        pltpu.make_async_copy(sq_ref, sq_hbm, kv_sem.at[0]),
        pltpu.make_async_copy(skv_ref, skv_hbm, kv_sem.at[1]),
    ]
    for c in finals:
        c.start()

    def stores(pair, which):
        slot = pair % 2
        t_rows = pl.ds(pl.multiple_of(pair * 2 * HD_T, 2 * HD_T), 2 * HD_T)
        s_rows = pl.ds(pl.multiple_of(pair * 2 * PAD, 2 * PAD), 2 * PAD)
        heads = pl.ds(pair * 2, 2)
        ends = (
            (e_ref.at[slot], saved_e_hbm.at[:, heads]),
            (g_ref.at[slot], saved_g_hbm.at[:, heads]),
            (tctx_ref.at[t_rows], tctx_hbm.at[t_rows]),
            (sctx_ref.at[s_rows], sctx_hbm.at[s_rows]),
        )
        return [pltpu.make_async_copy(*ends[k], out_sem.at[k, pair]) for k in which]

    def one_pair(pair, carry):
        @pl.when(pair >= 2)
        def _():
            for c in stores(pair - 2, (0, 1)):
                c.wait()

        attend_pair(pair)
        for c in stores(pair, range(4)):
            c.start()
        return carry

    def attend_pair(pair):
        e_out, g_out = e_ref.at[pair % 2], g_ref.at[pair % 2]
        def rows_of(w):
            left = slice(w * WIN, (w + 1) * WIN)
            own = slice((w + 1) * WIN, (w + 2) * WIN)
            right = slice((w + 2) * WIN, (w + 3) * WIN)
            return left, own, right, rows_ref[0:1, left], rows_ref[1:2, left], rows_ref[2:3, left]

        def first_pass(w, q_ref, k_ref, rows, work_ref):
            left, own, right, early, late, _ = rows_of(w)
            query = q_ref[rows, left]
            query_fold = jnp.concatenate([query * early.astype(BF16), query * late.astype(BF16)], axis=0)
            keys = k_ref[rows, own]
            keys_fold = jnp.concatenate([k_ref[rows, left], k_ref[rows, right]], axis=0)
            top = None
            for part, (a, b) in enumerate(((keys, query), (keys_fold, query_fold))):
                raw = tn(a, b)
                for c in range(0, WIN, CHUNK):
                    block = raw[c : c + CHUNK] + bias_ref[w, part * WIN + c : part * WIN + c + CHUNK, :]
                    work_ref[part * WIN + c : part * WIN + c + CHUNK, :] = block
                    for r in range(0, CHUNK, 8):
                        piece = block[r : r + 8]
                        top = piece if top is None else jnp.maximum(top, piece)
            return jnp.max(top, axis=0, keepdims=True)

        def second_pass(work_ref, top, low_ref):
            for c in range(0, 2 * WIN, CHUNK):
                e = jnp.exp2(work_ref[c : c + CHUNK, :] - top)
                work_ref[c : c + CHUNK, :] = e
                low_ref[c : c + CHUNK, :] = e.astype(BF16)

        def mix(w, v_ref, rows, low_ref, head_width):
            left, own, right, early, late, _ = rows_of(w)
            values = v_ref[rows, own]
            values_fold = jnp.concatenate([v_ref[rows, left], v_ref[rows, right]], axis=0)
            mixed = nn(values, low_ref[:WIN, :])
            side = nn(values_fold, low_ref[WIN:, :])
            n = values.shape[0]
            mixed = mixed + early * side[:n] + late * side[n:]
            inverse = 1.0 / mixed[head_width : head_width + 1]
            return mixed[: -TAIL if head_width == HD_T else n] * inverse, inverse

        units = [(w, h) for w in range(windows) for h in range(2)]
        state = {}

        def refs(u):
            w, h = units[u]
            head = 2 * pair + h
            t_rows = pl.ds(pl.multiple_of(head * HD_T, HD_T), HD_T)
            s_rows = pl.ds(pl.multiple_of(head * PAD, PAD), PAD)
            v_rows = pl.ds(pl.multiple_of(head * (HD_T + TAIL), TAIL), HD_T + TAIL)
            slot = u % SLOTS
            return w, h, t_rows, s_rows, v_rows, work_ref.at[2 * slot], work_ref.at[2 * slot + 1], low_ref.at[slot]

        def score_stage(u):
            w, h, t_rows, s_rows, _, work_t, work_s, _ = refs(u)
            state[u] = [
                first_pass(w, tq_ref, tk_ref, t_rows, work_t),
                first_pass(w, sq_ref, skv_ref.at[0], s_rows, work_s),
            ]

        def power_stage(u):
            w, h, _, _, _, work_t, work_s, low_t = refs(u)
            second_pass(work_t, state[u][0], low_t)
            second_pass(work_s, state[u][1], e_out.at[w, h])

        def mix_stage(u):
            w, h, t_rows, s_rows, v_rows, _, _, low_t = refs(u)
            left = rows_of(w)[0]
            t_mixed, t_inv = mix(w, tv_ref, v_rows, low_t, HD_T)
            s_mixed, s_inv = mix(w, skv_ref.at[1], s_rows, e_out.at[w, h], SLOT_ONE)
            tctx_ref[t_rows, left] = t_mixed.astype(BF16)
            sctx_ref[s_rows, left] = s_mixed
            state[u] = [t_inv, s_inv]

        def gap_stage(u):
            w, h, _, _, _, work_t, work_s, _ = refs(u)
            left, _, _, _, _, filled = rows_of(w)
            t_inv, s_inv = state.pop(u)
            width = 2.0 * HEADS * HD_T
            scale_s = (width * filled) * s_inv * s_inv
            scale_t = (width * filled) * s_inv * t_inv
            square = jnp.zeros((8, WIN), F32)
            cross = jnp.zeros((8, WIN), F32)
            for c in range(0, 2 * WIN, CHUNK):
                s = work_s[c : c + CHUNK, :]
                gap = s * scale_s - work_t[c : c + CHUNK, :] * scale_t
                g_out[w, h, c : c + CHUNK, :] = gap.astype(BF16)
                for r in range(0, CHUNK, 8):
                    piece = gap[r : r + 8]
                    square += piece * piece
                    cross += piece * s[r : r + 8]
            square = jnp.sum(square, axis=0, keepdims=True)
            cross = jnp.sum(cross, axis=0, keepdims=True)
            back = 1.0 / (s_inv * width)
            stats_ref[pair, h : h + 1, left] = s_inv
            stats_ref[pair, 2 + h : 3 + h, left] = cross
            loss_ref[0:1, left] += square * back * back

        last = len(units)
        for u in range(last + 2):
            if u < last:
                score_stage(u)
            if 0 <= u - 1 < last:
                power_stage(u - 1)
            if 0 <= u - 2 < last:
                mix_stage(u - 2)
                gap_stage(u - 2)


    lax.fori_loop(0, PAIRS, one_pair, 0)
    for pair in range(PAIRS):
        for c in stores(pair, range(0 if pair >= PAIRS - 2 else 2, 4)):
            c.wait()
    for c in finals:
        c.wait()


def attend(mask, lengths, xt, xs, wtq, wtk, wtv, wq, wk, wv):
    slots, width_t = xt.shape
    width_s = xs.shape[0]
    windows = slots // WIN
    row_windows = mask.shape[1] // WIN
    padded = HEADS * PAD
    extended = slots + 2 * WIN
    sds = jax.ShapeDtypeStruct
    anywhere = pl.BlockSpec(memory_space=pl.ANY)
    saved = (windows, HEADS, 2 * WIN, WIN)
    return pl.pallas_call(
        partial(attend_kernel, windows, row_windows),
        out_shape=(
            sds((PAIRS, 8, slots), F32),
            sds((8, slots), F32),
            sds((8, slots), F32),
            sds((width_t, slots), BF16),
            sds((padded, slots), F32),
            sds((padded, slots), BF16),
            sds((2, padded, extended), BF16),
            sds(saved, BF16),
            sds(saved, BF16),
        ),
        in_specs=[VMEM, VMEM, anywhere, VMEM] + [anywhere] * 3 + [VMEM] * 3,
        out_specs=[VMEM] * 3 + [anywhere] * 6,
        scratch_shapes=[
            pltpu.VMEM((extended, width_t), BF16),
            pltpu.VMEM((2, width_s, WIN), BF16),
            pltpu.VMEM((3, width_t, width_t), BF16),
            pltpu.VMEM((windows, 2 * WIN, WIN), F32),
            pltpu.VMEM((3, padded, width_s), BF16),
            pltpu.VMEM((width_t, slots), BF16),
            pltpu.VMEM((width_t, extended), BF16),
            pltpu.VMEM((HEADS * (HD_T + TAIL), extended), BF16),
            pltpu.VMEM((padded, slots), BF16),
            pltpu.VMEM((2, padded, extended), BF16),
            pltpu.VMEM((width_t, slots), BF16),
            pltpu.VMEM((padded, slots), F32),
            pltpu.VMEM((2, windows, 2, 2 * WIN, WIN), BF16),
            pltpu.VMEM((2, windows, 2, 2 * WIN, WIN), BF16),
            pltpu.VMEM((2 * SLOTS, 2 * WIN, WIN), F32),
            pltpu.VMEM((SLOTS, 2 * WIN, WIN), BF16),
            pltpu.SemaphoreType.DMA((4,)),
            pltpu.SemaphoreType.DMA((2, 2)),
            pltpu.SemaphoreType.DMA((2, 2)),
            pltpu.SemaphoreType.DMA((2,)),
            pltpu.SemaphoreType.DMA((4, PAIRS)),
        ],
        compiler_params=pltpu.CompilerParams(
            vmem_limit_bytes=BIG, collective_id=1, has_side_effects=True
        ),
    )(mask, lengths, xt, xs, wtq, wtk, wtv, wq, wk, wv)


def normalize(values, gain, shift):
    n = values.shape[0]
    center = values - jnp.sum(values, axis=0, keepdims=True) * (1.0 / n)
    rscale = lax.rsqrt(jnp.sum(center * center, axis=0, keepdims=True) * (1.0 / n) + EPSILON)
    unit = center * rscale
    return unit * gain + shift, unit, rscale


def normalize_back(grad, unit, rscale, gain):
    n = grad.shape[0]
    scaled = grad * gain
    first = jnp.sum(scaled, axis=0, keepdims=True) * (1.0 / n)
    second = jnp.sum(scaled * unit, axis=0, keepdims=True) * (1.0 / n)
    return rscale * (scaled - first - unit * second)


def fold_lanes(values):
    total = values[:, :128]
    for at in range(128, values.shape[1], 128):
        total = total + values[:, at : at + 128]
    return total


ROOT_HALF = 0.7071067811865476
ROOT_PI = 0.3989422804014327


DENSE_IN = ("xt", "tctx", "two", "xs", "sctx", "tin", "tout", "wo", "w1", "w2", "wh")


def dense_kernel(
    xt_hbm,
    tctx_hbm,
    two_hbm,
    xs_hbm,
    sctx_hbm,
    tin_hbm,
    tout_hbm,
    wo_hbm,
    w1_hbm,
    w2_hbm,
    wh_hbm,
    stats_ref,
    rows_ref,
    loss_ref,
    t_gain_one_ref,
    t_shift_one_ref,
    t_gain_two_ref,
    t_shift_two_ref,
    gain_one_ref,
    shift_one_ref,
    b_outer_ref,
    gain_two_ref,
    shift_two_ref,
    b_inner_ref,
    out_hbm,
    dctx_hbm,
    dres_hbm,
    pack_hbm,
    xt_ref,
    tctx_ref,
    two_ref,
    xs_ref,
    sctx_ref,
    tin_ref,
    tout_ref,
    wo_ref,
    w1_ref,
    w2_ref,
    wh_ref,
    out_ref,
    dctx_ref,
    dres_ref,
    pack_ref,
    act_ref,
    slope_ref,
    t_low_ref,
    t_sum_ref,
    in_sem,
    out_sem,
):
    sources = (
        xt_hbm, tctx_hbm, two_hbm, xs_hbm, sctx_hbm, tin_hbm, tout_hbm, wo_hbm, w1_hbm, w2_hbm, wh_hbm
    )
    targets = (xt_ref, tctx_ref, two_ref, xs_ref, sctx_ref, tin_ref, tout_ref, wo_ref, w1_ref, w2_ref, wh_ref)
    loads = {
        name: pltpu.make_async_copy(source, target, in_sem.at[k])
        for k, (name, source, target) in enumerate(zip(DENSE_IN, sources, targets))
    }
    for c in loads.values():
        c.start()
    width_s, units_s = w1_ref.shape
    width_t, units_t = tin_ref.shape
    slots = xt_ref.shape[0]
    low = lambda v: v.astype(BF16)
    stores = []

    def store(source, target):
        stores.append(pltpu.make_async_copy(source, target, out_sem.at[len(stores)]))
        stores[-1].start()

    def columns(*refs):
        n = refs[0].shape[0]
        index = lax.broadcasted_iota(jnp.int32, (8, n), 0)
        block = jnp.zeros((8, n), F32)
        for k, ref in enumerate(refs):
            block = jnp.where(index == k, ref[...].reshape(1, n), block)
        turned = jnp.transpose(block)
        return [turned[:, k : k + 1] for k in range(len(refs))]

    t_gain_one, t_shift_one, t_gain_two, t_shift_two = columns(
        t_gain_one_ref, t_shift_one_ref, t_gain_two_ref, t_shift_two_ref
    )
    gain_one, shift_one, b_outer, gain_two, shift_two = columns(
        gain_one_ref, shift_one_ref, b_outer_ref, gain_two_ref, shift_two_ref
    )
    (b_inner,) = columns(b_inner_ref)
    spot = pad_heads()
    pack_ref[...] = jnp.zeros_like(pack_ref)
    act_ref[units_s:, :] = jnp.ones((act_ref.shape[0] - units_s, slots), BF16)
    for name in ("xt", "tctx", "two"):
        loads[name].wait()
    start = jnp.transpose(xt_ref[...]).astype(F32) + tn(two_ref[...], tctx_ref[...])
    t_normed = normalize(start, t_gain_one, t_shift_one)[0]
    t_low_ref[...] = low(t_normed)
    t_sum_ref[...] = t_normed
    for name in ("xs", "sctx", "tin", "tout"):
        loads[name].wait()

    def feed_forward(c, carry):
        units = pl.ds(pl.multiple_of(c * width_t, width_t), width_t)
        pre = tn(tin_ref[:, units], t_low_ref[...])
        active = low(0.5 * pre * (1.0 + lax.erf(pre * ROOT_HALF)))
        t_sum_ref[...] += tn(tout_ref[units, :], active)
        return carry

    lax.fori_loop(0, units_t // width_t, feed_forward, 0)
    target = normalize(t_sum_ref[...], t_gain_two, t_shift_two)[0]
    for name in ("wo", "w1", "w2", "wh"):
        loads[name].wait()
    wop = low(nn(spot, wo_ref[...]))
    context = sctx_ref[...]
    context_low = low(context)
    normed, unit_one, rscale_one = normalize(
        xs_ref[...].astype(F32) + tn(wop, context_low), gain_one, shift_one
    )
    normed_low = low(normed)
    pre = tn(w1_ref[...], normed_low) + b_inner
    half = 0.5 * (1.0 + lax.erf(pre * ROOT_HALF))
    slope_ref[...] = half + pre * (ROOT_PI * jnp.exp(-0.5 * pre * pre))
    act_ref[:units_s, :] = low(pre * half)
    student, unit_two, rscale_two = normalize(
        normed + nn(w2_ref[...], act_ref[:units_s, :]) + b_outer, gain_two, shift_two
    )
    student_low = low(student)
    out_ref[...] = student_low
    store(out_ref, out_hbm)
    gap = tn(wh_ref[...], student_low) - target
    filled = rows_ref[2:3, :]
    masked = filled * gap
    d_proj = low(2.0 * masked)
    third = slice(2 * BLOCK, 2 * BLOCK + width_s)
    pack_ref[third, :width_t] = low(nt(student_low, d_proj))
    d_student = nn(wh_ref[...], d_proj)
    d_two = normalize_back(d_student, unit_two, rscale_two, gain_two)
    d_outer = low(d_two)
    main = units_s // 128 * 128
    spare = units_s - main
    strip = 3 * BLOCK
    pack_ref[:width_s, :main] = low(nt(d_outer, act_ref[:main, :]))
    pack_ref[strip : strip + STRIP, STRIP_OUTER : STRIP_OUTER + width_s] = low(
        nt(act_ref[main : main + STRIP, :], d_outer)
    )
    store(pack_ref.at[:BLOCK], pack_hbm.at[:BLOCK])
    d_inner = low(tn(w2_ref[...], d_outer) * slope_ref[...])
    ones = jnp.ones((8, slots), BF16)
    pack_ref[BLOCK : BLOCK + width_s, :main] = low(nt(normed_low, d_inner[:main]))
    pack_ref[BLOCK + width_s : BLOCK + width_s + 8, :main] = low(nt(ones, d_inner[:main]))
    pack_ref[strip : strip + spare, :width_s] = low(nt(d_inner[main:], normed_low))
    pack_ref[strip : strip + spare, STRIP_BIAS : STRIP_BIAS + 8] = low(nt(d_inner[main:], ones))
    store(pack_ref.at[BLOCK : 2 * BLOCK], pack_hbm.at[BLOCK : 2 * BLOCK])
    d_normed = nn(w1_ref[...], d_inner) + d_two
    d_one = normalize_back(d_normed, unit_one, rscale_one, gain_one)
    dres_ref[...] = d_one
    store(dres_ref, dres_hbm)
    d_att = low(d_one)
    gwo = low(nt(context_low, d_att))
    pack_ref[third, width_t : width_t + width_s] = low(tn(spot, gwo))
    d_context = nn(wop, d_att)
    row = lax.broadcasted_iota(jnp.int32, (PAD, slots), 0)
    for head in range(HEADS):
        pair, h = head // 2, head % 2
        inverse = stats_ref[pair, h : h + 1, :]
        cross = stats_ref[pair, 2 + h : 3 + h, :]
        rows = slice(head * PAD, (head + 1) * PAD)
        part = low(d_context[rows] * inverse).astype(F32)
        delta = -jnp.sum(part * context[rows], axis=0, keepdims=True) - inverse * cross
        high = low(delta).astype(F32)
        rest = delta - high
        middle = low(rest).astype(F32)
        part = jnp.where(row == SLOT_ONE, high, part)
        part = jnp.where(row == SLOT_ONE + 1, middle, part)
        part = jnp.where(row == SLOT_ONE + 2, rest - middle, part)
        dctx_ref[rows, :] = low(part)
    store(dctx_ref, dctx_hbm)
    lane = lax.broadcasted_iota(jnp.int32, (width_s, 128), 1)
    sums = jnp.zeros((width_s, 128), F32)
    for k, values in enumerate((d_normed * unit_one, d_normed, d_student * unit_two, d_student)):
        sums = jnp.where(lane == k, jnp.sum(fold_lanes(values), axis=1, keepdims=True), sums)
    pack_ref[strip + spare : strip + spare + 8, :width_s] = low(jnp.transpose(sums)[:8])
    square = jnp.sum(fold_lanes(masked * gap).reshape(-1, 8, 128), axis=0)
    row = lax.broadcasted_iota(jnp.int32, (8, 128), 0)
    for c in range(slots // 128):
        square += jnp.where(row == c % 8, width_t * loss_ref[0:1, c * 128 : (c + 1) * 128], 0.0)
    pack_ref[2 * BLOCK + width_s : 2 * BLOCK + width_s + 8, :128] = low(square)
    store(pack_ref.at[2 * BLOCK :], pack_hbm.at[2 * BLOCK :])
    for c in stores:
        c.wait()


def dense(packed_rows, big, small):
    xt, tctx, two, xs, sctx, tin, tout, wo, w1, w2, wh = big
    slots, width_t = xt.shape
    width_s, units_s = w1.shape
    padded = HEADS * PAD
    inner_pad = -(-units_s // 128) * 128
    sds = jax.ShapeDtypeStruct
    outs = [
        sds((width_s, slots), BF16),
        sds((padded, slots), BF16),
        sds((width_s, slots), F32),
        sds((packed_rows, units_s // 128 * 128), BF16),
    ]
    anywhere = pl.BlockSpec(memory_space=pl.ANY)
    return pl.pallas_call(
        dense_kernel,
        out_shape=outs,
        in_specs=[anywhere] * len(big) + [VMEM] * len(small),
        out_specs=[anywhere] * len(outs),
        scratch_shapes=[pltpu.VMEM(a.shape, a.dtype) for a in big]
        + [pltpu.VMEM(a.shape, a.dtype) for a in outs]
        + [
            pltpu.VMEM((inner_pad, slots), BF16),
            pltpu.VMEM((units_s, slots), F32),
            pltpu.VMEM((width_t, slots), BF16),
            pltpu.VMEM((width_t, slots), F32),
            pltpu.SemaphoreType.DMA((len(big),)),
            pltpu.SemaphoreType.DMA((6,)),
        ],
        compiler_params=pltpu.CompilerParams(vmem_limit_bytes=BIG),
    )(*big, *small)


def group_sizes():
    seq = lax.axis_size("seq")
    core = 2 if seq % 2 == 0 else 1
    chain = 4 if seq // core % 4 == 0 else 1
    return {"core": core, "batch": lax.axis_size("batch"), "chain": chain, "outer": seq // core // chain}


class Group:
    def __init__(self, name):
        batch, seq = lax.axis_index("batch"), lax.axis_index("seq")
        sizes = group_sizes()
        self.size = sizes[name]
        if name == "batch":
            self.place = batch
            self.device = lambda j: (j, seq)
        else:
            stride = {"core": 1, "chain": sizes["core"], "outer": sizes["core"] * sizes["chain"]}[name]
            self.place = seq // stride % self.size
            self.device = lambda j: (batch, seq + (j - self.place) * stride)

    def other(self, k):
        return (self.place + k) % self.size


class Chain:
    def __init__(self, names, source, scratch, local=None):
        self.names, self.source, self.local = names, source, local
        self.groups = [Group(n) for n in names]
        count = len(names)
        self.outer = Group("outer")
        self.received, self.sums = scratch[:count], scratch[count : 2 * count]
        self.around, self.whole, self.send, self.arrive = scratch[2 * count :]
        rows = self.whole.shape[0]
        self.rows, self.base, base = [], [], 0
        for g in self.groups:
            self.base.append(base)
            rows //= g.size
            base = base + g.place * rows
            self.rows.append(rows)
        self.mine = base
        self.sem = 0
        self.pending = []

    @staticmethod
    def scratch(names, rows, lanes):
        received, sums, copies = [], [], 0
        total, sizes = rows, group_sizes()
        for size in (sizes[n] for n in names):
            rows = rows // size
            received.append(pltpu.VMEM((max(size - 1, 1), rows, lanes), BF16))
            sums.append(pltpu.VMEM((rows, lanes), BF16))
            copies += 2 * (size - 1)
        copies = max(copies + sizes["outer"] - 1, 1)
        return (
            received
            + sums
            + [
                pltpu.VMEM((max(sizes["outer"] - 1, 1), rows, lanes), BF16),
                pltpu.VMEM((total, lanes), BF16),
                pltpu.SemaphoreType.DMA((copies,)),
                pltpu.SemaphoreType.DMA((copies,)),
            ]
        )

    def copy(self, ends):
        at = self.sem
        self.sem += 1

        def form():
            source, target, device = ends()
            return pltpu.make_async_remote_copy(
                src_ref=source,
                dst_ref=target,
                send_sem=self.send.at[at],
                recv_sem=self.arrive.at[at],
                device_id=device,
                device_id_type=MESH,
            )

        form().start()
        self.pending.append(form)

    def scatter(self, k):
        g, rows = self.groups[k], self.rows[k]
        source = self.source if k == 0 else self.sums[k - 1]

        def ends(step):
            other = g.other(step)
            there = pl.ds(pl.multiple_of(other * rows, 16), rows)
            return source.at[there], self.received[k].at[step - 1], g.device(other)

        for step in range(1, g.size):
            self.copy(partial(ends, step))

    def wait(self):
        for form in self.pending:
            form().wait()
        self.pending = []

    def add(self, k):
        self.wait()
        g, rows = self.groups[k], self.rows[k]
        source = self.source if k == 0 else self.sums[k - 1]
        if k == 0 and self.local is not None:
            total = self.local[...].astype(F32)
        else:
            total = source[pl.ds(pl.multiple_of(g.place * rows, 16), rows), :].astype(F32)
        for step in range(1, g.size):
            total = total + self.received[k][step - 1].astype(F32)
        total = total.astype(BF16)
        if k < len(self.groups) - 1 or self.outer.size > 1:
            self.sums[k][...] = total
        if k == len(self.groups) - 1:
            if self.outer.size > 1:
                total = self.exchange(total)
            self.whole[pl.ds(pl.multiple_of(self.mine, 16), rows), :] = total

    def exchange(self, total):
        g = self.outer

        def ends(step):
            return self.sums[-1], self.around.at[step - 1], g.device(g.other(step))

        for step in range(1, g.size):
            self.copy(partial(ends, step))
        self.wait()
        total = total.astype(F32)
        for step in range(1, g.size):
            total = total + self.around[step - 1].astype(F32)
        return total.astype(BF16)

    def gather(self, k):
        g, rows = self.groups[k], self.rows[k]

        def ends(step):
            here = self.whole.at[pl.ds(pl.multiple_of(self.base[k] + g.place * rows, 16), rows)]
            return here, here, g.device(g.other(step))

        for step in range(1, g.size):
            self.copy(partial(ends, step))

    def advance(self, stage):
        count = len(self.groups)
        if 0 < stage <= count:
            self.add(stage - 1)
        else:
            self.wait()
        if stage < count:
            self.scatter(stage)
        elif stage < 2 * count:
            self.gather(2 * count - 1 - stage)


EARLY = (
    (0, 384, ("core", "batch", "chain")),
    (384, 768, ("core", "batch", "chain")),
    (768, 1152, ("core", "chain", "batch")),
)
LATE = (
    (0, 128, ("core", "batch", "chain")),
    (128, 256, ("core", "batch", "chain")),
    (256, 384, ("core", "chain", "batch")),
)


def back_kernel(
    windows,
    sq_hbm,
    skv_hbm,
    dctx_hbm,
    e_hbm,
    g_hbm,
    pack_hbm,
    xs_hbm,
    dres_hbm,
    wq_hbm,
    wk_hbm,
    wv_hbm,
    rows_ref,
    dx_ref,
    early_ref,
    late_ref,
    sq_ref,
    skv_ref,
    dctx_ref,
    e_ref,
    g_ref,
    half_ref,
    xs_ref,
    dres_ref,
    wq_ref,
    wk_ref,
    wv_ref,
    in_sem,
    block_sem,
    dq_ref,
    dkv_ref,
    give_ref,
    take_ref,
    qkv_ref,
    halo_send,
    halo_arrive,
    out_sem,
    *scratch,
):
    step = pl.program_id(0)
    w = (windows - step) % windows
    slots = windows * WIN
    width_s = xs_ref.shape[0]
    batch, seq = lax.axis_index("batch"), lax.axis_index("seq")
    peers = lax.axis_size("seq")
    chains, used = [], 0
    for source, local, cuts in ((pack_hbm, half_ref, EARLY), (qkv_ref, None, LATE)):
        for first, last, names in cuts:
            size = 2 * len(names) + 4
            mine = local.at[:, first:last] if local is not None else None
            chains.append(Chain(names, source.at[:, first:last], scratch[used : used + size], mine))
            used += size
    soon, late = chains[: len(EARLY)], chains[len(EARLY) :]
    first_seq, last_seq = seq == 0, seq == peers - 1

    def halo(side):
        return pltpu.make_async_remote_copy(
            src_ref=give_ref.at[side],
            dst_ref=take_ref.at[1 - side],
            send_sem=halo_send.at[side],
            recv_sem=halo_arrive.at[1 - side],
            device_id=(batch, seq - 1 + 2 * side),
            device_id_type=MESH,
        )

    half_rows = half_ref.shape[0]
    ends = {
        "half": (pack_hbm.at[pl.ds(pl.multiple_of(seq % group_sizes()["core"] * half_rows, 16), half_rows)], half_ref),
        "sq": (sq_hbm, sq_ref),
        "skv": (skv_hbm, skv_ref),
        "dctx": (dctx_hbm, dctx_ref),
        "xs": (xs_hbm, xs_ref),
        "dres": (dres_hbm, dres_ref),
        "wq": (wq_hbm, wq_ref),
        "wk": (wk_hbm, wk_ref),
        "wv": (wv_hbm, wv_ref),
    }
    load = lambda name: pltpu.make_async_copy(*ends[name], in_sem.at[list(ends).index(name)])

    def blocks(number):
        slot, window = number % 2, (windows - number) % windows
        return [
            pltpu.make_async_copy(source.at[window], target.at[slot], block_sem.at[k, slot])
            for k, (source, target) in enumerate(((e_hbm, e_ref), (g_hbm, g_ref)))
        ]

    @pl.when(step == 0)
    def _():
        load("half").start()
        dkv_ref[...] = jnp.zeros_like(dkv_ref)
        take_ref[...] = jnp.zeros_like(take_ref)
        qkv_ref[...] = jnp.zeros_like(qkv_ref)
        barrier = pltpu.get_barrier_semaphore()
        count = 0
        for g in (Group(n) for n in ("core", "batch", "chain", "outer")):
            for k in range(1, g.size):
                pl.semaphore_signal(barrier, inc=1, device_id=g.device(g.other(k)), device_id_type=MESH)
                count += 1

        for move in (1, peers - 1):
            pl.semaphore_signal(
                barrier, inc=1, device_id=(batch, (seq + move) % peers), device_id_type=MESH
            )
        pl.semaphore_wait(barrier, count + 2)

        for c in soon:
            c.advance(0)
        for c in blocks(0):
            c.start()
        for name in ("sq", "skv", "dctx"):
            load(name).start()
        for c in blocks(1):
            c.start()
        for name in ("xs", "dres", "wq", "wk", "wv"):
            load(name).start()
        for name in ("sq", "skv", "dctx", "half"):
            load(name).wait()

    for c in blocks(step):
        c.wait()
    slot = step % 2
    at = pl.multiple_of(w * WIN, WIN)
    left = pl.ds(at, WIN)
    own = pl.ds(pl.multiple_of(at + WIN, WIN), WIN)
    right = pl.ds(pl.multiple_of(at + 2 * WIN, WIN), WIN)
    early_row, late_row = rows_ref[0:1, left], rows_ref[1:2, left]
    early_low, late_low = early_row.astype(BF16), late_row.astype(BF16)

    def one_head(head):
        rows = pl.ds(pl.multiple_of(head * PAD, PAD), PAD)
        query, grad = sq_ref[rows, left], dctx_ref[rows, left]
        stacked = lambda a: jnp.concatenate([a * early_low, a * late_low], axis=0)
        query_fold, grad_fold = stacked(query), stacked(grad)
        beside = lambda k: jnp.concatenate([skv_ref[k, rows, left], skv_ref[k, rows, right]], axis=0)
        keys_fold, values_fold = beside(0), beside(1)
        keys, values = skv_ref[0, rows, own], skv_ref[1, rows, own]
        e_own, e_side = e_ref[slot, head, :WIN, :], e_ref[slot, head, WIN:, :]
        d_own = (e_own.astype(F32) * (tn(values, grad) + g_ref[slot, head, :WIN, :].astype(F32))).astype(BF16)
        d_side = (
            e_side.astype(F32) * (tn(values_fold, grad_fold) + g_ref[slot, head, WIN:, :].astype(F32))
        ).astype(BF16)
        side = nn(keys_fold, d_side)
        d_query = nn(keys, d_own) + early_row * side[:PAD] + late_row * side[PAD:]
        dq_ref[rows, left] = (d_query * HD_S**-0.5).astype(BF16)
        for k, (a, a_fold, b, b_fold, scale) in enumerate(
            ((query, query_fold, d_own, d_side, 1.0 / LOG2E), (grad, grad_fold, e_own, e_side, None))
        ):
            fix = (lambda v: v * scale) if scale else (lambda v: v)
            side = fix(nt(a_fold, b_fold))
            dkv_ref[k, rows, own] += fix(nt(a, b))
            dkv_ref[k, rows, left] += side[:PAD]
            dkv_ref[k, rows, right] += side[PAD:]

    def body(pair, carry):
        one_head(2 * pair)
        one_head(2 * pair + 1)
        return carry

    def send_halo():
        for side, lanes in ((0, slice(0, WIN)), (1, slice(WIN + slots, 2 * WIN + slots))):
            give_ref[side] = dkv_ref[:, :, lanes].astype(BF16)

        @pl.when(jnp.logical_not(first_seq))
        def _():
            halo(0).start()

        @pl.when(jnp.logical_not(last_seq))
        def _():
            halo(1).start()

    def advance(which, stage):
        for c in which:
            c.advance(stage)

    half = PAIRS // 2
    plan = {
        (0, 0): [partial(advance, soon, 1)],
        (1, 1): [send_halo],
        (2, 0): [partial(advance, soon, 2)],
        (3, 0): [partial(advance, soon, 3)],
    }
    for part in range(2):
        lax.fori_loop(part * half, (part + 1) * half, body, 0)
        for k in range(windows):
            for action in plan.get((k, part), []):
                pl.when(step == k)(action)

    @pl.when(step < windows - 2)
    def _():
        for c in blocks(step + 2):
            c.start()

    @pl.when(step == windows - 1)
    def _():
        for name in ("xs", "dres", "wq", "wk", "wv"):
            load(name).wait()

        @pl.when(jnp.logical_not(first_seq))
        def _():
            halo(0).wait_send()
            halo(1).wait_recv()

        @pl.when(jnp.logical_not(last_seq))
        def _():
            halo(1).wait_send()
            halo(0).wait_recv()

        spot = pad_heads()
        plains = []
        for k in range(3):
            if k == 0:
                grad = dq_ref[...]
            else:
                mine = dkv_ref[k - 1, :, WIN : WIN + slots]
                first = mine[:, :WIN] + take_ref[0, k - 1].astype(F32)
                last = mine[:, slots - WIN :] + take_ref[1, k - 1].astype(F32)
                grad = jnp.concatenate([first, mine[:, WIN : slots - WIN], last], axis=1).astype(BF16)
            plain = tn(spot, grad).astype(BF16)
            plains.append(plain)
            qkv_ref[k * BLOCK : k * BLOCK + width_s, :width_s] = nt(xs_ref[...], plain).astype(BF16)
        advance(soon, 4)
        advance(late, 0)
        total = dres_ref[...]
        for w_ref, plain in zip((wq_ref, wk_ref, wv_ref), plains):
            total = total + nn(w_ref[...], plain)
        dx_ref[...] = total.astype(BF16)
        advance(late, 1)
        advance(late, 2)
        advance(soon, 5)
        advance(late, 3)
        advance(soon, 6)

        def put(group, cuts, target, first_sem):
            made = []
            for n, (c, (first, last, _)) in enumerate(zip(group, cuts)):
                made.append(pltpu.make_async_copy(c.whole, target.at[:, first:last], out_sem.at[first_sem + n]))
                made[-1].start()
            return made

        copies = put(soon, EARLY, early_ref, 0)
        advance(late, 4)
        advance(late, 5)
        advance(late, 6)
        copies += put(late, LATE, late_ref, len(EARLY))
        for c in copies:
            c.wait()


def back(sq, skv, dctx, e, g, rows, pack, xs, dres, wq, wk, wv):
    padded, slots = sq.shape
    windows = slots // WIN
    width_s = xs.shape[0]
    packed_rows = pack.shape[0]
    anywhere = pl.BlockSpec(memory_space=pl.ANY)
    held = lambda a: pltpu.VMEM(a.shape, a.dtype)
    scratch = [held(sq), held(skv), held(dctx)]
    scratch += [pltpu.VMEM((2,) + a.shape[1:], a.dtype) for a in (e, g)]
    scratch += [pltpu.VMEM((packed_rows // group_sizes()["core"], pack.shape[1]), BF16)]
    scratch += [held(a) for a in (xs, dres, wq, wk, wv)]
    scratch += [
        pltpu.SemaphoreType.DMA((9,)),
        pltpu.SemaphoreType.DMA((2, 2)),
        pltpu.VMEM((padded, slots), BF16),
        pltpu.VMEM((2, padded, slots + 2 * WIN), F32),
        pltpu.VMEM((2, 2, padded, WIN), BF16),
        pltpu.VMEM((2, 2, padded, WIN), BF16),
        pltpu.VMEM((packed_rows, QKV_LANES), BF16),
        pltpu.SemaphoreType.DMA((2,)),
        pltpu.SemaphoreType.DMA((2,)),
        pltpu.SemaphoreType.DMA((len(EARLY) + len(LATE),)),
    ]
    for first, last, names in EARLY + LATE:
        scratch += Chain.scratch(names, packed_rows, last - first)
    return pl.pallas_call(
        partial(back_kernel, windows),
        grid=(windows,),
        out_shape=[
            jax.ShapeDtypeStruct((width_s, slots), BF16),
            jax.ShapeDtypeStruct(pack.shape, BF16),
            jax.ShapeDtypeStruct((packed_rows, QKV_LANES), BF16),
        ],
        in_specs=[anywhere] * 11 + [VMEM],
        out_specs=[pl.BlockSpec((width_s, slots), lambda i: (0, 0)), anywhere, anywhere],
        scratch_shapes=scratch,
        compiler_params=pltpu.CompilerParams(
            vmem_limit_bytes=BIG,
            dimension_semantics=("arbitrary",),
            collective_id=0,
            has_side_effects=True,
        ),
    )(sq, skv, dctx, e, g, pack, xs, dres, wq, wk, wv, rows)


def unpack_kernel(
    every,
    width_t,
    early_hbm,
    late_hbm,
    dx_in_ref,
    dx_ref,
    loss_ref,
    gq_hbm,
    gk_hbm,
    gv_hbm,
    gwo_hbm,
    ginner_hbm,
    gouter_hbm,
    ghid_hbm,
    bouter_ref,
    binner_ref,
    gain_one_ref,
    shift_one_ref,
    gain_two_ref,
    shift_two_ref,
    early_ref,
    late_ref,
    gq_ref,
    gk_ref,
    gv_ref,
    gwo_ref,
    ginner_ref,
    gouter_ref,
    ghid_ref,
    in_sem,
    out_sem,
):
    width_s = gq_ref.shape[0]
    units = ginner_ref.shape[1]
    scale = 1.0 / every
    full = lambda v: v.astype(F32) * scale
    main = units // 128 * 128
    rest = units - main
    cuts = (slice(3 * BLOCK, 3 * BLOCK + STRIP),) + tuple(slice(k * BLOCK, (k + 1) * BLOCK) for k in range(3))
    loads = [pltpu.make_async_copy(early_hbm.at[c], early_ref.at[c], in_sem.at[k]) for k, c in enumerate(cuts)]
    loads.append(pltpu.make_async_copy(late_hbm, late_ref, in_sem.at[4]))
    for c in loads:
        c.start()
    stores = []

    def store(source, target):
        stores.append(pltpu.make_async_copy(source, target, out_sem.at[len(stores)]))
        stores[-1].start()

    dx_ref[...] = dx_in_ref[...]
    loads[0].wait()
    strip = full(early_ref[3 * BLOCK : 3 * BLOCK + STRIP, :])
    turned = lambda at, n: jnp.transpose(strip[:, at : at + n])
    for k, ref in enumerate((gain_one_ref, shift_one_ref, gain_two_ref, shift_two_ref)):
        ref[...] = strip[rest + k, :width_s]
    bouter_ref[...] = strip[rest, STRIP_OUTER : STRIP_OUTER + width_s]
    loads[1].wait()
    gouter_ref[:, :main] = full(early_ref[:width_s, :main])
    gouter_ref[:, main:] = turned(STRIP_OUTER, STRIP_BIAS - STRIP_OUTER)[:width_s, :rest]
    store(gouter_ref, gouter_hbm)
    loads[2].wait()
    ginner_ref[:, :main] = full(early_ref[BLOCK : BLOCK + width_s, :main])
    ginner_ref[:, main:] = turned(0, STRIP_OUTER)[:width_s, :rest]
    store(ginner_ref, ginner_hbm)
    first = full(early_ref[BLOCK + width_s : BLOCK + width_s + 8, :main])[0:1]
    binner_ref[...] = jnp.concatenate([first, turned(STRIP_BIAS, 128)[0:1, :rest]], axis=1)[0]
    loads[3].wait()
    third = slice(2 * BLOCK, 2 * BLOCK + width_s)
    ghid_ref[...] = full(early_ref[third, :width_t])
    store(ghid_ref, ghid_hbm)
    gwo_ref[...] = full(early_ref[third, width_t : width_t + width_s])
    store(gwo_ref, gwo_hbm)
    loads[4].wait()
    for k, (ref, hbm) in enumerate(((gq_ref, gq_hbm), (gk_ref, gk_hbm), (gv_ref, gv_hbm))):
        ref[...] = full(late_ref[k * BLOCK : k * BLOCK + width_s, :width_s])
        store(ref, hbm)
    part = early_ref[2 * BLOCK + width_s : 2 * BLOCK + width_s + 8, :128].astype(F32)
    total = jnp.sum(jnp.sum(part, axis=0, keepdims=True), axis=1, keepdims=True)
    loss_ref[...] = total
    for c in stores:
        c.wait()


def unpack(every, width_t, units, early, late, dx):
    width_s = dx.shape[0]
    sds = lambda *shape: jax.ShapeDtypeStruct(shape, F32)
    square = sds(width_s, width_s)
    large = [square, square, square, square, sds(width_s, units), sds(width_s, units), sds(width_s, width_t)]
    vectors = [sds(width_s), sds(units)] + [sds(width_s)] * 4
    anywhere = pl.BlockSpec(memory_space=pl.ANY)
    return pl.pallas_call(
        partial(unpack_kernel, every, width_t),
        out_shape=[jax.ShapeDtypeStruct(dx.shape, BF16), sds(1, 1)] + large + vectors,
        in_specs=[anywhere, anywhere, VMEM],
        out_specs=[VMEM] * 2 + [anywhere] * len(large) + [VMEM] * len(vectors),
        scratch_shapes=[pltpu.VMEM(early.shape, BF16), pltpu.VMEM(late.shape, BF16)]
        + [pltpu.VMEM(a.shape, F32) for a in large]
        + [pltpu.SemaphoreType.DMA((5,)), pltpu.SemaphoreType.DMA((len(large),))],
        compiler_params=pltpu.CompilerParams(vmem_limit_bytes=BIG),
    )(early, late, dx)


def local(
    inputs,
    teacher_input,
    filled_slot_mask,
    seg_lengths,
    query_weight,
    key_weight,
    value_weight,
    w_output,
    gain_one,
    shift_one,
    w_inner,
    b_inner,
    w_outer,
    b_outer,
    gain_two,
    shift_two,
    w_hidden,
    teacher_query_weight,
    teacher_key_weight,
    teacher_value_weight,
    teacher_output,
    teacher_gain_one,
    teacher_shift_one,
    teacher_inner,
    teacher_outer,
    teacher_gain_two,
    teacher_shift_two,
):
    xs = jnp.transpose(inputs[0])
    xt = teacher_input[0]
    slots, width_t = xt.shape
    width_s = xs.shape[0]
    stats, loss_rows, rows, tctx, sctx, sq, skv, e, g = attend(
        filled_slot_mask,
        seg_lengths,
        xt,
        xs,
        teacher_query_weight,
        teacher_key_weight,
        teacher_value_weight,
        query_weight,
        key_weight,
        value_weight,
    )
    devices = lax.axis_size("seq") * lax.axis_size("batch")
    sizes = group_sizes()
    unit = 16 * sizes["core"] * sizes["batch"] * sizes["chain"]
    packed_rows = -(-3 * BLOCK // unit) * unit
    out, dctx, dres, pack = dense(
        packed_rows,
        (
            xt,
            tctx,
            teacher_output,
            xs,
            sctx,
            teacher_inner,
            teacher_outer,
            w_output,
            w_inner,
            jnp.transpose(w_outer),
            w_hidden,
        ),
        (stats, rows, loss_rows)
        + (
            teacher_gain_one,
            teacher_shift_one,
            teacher_gain_two,
            teacher_shift_two,
            gain_one,
            shift_one,
            b_outer,
            gain_two,
            shift_two,
            b_inner,
        ),
    )
    dx, early, late = back(sq, skv, dctx, e, g, rows, pack, xs, dres, query_weight, key_weight, value_weight)
    dx, loss, gq, gk, gv, gwo, ginner, gouter, ghid, *vectors = unpack(
        slots * devices, width_t, w_inner.shape[1], early, late, dx
    )
    g_b_outer, g_b_inner, g_gain_one, g_shift_one, g_gain_two, g_shift_two = vectors
    return (
        jnp.transpose(out)[None],
        jnp.transpose(dx)[None],
        loss[0, 0] / (slots * devices * width_t),
        gq,
        gk,
        gv,
        gwo,
        g_gain_one,
        g_shift_one,
        ginner,
        g_b_inner,
        jnp.transpose(gouter),
        g_b_outer,
        g_gain_two,
        g_shift_two,
        ghid,
    )


def solution(mesh):
    row_split = P("batch", "seq", None)
    return jax.shard_map(
        local,
        mesh=mesh,
        in_specs=(row_split, row_split, P("batch", None), P("batch", None)) + (P(),) * 23,
        out_specs=(row_split, row_split) + (P(),) * 14,
        check_vma=False,
    )
```

```python
from functools import partial

import jax
import jax.numpy as jnp
from jax import lax
from jax.experimental import pallas as pl
from jax.experimental.pallas import tpu as pltpu
from jax.sharding import PartitionSpec as P

HEADS = 12
HD_S = 26
HD_T = 64
WIN = 256
PAD = 32
SLOT_ONE = 26
PAIRS = HEADS // 2
CHUNK = 64
TAIL = 16
SLOTS = 4
BLOCK = 320
STRIP = 64
STRIP_OUTER = 384
STRIP_BIAS = 768
QKV_LANES = 384
MESH = pl.DeviceIdType.MESH
EPSILON = 1e-05
NEGATIVE = -1e30
LOG2E = 1.4426950408889634
F32 = jnp.float32
BF16 = jnp.bfloat16
VMEM = pl.BlockSpec(memory_space=pltpu.VMEM)
BIG = 60 << 20


def mm(left, right, dims):
    return lax.dot_general(left, right, ((dims[:1], dims[1:]), ((), ())), preferred_element_type=F32)


def nn(left, right):
    return mm(left, right, (1, 0))


def tn(left, right):
    return mm(left, right, (0, 0))


def nt(left, right):
    return mm(left, right, (1, 1))


def tt(left, right):
    return mm(left, right, (0, 1))


def pad_heads():
    row = lax.broadcasted_iota(jnp.int32, (HEADS * PAD, HEADS * HD_S), 0)
    col = lax.broadcasted_iota(jnp.int32, (HEADS * PAD, HEADS * HD_S), 1)
    spot = jnp.zeros((HEADS * PAD, HEADS * HD_S), F32)
    for head in range(HEADS):
        here = (row - head * PAD == col - head * HD_S) & (col >= head * HD_S) & (col < (head + 1) * HD_S)
        spot = jnp.where(here, 1.0, spot)
    return spot.astype(BF16)


def window_rows(mask_ref, lengths_ref, seq_index, windows, row_windows):
    lengths = lengths_ref[...].astype(F32)
    order = lax.broadcasted_iota(jnp.int32, lengths.shape, 1)
    lane = lax.broadcasted_iota(jnp.int32, (1, WIN), 1).astype(F32)
    out = []
    for j in range(windows + 2):
        number = seq_index * windows + (j - 1)
        inside = (number >= 0) & (number < row_windows)
        safe = jnp.clip(number, 0, row_windows - 1)
        start = jnp.sum(jnp.where(order < safe, lengths, 0.0), axis=1, keepdims=True)
        offset = start - (safe * WIN).astype(F32)
        late = (lane >= offset).astype(F32)
        filled = mask_ref[:, pl.ds(pl.multiple_of(safe * WIN, WIN), WIN)]
        filled = jnp.where(inside, filled.astype(F32), 0.0)
        out.append((late, filled))
    return out


def stack_rows(*rows):
    n = rows[0].shape[1]
    index = lax.broadcasted_iota(jnp.int32, (8, n), 0)
    block = jnp.zeros((8, n), F32)
    for k, row in enumerate(rows):
        block = jnp.where(index == k, row, block)
    return block.astype(BF16)


def attend_kernel(
    windows,
    row_windows,
    mask_ref,
    lengths_ref,
    xt_hbm,
    xs_ref,
    wtq_hbm,
    wtk_hbm,
    wtv_hbm,
    wq_ref,
    wk_ref,
    wv_ref,
    stats_ref,
    loss_ref,
    rows_ref,
    tctx_hbm,
    sctx_hbm,
    sq_hbm,
    skv_hbm,
    saved_e_hbm,
    saved_g_hbm,
    x_ref,
    xs_side_ref,
    wt_ref,
    bias_ref,
    wst_ref,
    tq_ref,
    tk_ref,
    tv_ref,
    sq_ref,
    skv_ref,
    tctx_ref,
    sctx_ref,
    e_ref,
    g_ref,
    work_ref,
    low_ref,
    in_sem,
    halo_send,
    halo_arrive,
    kv_sem,
    out_sem,
):
    slots = windows * WIN
    batch, seq = lax.axis_index("batch"), lax.axis_index("seq")
    peers = lax.axis_size("seq")
    has_left, has_right = seq > 0, seq < peers - 1
    width_t = x_ref.shape[1]
    extended = slots + 2 * WIN

    barrier = pltpu.get_barrier_semaphore()
    for move in (1, peers - 1):
        pl.semaphore_signal(barrier, inc=1, device_id=(batch, (seq + move) % peers), device_id_type=MESH)
    loads = [pltpu.make_async_copy(xt_hbm, x_ref.at[pl.ds(WIN, slots)], in_sem.at[0])]
    for k, w_hbm in enumerate((wtq_hbm, wtk_hbm, wtv_hbm)):
        loads.append(pltpu.make_async_copy(w_hbm, wt_ref.at[k], in_sem.at[1 + k]))
    for c in loads:
        c.start()
    pl.semaphore_wait(barrier, 2)

    def halo(side):
        device = (batch, seq - 1 + 2 * side)
        first = pl.multiple_of(side * (slots - WIN), WIN)
        return [
            pltpu.make_async_remote_copy(
                src_ref=xt_hbm.at[pl.ds(first, WIN)],
                dst_ref=x_ref.at[pl.ds(pl.multiple_of((1 - side) * (WIN + slots), WIN), WIN)],
                send_sem=halo_send.at[0, side],
                recv_sem=halo_arrive.at[0, 1 - side],
                device_id=device,
                device_id_type=MESH,
            ),
            pltpu.make_async_remote_copy(
                src_ref=xs_ref.at[:, pl.ds(first, WIN)],
                dst_ref=xs_side_ref.at[1 - side],
                send_sem=halo_send.at[1, side],
                recv_sem=halo_arrive.at[1, 1 - side],
                device_id=device,
                device_id_type=MESH,
            ),
        ]

    for side, present in ((0, has_left), (1, has_right)):

        @pl.when(present)
        def _():
            for c in halo(side):
                c.start()

        @pl.when(jnp.logical_not(present))
        def _():
            x_ref[side * (WIN + slots) : side * (WIN + slots) + WIN, :] = jnp.zeros((WIN, width_t), BF16)
            xs_side_ref[side] = jnp.zeros(xs_side_ref.shape[1:], BF16)

    info = window_rows(mask_ref, lengths_ref, seq, windows, row_windows)
    eye = lax.broadcasted_iota(jnp.int32, (WIN, WIN), 0) == lax.broadcasted_iota(jnp.int32, (WIN, WIN), 1)
    rows_ref[...] = jnp.zeros_like(rows_ref)
    for w in range(windows):
        late, filled = info[w + 1]
        late_l, filled_l = info[w]
        late_r, filled_r = info[w + 2]
        early = 1.0 - late
        here = slice(w * WIN, (w + 1) * WIN)
        rows_ref[0:1, here] = early
        rows_ref[1:2, here] = late
        rows_ref[2:3, here] = filled
        query = stack_rows(early, late)
        own = tn(stack_rows(NEGATIVE * (1.0 - early * filled), NEGATIVE * (1.0 - late * filled)), query)
        bias_ref[w, :WIN, :] = jnp.where(eye, 0.0, own)
        bias_ref[w, WIN:, :] = tn(
            stack_rows(
                NEGATIVE * (1.0 - late_l * filled_l), NEGATIVE * (1.0 - (1.0 - late_r) * filled_r)
            ),
            query,
        )
    loss_ref[...] = jnp.zeros_like(loss_ref)
    stats_ref[...] = jnp.zeros_like(stats_ref)
    spot = pad_heads()
    padded = HEADS * PAD
    row = lax.broadcasted_iota(jnp.int32, (padded, 1), 0) % PAD
    ones = (row >= SLOT_ONE) & (row < SLOT_ONE + 3)

    xs = xs_ref[...]
    for k, w_ref in enumerate((wq_ref, wk_ref, wv_ref)):
        wst_ref[k] = nt(spot, w_ref[...]).astype(BF16)
        made = nn(wst_ref[k], xs)
        if k == 0:
            sq_ref[...] = (made * (LOG2E * HD_S**-0.5)).astype(BF16)
        else:
            if k == 2:
                made = jnp.where(ones, 1.0, made)
            skv_ref[k - 1, :, WIN : WIN + slots] = made.astype(BF16)
    tail = (lax.broadcasted_iota(jnp.int32, (TAIL, extended), 0) == 0).astype(BF16)
    for head in range(HEADS):
        tv_ref[head * (HD_T + TAIL) + HD_T : (head + 1) * (HD_T + TAIL), :] = tail

    def put_values(made, first_head, lanes):
        for j in range(made.shape[0] // HD_T):
            at = pl.multiple_of((first_head + j) * (HD_T + TAIL), TAIL)
            tv_ref[pl.ds(at, HD_T), lanes] = made[j * HD_T : (j + 1) * HD_T]

    part = width_t // 2
    loads[0].wait()
    for k in range(3):
        loads[1 + k].wait()

        def project(half, carry, k=k):
            rows = pl.ds(pl.multiple_of(half * part, 128), part)
            made = tt(wt_ref[k, :, rows], x_ref[WIN : WIN + slots, :])
            if k == 0:
                tq_ref[rows, :] = (made * (LOG2E * HD_T**-0.5)).astype(BF16)
            elif k == 1:
                tk_ref[rows, WIN : WIN + slots] = made.astype(BF16)
            else:
                put_values(made.astype(BF16), half * (HEADS // 2), slice(WIN, WIN + slots))
            return carry

        lax.fori_loop(0, 2, project, 0)

    def project_side(side, carry):
        @pl.when(jnp.where(side == 0, has_left, has_right))
        def _():
            for sent, landed in zip(halo(side), halo(1 - side)):
                sent.wait_send()
                landed.wait_recv()

        lanes = pl.ds(pl.multiple_of(side * (WIN + slots), WIN), WIN)
        for k in (1, 2):
            made = tt(wt_ref[k], x_ref[lanes, :]).astype(BF16)
            if k == 1:
                tk_ref[:, lanes] = made
            else:
                put_values(made, 0, lanes)
            made = nn(wst_ref[k], xs_side_ref[side])
            if k == 2:
                made = jnp.where(ones, 1.0, made)
            skv_ref[k - 1, :, lanes] = made.astype(BF16)
        return carry

    lax.fori_loop(0, 2, project_side, 0)
    finals = [
        pltpu.make_async_copy(sq_ref, sq_hbm, kv_sem.at[0]),
        pltpu.make_async_copy(skv_ref, skv_hbm, kv_sem.at[1]),
    ]
    for c in finals:
        c.start()

    def stores(pair, which):
        slot = pair % 2
        t_rows = pl.ds(pl.multiple_of(pair * 2 * HD_T, 2 * HD_T), 2 * HD_T)
        s_rows = pl.ds(pl.multiple_of(pair * 2 * PAD, 2 * PAD), 2 * PAD)
        heads = pl.ds(pair * 2, 2)
        ends = (
            (e_ref.at[slot], saved_e_hbm.at[:, heads]),
            (g_ref.at[slot], saved_g_hbm.at[:, heads]),
            (tctx_ref.at[t_rows], tctx_hbm.at[t_rows]),
            (sctx_ref.at[s_rows], sctx_hbm.at[s_rows]),
        )
        return [pltpu.make_async_copy(*ends[k], out_sem.at[k, pair]) for k in which]

    def one_pair(pair, carry):
        @pl.when(pair >= 2)
        def _():
            for c in stores(pair - 2, (0, 1)):
                c.wait()

        attend_pair(pair)
        for c in stores(pair, range(4)):
            c.start()
        return carry

    def attend_pair(pair):
        e_out, g_out = e_ref.at[pair % 2], g_ref.at[pair % 2]
        def rows_of(w):
            left = slice(w * WIN, (w + 1) * WIN)
            own = slice((w + 1) * WIN, (w + 2) * WIN)
            right = slice((w + 2) * WIN, (w + 3) * WIN)
            return left, own, right, rows_ref[0:1, left], rows_ref[1:2, left], rows_ref[2:3, left]

        def first_pass(w, q_ref, k_ref, rows, work_ref):
            left, own, right, early, late, _ = rows_of(w)
            query = q_ref[rows, left]
            query_fold = jnp.concatenate([query * early.astype(BF16), query * late.astype(BF16)], axis=0)
            keys = k_ref[rows, own]
            keys_fold = jnp.concatenate([k_ref[rows, left], k_ref[rows, right]], axis=0)
            top = None
            for part, (a, b) in enumerate(((keys, query), (keys_fold, query_fold))):
                raw = tn(a, b)
                for c in range(0, WIN, CHUNK):
                    block = raw[c : c + CHUNK] + bias_ref[w, part * WIN + c : part * WIN + c + CHUNK, :]
                    work_ref[part * WIN + c : part * WIN + c + CHUNK, :] = block
                    for r in range(0, CHUNK, 8):
                        piece = block[r : r + 8]
                        top = piece if top is None else jnp.maximum(top, piece)
            return jnp.max(top, axis=0, keepdims=True)

        def second_pass(work_ref, top, low_ref):
            for c in range(0, 2 * WIN, CHUNK):
                e = jnp.exp2(work_ref[c : c + CHUNK, :] - top)
                work_ref[c : c + CHUNK, :] = e
                low_ref[c : c + CHUNK, :] = e.astype(BF16)

        def mix(w, v_ref, rows, low_ref, head_width):
            left, own, right, early, late, _ = rows_of(w)
            values = v_ref[rows, own]
            values_fold = jnp.concatenate([v_ref[rows, left], v_ref[rows, right]], axis=0)
            mixed = nn(values, low_ref[:WIN, :])
            side = nn(values_fold, low_ref[WIN:, :])
            n = values.shape[0]
            mixed = mixed + early * side[:n] + late * side[n:]
            inverse = 1.0 / mixed[head_width : head_width + 1]
            return mixed[: -TAIL if head_width == HD_T else n] * inverse, inverse

        units = [(w, h) for w in range(windows) for h in range(2)]
        state = {}

        def refs(u):
            w, h = units[u]
            head = 2 * pair + h
            t_rows = pl.ds(pl.multiple_of(head * HD_T, HD_T), HD_T)
            s_rows = pl.ds(pl.multiple_of(head * PAD, PAD), PAD)
            v_rows = pl.ds(pl.multiple_of(head * (HD_T + TAIL), TAIL), HD_T + TAIL)
            slot = u % SLOTS
            return w, h, t_rows, s_rows, v_rows, work_ref.at[2 * slot], work_ref.at[2 * slot + 1], low_ref.at[slot]

        def score_stage(u):
            w, h, t_rows, s_rows, _, work_t, work_s, _ = refs(u)
            state[u] = [
                first_pass(w, tq_ref, tk_ref, t_rows, work_t),
                first_pass(w, sq_ref, skv_ref.at[0], s_rows, work_s),
            ]

        def power_stage(u):
            w, h, _, _, _, work_t, work_s, low_t = refs(u)
            second_pass(work_t, state[u][0], low_t)
            second_pass(work_s, state[u][1], e_out.at[w, h])

        def mix_stage(u):
            w, h, t_rows, s_rows, v_rows, _, _, low_t = refs(u)
            left = rows_of(w)[0]
            t_mixed, t_inv = mix(w, tv_ref, v_rows, low_t, HD_T)
            s_mixed, s_inv = mix(w, skv_ref.at[1], s_rows, e_out.at[w, h], SLOT_ONE)
            tctx_ref[t_rows, left] = t_mixed.astype(BF16)
            sctx_ref[s_rows, left] = s_mixed
            state[u] = [t_inv, s_inv]

        def gap_stage(u):
            w, h, _, _, _, work_t, work_s, _ = refs(u)
            left, _, _, _, _, filled = rows_of(w)
            t_inv, s_inv = state.pop(u)
            width = 2.0 * HEADS * HD_T
            scale_s = (width * filled) * s_inv * s_inv
            scale_t = (width * filled) * s_inv * t_inv
            square = jnp.zeros((8, WIN), F32)
            cross = jnp.zeros((8, WIN), F32)
            for c in range(0, 2 * WIN, CHUNK):
                s = work_s[c : c + CHUNK, :]
                gap = s * scale_s - work_t[c : c + CHUNK, :] * scale_t
                g_out[w, h, c : c + CHUNK, :] = gap.astype(BF16)
                for r in range(0, CHUNK, 8):
                    piece = gap[r : r + 8]
                    square += piece * piece
                    cross += piece * s[r : r + 8]
            square = jnp.sum(square, axis=0, keepdims=True)
            cross = jnp.sum(cross, axis=0, keepdims=True)
            back = 1.0 / (s_inv * width)
            stats_ref[pair, h : h + 1, left] = s_inv
            stats_ref[pair, 2 + h : 3 + h, left] = cross
            loss_ref[0:1, left] += square * back * back

        last = len(units)
        for u in range(last + 2):
            if u < last:
                score_stage(u)
            if 0 <= u - 1 < last:
                power_stage(u - 1)
            if 0 <= u - 2 < last:
                mix_stage(u - 2)
                gap_stage(u - 2)


    lax.fori_loop(0, PAIRS, one_pair, 0)
    for pair in range(PAIRS):
        for c in stores(pair, range(0 if pair >= PAIRS - 2 else 2, 4)):
            c.wait()
    for c in finals:
        c.wait()


def attend(mask, lengths, xt, xs, wtq, wtk, wtv, wq, wk, wv):
    slots, width_t = xt.shape
    width_s = xs.shape[0]
    windows = slots // WIN
    row_windows = mask.shape[1] // WIN
    padded = HEADS * PAD
    extended = slots + 2 * WIN
    sds = jax.ShapeDtypeStruct
    anywhere = pl.BlockSpec(memory_space=pl.ANY)
    saved = (windows, HEADS, 2 * WIN, WIN)
    return pl.pallas_call(
        partial(attend_kernel, windows, row_windows),
        out_shape=(
            sds((PAIRS, 8, slots), F32),
            sds((8, slots), F32),
            sds((8, slots), F32),
            sds((width_t, slots), BF16),
            sds((padded, slots), F32),
            sds((padded, slots), BF16),
            sds((2, padded, extended), BF16),
            sds(saved, BF16),
            sds(saved, BF16),
        ),
        in_specs=[VMEM, VMEM, anywhere, VMEM] + [anywhere] * 3 + [VMEM] * 3,
        out_specs=[VMEM] * 3 + [anywhere] * 6,
        scratch_shapes=[
            pltpu.VMEM((extended, width_t), BF16),
            pltpu.VMEM((2, width_s, WIN), BF16),
            pltpu.VMEM((3, width_t, width_t), BF16),
            pltpu.VMEM((windows, 2 * WIN, WIN), F32),
            pltpu.VMEM((3, padded, width_s), BF16),
            pltpu.VMEM((width_t, slots), BF16),
            pltpu.VMEM((width_t, extended), BF16),
            pltpu.VMEM((HEADS * (HD_T + TAIL), extended), BF16),
            pltpu.VMEM((padded, slots), BF16),
            pltpu.VMEM((2, padded, extended), BF16),
            pltpu.VMEM((width_t, slots), BF16),
            pltpu.VMEM((padded, slots), F32),
            pltpu.VMEM((2, windows, 2, 2 * WIN, WIN), BF16),
            pltpu.VMEM((2, windows, 2, 2 * WIN, WIN), BF16),
            pltpu.VMEM((2 * SLOTS, 2 * WIN, WIN), F32),
            pltpu.VMEM((SLOTS, 2 * WIN, WIN), BF16),
            pltpu.SemaphoreType.DMA((4,)),
            pltpu.SemaphoreType.DMA((2, 2)),
            pltpu.SemaphoreType.DMA((2, 2)),
            pltpu.SemaphoreType.DMA((2,)),
            pltpu.SemaphoreType.DMA((4, PAIRS)),
        ],
        compiler_params=pltpu.CompilerParams(
            vmem_limit_bytes=BIG, collective_id=1, has_side_effects=True
        ),
    )(mask, lengths, xt, xs, wtq, wtk, wtv, wq, wk, wv)


def normalize(values, gain, shift):
    n = values.shape[0]
    center = values - jnp.sum(values, axis=0, keepdims=True) * (1.0 / n)
    rscale = lax.rsqrt(jnp.sum(center * center, axis=0, keepdims=True) * (1.0 / n) + EPSILON)
    unit = center * rscale
    return unit * gain + shift, unit, rscale


def normalize_back(grad, unit, rscale, gain):
    n = grad.shape[0]
    scaled = grad * gain
    first = jnp.sum(scaled, axis=0, keepdims=True) * (1.0 / n)
    second = jnp.sum(scaled * unit, axis=0, keepdims=True) * (1.0 / n)
    return rscale * (scaled - first - unit * second)


def fold_lanes(values):
    total = values[:, :128]
    for at in range(128, values.shape[1], 128):
        total = total + values[:, at : at + 128]
    return total


ROOT_HALF = 0.7071067811865476
ROOT_PI = 0.3989422804014327


DENSE_IN = ("xt", "tctx", "two", "xs", "sctx", "tin", "tout", "wo", "w1", "w2", "wh")


def dense_kernel(
    xt_hbm,
    tctx_hbm,
    two_hbm,
    xs_hbm,
    sctx_hbm,
    tin_hbm,
    tout_hbm,
    wo_hbm,
    w1_hbm,
    w2_hbm,
    wh_hbm,
    stats_ref,
    rows_ref,
    loss_ref,
    t_gain_one_ref,
    t_shift_one_ref,
    t_gain_two_ref,
    t_shift_two_ref,
    gain_one_ref,
    shift_one_ref,
    b_outer_ref,
    gain_two_ref,
    shift_two_ref,
    b_inner_ref,
    out_hbm,
    dctx_hbm,
    dres_hbm,
    pack_hbm,
    xt_ref,
    tctx_ref,
    two_ref,
    xs_ref,
    sctx_ref,
    tin_ref,
    tout_ref,
    wo_ref,
    w1_ref,
    w2_ref,
    wh_ref,
    out_ref,
    dctx_ref,
    dres_ref,
    pack_ref,
    act_ref,
    slope_ref,
    t_low_ref,
    t_sum_ref,
    in_sem,
    out_sem,
):
    sources = (
        xt_hbm, tctx_hbm, two_hbm, xs_hbm, sctx_hbm, tin_hbm, tout_hbm, wo_hbm, w1_hbm, w2_hbm, wh_hbm
    )
    targets = (xt_ref, tctx_ref, two_ref, xs_ref, sctx_ref, tin_ref, tout_ref, wo_ref, w1_ref, w2_ref, wh_ref)
    loads = {
        name: pltpu.make_async_copy(source, target, in_sem.at[k])
        for k, (name, source, target) in enumerate(zip(DENSE_IN, sources, targets))
    }
    for c in loads.values():
        c.start()
    width_s, units_s = w1_ref.shape
    width_t, units_t = tin_ref.shape
    slots = xt_ref.shape[0]
    low = lambda v: v.astype(BF16)
    stores = []

    def store(source, target):
        stores.append(pltpu.make_async_copy(source, target, out_sem.at[len(stores)]))
        stores[-1].start()

    def columns(*refs):
        n = refs[0].shape[0]
        index = lax.broadcasted_iota(jnp.int32, (8, n), 0)
        block = jnp.zeros((8, n), F32)
        for k, ref in enumerate(refs):
            block = jnp.where(index == k, ref[...].reshape(1, n), block)
        turned = jnp.transpose(block)
        return [turned[:, k : k + 1] for k in range(len(refs))]

    t_gain_one, t_shift_one, t_gain_two, t_shift_two = columns(
        t_gain_one_ref, t_shift_one_ref, t_gain_two_ref, t_shift_two_ref
    )
    gain_one, shift_one, b_outer, gain_two, shift_two = columns(
        gain_one_ref, shift_one_ref, b_outer_ref, gain_two_ref, shift_two_ref
    )
    (b_inner,) = columns(b_inner_ref)
    spot = pad_heads()
    pack_ref[...] = jnp.zeros_like(pack_ref)
    act_ref[units_s:, :] = jnp.ones((act_ref.shape[0] - units_s, slots), BF16)
    for name in ("xt", "tctx", "two"):
        loads[name].wait()
    start = jnp.transpose(xt_ref[...]).astype(F32) + tn(two_ref[...], tctx_ref[...])
    t_normed = normalize(start, t_gain_one, t_shift_one)[0]
    t_low_ref[...] = low(t_normed)
    t_sum_ref[...] = t_normed
    for name in ("xs", "sctx", "tin", "tout"):
        loads[name].wait()

    def feed_forward(c, carry):
        units = pl.ds(pl.multiple_of(c * width_t, width_t), width_t)
        pre = tn(tin_ref[:, units], t_low_ref[...])
        active = low(0.5 * pre * (1.0 + lax.erf(pre * ROOT_HALF)))
        t_sum_ref[...] += tn(tout_ref[units, :], active)
        return carry

    lax.fori_loop(0, units_t // width_t, feed_forward, 0)
    target = normalize(t_sum_ref[...], t_gain_two, t_shift_two)[0]
    for name in ("wo", "w1", "w2", "wh"):
        loads[name].wait()
    wop = low(nn(spot, wo_ref[...]))
    context = sctx_ref[...]
    context_low = low(context)
    normed, unit_one, rscale_one = normalize(
        xs_ref[...].astype(F32) + tn(wop, context_low), gain_one, shift_one
    )
    normed_low = low(normed)
    pre = tn(w1_ref[...], normed_low) + b_inner
    half = 0.5 * (1.0 + lax.erf(pre * ROOT_HALF))
    slope_ref[...] = half + pre * (ROOT_PI * jnp.exp(-0.5 * pre * pre))
    act_ref[:units_s, :] = low(pre * half)
    student, unit_two, rscale_two = normalize(
        normed + nn(w2_ref[...], act_ref[:units_s, :]) + b_outer, gain_two, shift_two
    )
    student_low = low(student)
    out_ref[...] = student_low
    store(out_ref, out_hbm)
    gap = tn(wh_ref[...], student_low) - target
    filled = rows_ref[2:3, :]
    masked = filled * gap
    d_proj = low(2.0 * masked)
    third = slice(2 * BLOCK, 2 * BLOCK + width_s)
    pack_ref[third, :width_t] = low(nt(student_low, d_proj))
    d_student = nn(wh_ref[...], d_proj)
    d_two = normalize_back(d_student, unit_two, rscale_two, gain_two)
    d_outer = low(d_two)
    main = units_s // 128 * 128
    spare = units_s - main
    strip = 3 * BLOCK
    pack_ref[:width_s, :main] = low(nt(d_outer, act_ref[:main, :]))
    pack_ref[strip : strip + STRIP, STRIP_OUTER : STRIP_OUTER + width_s] = low(
        nt(act_ref[main : main + STRIP, :], d_outer)
    )
    store(pack_ref.at[:BLOCK], pack_hbm.at[:BLOCK])
    d_inner = low(tn(w2_ref[...], d_outer) * slope_ref[...])
    ones = jnp.ones((8, slots), BF16)
    pack_ref[BLOCK : BLOCK + width_s, :main] = low(nt(normed_low, d_inner[:main]))
    pack_ref[BLOCK + width_s : BLOCK + width_s + 8, :main] = low(nt(ones, d_inner[:main]))
    pack_ref[strip : strip + spare, :width_s] = low(nt(d_inner[main:], normed_low))
    pack_ref[strip : strip + spare, STRIP_BIAS : STRIP_BIAS + 8] = low(nt(d_inner[main:], ones))
    store(pack_ref.at[BLOCK : 2 * BLOCK], pack_hbm.at[BLOCK : 2 * BLOCK])
    d_normed = nn(w1_ref[...], d_inner) + d_two
    d_one = normalize_back(d_normed, unit_one, rscale_one, gain_one)
    dres_ref[...] = d_one
    store(dres_ref, dres_hbm)
    d_att = low(d_one)
    gwo = low(nt(context_low, d_att))
    pack_ref[third, width_t : width_t + width_s] = low(tn(spot, gwo))
    d_context = nn(wop, d_att)
    row = lax.broadcasted_iota(jnp.int32, (PAD, slots), 0)
    for head in range(HEADS):
        pair, h = head // 2, head % 2
        inverse = stats_ref[pair, h : h + 1, :]
        cross = stats_ref[pair, 2 + h : 3 + h, :]
        rows = slice(head * PAD, (head + 1) * PAD)
        part = low(d_context[rows] * inverse).astype(F32)
        delta = -jnp.sum(part * context[rows], axis=0, keepdims=True) - inverse * cross
        high = low(delta).astype(F32)
        rest = delta - high
        middle = low(rest).astype(F32)
        part = jnp.where(row == SLOT_ONE, high, part)
        part = jnp.where(row == SLOT_ONE + 1, middle, part)
        part = jnp.where(row == SLOT_ONE + 2, rest - middle, part)
        dctx_ref[rows, :] = low(part)
    store(dctx_ref, dctx_hbm)
    lane = lax.broadcasted_iota(jnp.int32, (width_s, 128), 1)
    sums = jnp.zeros((width_s, 128), F32)
    for k, values in enumerate((d_normed * unit_one, d_normed, d_student * unit_two, d_student)):
        sums = jnp.where(lane == k, jnp.sum(fold_lanes(values), axis=1, keepdims=True), sums)
    pack_ref[strip + spare : strip + spare + 8, :width_s] = low(jnp.transpose(sums)[:8])
    square = jnp.sum(fold_lanes(masked * gap).reshape(-1, 8, 128), axis=0)
    row = lax.broadcasted_iota(jnp.int32, (8, 128), 0)
    for c in range(slots // 128):
        square += jnp.where(row == c % 8, width_t * loss_ref[0:1, c * 128 : (c + 1) * 128], 0.0)
    pack_ref[2 * BLOCK + width_s : 2 * BLOCK + width_s + 8, :128] = low(square)
    store(pack_ref.at[2 * BLOCK :], pack_hbm.at[2 * BLOCK :])
    for c in stores:
        c.wait()


def dense(packed_rows, big, small):
    xt, tctx, two, xs, sctx, tin, tout, wo, w1, w2, wh = big
    slots, width_t = xt.shape
    width_s, units_s = w1.shape
    padded = HEADS * PAD
    inner_pad = -(-units_s // 128) * 128
    sds = jax.ShapeDtypeStruct
    outs = [
        sds((width_s, slots), BF16),
        sds((padded, slots), BF16),
        sds((width_s, slots), F32),
        sds((packed_rows, units_s // 128 * 128), BF16),
    ]
    anywhere = pl.BlockSpec(memory_space=pl.ANY)
    return pl.pallas_call(
        dense_kernel,
        out_shape=outs,
        in_specs=[anywhere] * len(big) + [VMEM] * len(small),
        out_specs=[anywhere] * len(outs),
        scratch_shapes=[pltpu.VMEM(a.shape, a.dtype) for a in big]
        + [pltpu.VMEM(a.shape, a.dtype) for a in outs]
        + [
            pltpu.VMEM((inner_pad, slots), BF16),
            pltpu.VMEM((units_s, slots), F32),
            pltpu.VMEM((width_t, slots), BF16),
            pltpu.VMEM((width_t, slots), F32),
            pltpu.SemaphoreType.DMA((len(big),)),
            pltpu.SemaphoreType.DMA((6,)),
        ],
        compiler_params=pltpu.CompilerParams(vmem_limit_bytes=BIG),
    )(*big, *small)


def group_sizes():
    seq = lax.axis_size("seq")
    core = 2 if seq % 2 == 0 else 1
    chain = 4 if seq // core % 4 == 0 else 1
    return {"core": core, "batch": lax.axis_size("batch"), "chain": chain, "outer": seq // core // chain}


class Group:
    def __init__(self, name):
        batch, seq = lax.axis_index("batch"), lax.axis_index("seq")
        sizes = group_sizes()
        self.size = sizes[name]
        if name == "batch":
            self.place = batch
            self.device = lambda j: (j, seq)
        else:
            stride = {"core": 1, "chain": sizes["core"], "outer": sizes["core"] * sizes["chain"]}[name]
            self.place = seq // stride % self.size
            self.device = lambda j: (batch, seq + (j - self.place) * stride)

    def other(self, k):
        return (self.place + k) % self.size


class Chain:
    def __init__(self, names, source, scratch, local=None):
        self.names, self.source, self.local = names, source, local
        self.groups = [Group(n) for n in names]
        count = len(names)
        self.outer = Group("outer")
        self.received, self.sums = scratch[:count], scratch[count : 2 * count]
        self.around, self.whole, self.send, self.arrive = scratch[2 * count :]
        rows = self.whole.shape[0]
        self.rows, self.base, base = [], [], 0
        for g in self.groups:
            self.base.append(base)
            rows //= g.size
            base = base + g.place * rows
            self.rows.append(rows)
        self.mine = base
        self.sem = 0
        self.pending = []

    @staticmethod
    def scratch(names, rows, lanes):
        received, sums, copies = [], [], 0
        total, sizes = rows, group_sizes()
        for size in (sizes[n] for n in names):
            rows = rows // size
            received.append(pltpu.VMEM((max(size - 1, 1), rows, lanes), BF16))
            sums.append(pltpu.VMEM((rows, lanes), BF16))
            copies += 2 * (size - 1)
        copies = max(copies + sizes["outer"] - 1, 1)
        return (
            received
            + sums
            + [
                pltpu.VMEM((max(sizes["outer"] - 1, 1), rows, lanes), BF16),
                pltpu.VMEM((total, lanes), BF16),
                pltpu.SemaphoreType.DMA((copies,)),
                pltpu.SemaphoreType.DMA((copies,)),
            ]
        )

    def copy(self, ends):
        at = self.sem
        self.sem += 1

        def form():
            source, target, device = ends()
            return pltpu.make_async_remote_copy(
                src_ref=source,
                dst_ref=target,
                send_sem=self.send.at[at],
                recv_sem=self.arrive.at[at],
                device_id=device,
                device_id_type=MESH,
            )

        form().start()
        self.pending.append(form)

    def scatter(self, k):
        g, rows = self.groups[k], self.rows[k]
        source = self.source if k == 0 else self.sums[k - 1]

        def ends(step):
            other = g.other(step)
            there = pl.ds(pl.multiple_of(other * rows, 16), rows)
            return source.at[there], self.received[k].at[step - 1], g.device(other)

        for step in range(1, g.size):
            self.copy(partial(ends, step))

    def wait(self):
        for form in self.pending:
            form().wait()
        self.pending = []

    def add(self, k):
        self.wait()
        g, rows = self.groups[k], self.rows[k]
        source = self.source if k == 0 else self.sums[k - 1]
        if k == 0 and self.local is not None:
            total = self.local[...].astype(F32)
        else:
            total = source[pl.ds(pl.multiple_of(g.place * rows, 16), rows), :].astype(F32)
        for step in range(1, g.size):
            total = total + self.received[k][step - 1].astype(F32)
        total = total.astype(BF16)
        if k < len(self.groups) - 1 or self.outer.size > 1:
            self.sums[k][...] = total
        if k == len(self.groups) - 1:
            if self.outer.size > 1:
                total = self.exchange(total)
            self.whole[pl.ds(pl.multiple_of(self.mine, 16), rows), :] = total

    def exchange(self, total):
        g = self.outer

        def ends(step):
            return self.sums[-1], self.around.at[step - 1], g.device(g.other(step))

        for step in range(1, g.size):
            self.copy(partial(ends, step))
        self.wait()
        total = total.astype(F32)
        for step in range(1, g.size):
            total = total + self.around[step - 1].astype(F32)
        return total.astype(BF16)

    def gather(self, k):
        g, rows = self.groups[k], self.rows[k]

        def ends(step):
            here = self.whole.at[pl.ds(pl.multiple_of(self.base[k] + g.place * rows, 16), rows)]
            return here, here, g.device(g.other(step))

        for step in range(1, g.size):
            self.copy(partial(ends, step))

    def advance(self, stage):
        count = len(self.groups)
        if 0 < stage <= count:
            self.add(stage - 1)
        else:
            self.wait()
        if stage < count:
            self.scatter(stage)
        elif stage < 2 * count:
            self.gather(2 * count - 1 - stage)


EARLY = (
    (0, 384, ("core", "batch", "chain")),
    (384, 768, ("core", "batch", "chain")),
    (768, 1152, ("core", "chain", "batch")),
)
LATE = (
    (0, 128, ("core", "batch", "chain")),
    (128, 256, ("core", "batch", "chain")),
    (256, 384, ("core", "chain", "batch")),
)


def back_kernel(
    windows,
    sq_hbm,
    skv_hbm,
    dctx_hbm,
    e_hbm,
    g_hbm,
    pack_hbm,
    xs_hbm,
    dres_hbm,
    wq_hbm,
    wk_hbm,
    wv_hbm,
    rows_ref,
    dx_ref,
    early_ref,
    late_ref,
    sq_ref,
    skv_ref,
    dctx_ref,
    e_ref,
    g_ref,
    half_ref,
    xs_ref,
    dres_ref,
    wq_ref,
    wk_ref,
    wv_ref,
    in_sem,
    block_sem,
    dq_ref,
    dkv_ref,
    give_ref,
    take_ref,
    qkv_ref,
    halo_send,
    halo_arrive,
    out_sem,
    *scratch,
):
    step = pl.program_id(0)
    w = (windows - step) % windows
    slots = windows * WIN
    width_s = xs_ref.shape[0]
    batch, seq = lax.axis_index("batch"), lax.axis_index("seq")
    peers = lax.axis_size("seq")
    chains, used = [], 0
    for source, local, cuts in ((pack_hbm, half_ref, EARLY), (qkv_ref, None, LATE)):
        for first, last, names in cuts:
            size = 2 * len(names) + 4
            mine = local.at[:, first:last] if local is not None else None
            chains.append(Chain(names, source.at[:, first:last], scratch[used : used + size], mine))
            used += size
    soon, late = chains[: len(EARLY)], chains[len(EARLY) :]
    first_seq, last_seq = seq == 0, seq == peers - 1

    def halo(side):
        return pltpu.make_async_remote_copy(
            src_ref=give_ref.at[side],
            dst_ref=take_ref.at[1 - side],
            send_sem=halo_send.at[side],
            recv_sem=halo_arrive.at[1 - side],
            device_id=(batch, seq - 1 + 2 * side),
            device_id_type=MESH,
        )

    half_rows = half_ref.shape[0]
    ends = {
        "half": (pack_hbm.at[pl.ds(pl.multiple_of(seq % group_sizes()["core"] * half_rows, 16), half_rows)], half_ref),
        "sq": (sq_hbm, sq_ref),
        "skv": (skv_hbm, skv_ref),
        "dctx": (dctx_hbm, dctx_ref),
        "xs": (xs_hbm, xs_ref),
        "dres": (dres_hbm, dres_ref),
        "wq": (wq_hbm, wq_ref),
        "wk": (wk_hbm, wk_ref),
        "wv": (wv_hbm, wv_ref),
    }
    load = lambda name: pltpu.make_async_copy(*ends[name], in_sem.at[list(ends).index(name)])

    def blocks(number):
        slot, window = number % 2, (windows - number) % windows
        return [
            pltpu.make_async_copy(source.at[window], target.at[slot], block_sem.at[k, slot])
            for k, (source, target) in enumerate(((e_hbm, e_ref), (g_hbm, g_ref)))
        ]

    @pl.when(step == 0)
    def _():
        load("half").start()
        dkv_ref[...] = jnp.zeros_like(dkv_ref)
        take_ref[...] = jnp.zeros_like(take_ref)
        qkv_ref[...] = jnp.zeros_like(qkv_ref)
        barrier = pltpu.get_barrier_semaphore()
        count = 0
        for g in (Group(n) for n in ("core", "batch", "chain", "outer")):
            for k in range(1, g.size):
                pl.semaphore_signal(barrier, inc=1, device_id=g.device(g.other(k)), device_id_type=MESH)
                count += 1

        for move in (1, peers - 1):
            pl.semaphore_signal(
                barrier, inc=1, device_id=(batch, (seq + move) % peers), device_id_type=MESH
            )
        pl.semaphore_wait(barrier, count + 2)

        for c in soon:
            c.advance(0)
        for c in blocks(0):
            c.start()
        for name in ("sq", "skv", "dctx"):
            load(name).start()
        for c in blocks(1):
            c.start()
        for name in ("xs", "dres", "wq", "wk", "wv"):
            load(name).start()
        for name in ("sq", "skv", "dctx", "half"):
            load(name).wait()

    for c in blocks(step):
        c.wait()
    slot = step % 2
    at = pl.multiple_of(w * WIN, WIN)
    left = pl.ds(at, WIN)
    own = pl.ds(pl.multiple_of(at + WIN, WIN), WIN)
    right = pl.ds(pl.multiple_of(at + 2 * WIN, WIN), WIN)
    early_row, late_row = rows_ref[0:1, left], rows_ref[1:2, left]
    early_low, late_low = early_row.astype(BF16), late_row.astype(BF16)

    def one_head(head):
        rows = pl.ds(pl.multiple_of(head * PAD, PAD), PAD)
        query, grad = sq_ref[rows, left], dctx_ref[rows, left]
        stacked = lambda a: jnp.concatenate([a * early_low, a * late_low], axis=0)
        query_fold, grad_fold = stacked(query), stacked(grad)
        beside = lambda k: jnp.concatenate([skv_ref[k, rows, left], skv_ref[k, rows, right]], axis=0)
        keys_fold, values_fold = beside(0), beside(1)
        keys, values = skv_ref[0, rows, own], skv_ref[1, rows, own]
        e_own, e_side = e_ref[slot, head, :WIN, :], e_ref[slot, head, WIN:, :]
        d_own = (e_own.astype(F32) * (tn(values, grad) + g_ref[slot, head, :WIN, :].astype(F32))).astype(BF16)
        d_side = (
            e_side.astype(F32) * (tn(values_fold, grad_fold) + g_ref[slot, head, WIN:, :].astype(F32))
        ).astype(BF16)
        side = nn(keys_fold, d_side)
        d_query = nn(keys, d_own) + early_row * side[:PAD] + late_row * side[PAD:]
        dq_ref[rows, left] = (d_query * HD_S**-0.5).astype(BF16)
        for k, (a, a_fold, b, b_fold, scale) in enumerate(
            ((query, query_fold, d_own, d_side, 1.0 / LOG2E), (grad, grad_fold, e_own, e_side, None))
        ):
            fix = (lambda v: v * scale) if scale else (lambda v: v)
            side = fix(nt(a_fold, b_fold))
            dkv_ref[k, rows, own] += fix(nt(a, b))
            dkv_ref[k, rows, left] += side[:PAD]
            dkv_ref[k, rows, right] += side[PAD:]

    def body(pair, carry):
        one_head(2 * pair)
        one_head(2 * pair + 1)
        return carry

    def send_halo():
        for side, lanes in ((0, slice(0, WIN)), (1, slice(WIN + slots, 2 * WIN + slots))):
            give_ref[side] = dkv_ref[:, :, lanes].astype(BF16)

        @pl.when(jnp.logical_not(first_seq))
        def _():
            halo(0).start()

        @pl.when(jnp.logical_not(last_seq))
        def _():
            halo(1).start()

    def advance(which, stage):
        for c in which:
            c.advance(stage)

    half = PAIRS // 2
    plan = {
        (0, 0): [partial(advance, soon, 1)],
        (1, 1): [send_halo],
        (2, 0): [partial(advance, soon, 2)],
        (3, 0): [partial(advance, soon, 3)],
    }
    for part in range(2):
        lax.fori_loop(part * half, (part + 1) * half, body, 0)
        for k in range(windows):
            for action in plan.get((k, part), []):
                pl.when(step == k)(action)

    @pl.when(step < windows - 2)
    def _():
        for c in blocks(step + 2):
            c.start()

    @pl.when(step == windows - 1)
    def _():
        for name in ("xs", "dres", "wq", "wk", "wv"):
            load(name).wait()

        @pl.when(jnp.logical_not(first_seq))
        def _():
            halo(0).wait_send()
            halo(1).wait_recv()

        @pl.when(jnp.logical_not(last_seq))
        def _():
            halo(1).wait_send()
            halo(0).wait_recv()

        advance(soon, 4)
        spot = pad_heads()
        plains = []
        for k in range(3):
            if k == 0:
                grad = dq_ref[...]
            else:
                mine = dkv_ref[k - 1, :, WIN : WIN + slots]
                first = mine[:, :WIN] + take_ref[0, k - 1].astype(F32)
                last = mine[:, slots - WIN :] + take_ref[1, k - 1].astype(F32)
                grad = jnp.concatenate([first, mine[:, WIN : slots - WIN], last], axis=1).astype(BF16)
            plain = tn(spot, grad).astype(BF16)
            plains.append(plain)
            qkv_ref[k * BLOCK : k * BLOCK + width_s, :width_s] = nt(xs_ref[...], plain).astype(BF16)
        advance(late, 0)
        total = dres_ref[...]
        for w_ref, plain in zip((wq_ref, wk_ref, wv_ref), plains):
            total = total + nn(w_ref[...], plain)
        dx_ref[...] = total.astype(BF16)
        advance(late, 1)
        advance(late, 2)
        advance(soon, 5)
        advance(late, 3)
        advance(soon, 6)

        def put(group, cuts, target, first_sem):
            made = []
            for n, (c, (first, last, _)) in enumerate(zip(group, cuts)):
                made.append(pltpu.make_async_copy(c.whole, target.at[:, first:last], out_sem.at[first_sem + n]))
                made[-1].start()
            return made

        copies = put(soon, EARLY, early_ref, 0)
        advance(late, 4)
        advance(late, 5)
        advance(late, 6)
        copies += put(late, LATE, late_ref, len(EARLY))
        for c in copies:
            c.wait()


def back(sq, skv, dctx, e, g, rows, pack, xs, dres, wq, wk, wv):
    padded, slots = sq.shape
    windows = slots // WIN
    width_s = xs.shape[0]
    packed_rows = pack.shape[0]
    anywhere = pl.BlockSpec(memory_space=pl.ANY)
    held = lambda a: pltpu.VMEM(a.shape, a.dtype)
    scratch = [held(sq), held(skv), held(dctx)]
    scratch += [pltpu.VMEM((2,) + a.shape[1:], a.dtype) for a in (e, g)]
    scratch += [pltpu.VMEM((packed_rows // group_sizes()["core"], pack.shape[1]), BF16)]
    scratch += [held(a) for a in (xs, dres, wq, wk, wv)]
    scratch += [
        pltpu.SemaphoreType.DMA((9,)),
        pltpu.SemaphoreType.DMA((2, 2)),
        pltpu.VMEM((padded, slots), BF16),
        pltpu.VMEM((2, padded, slots + 2 * WIN), F32),
        pltpu.VMEM((2, 2, padded, WIN), BF16),
        pltpu.VMEM((2, 2, padded, WIN), BF16),
        pltpu.VMEM((packed_rows, QKV_LANES), BF16),
        pltpu.SemaphoreType.DMA((2,)),
        pltpu.SemaphoreType.DMA((2,)),
        pltpu.SemaphoreType.DMA((len(EARLY) + len(LATE),)),
    ]
    for first, last, names in EARLY + LATE:
        scratch += Chain.scratch(names, packed_rows, last - first)
    return pl.pallas_call(
        partial(back_kernel, windows),
        grid=(windows,),
        out_shape=[
            jax.ShapeDtypeStruct((width_s, slots), BF16),
            jax.ShapeDtypeStruct(pack.shape, BF16),
            jax.ShapeDtypeStruct((packed_rows, QKV_LANES), BF16),
        ],
        in_specs=[anywhere] * 11 + [VMEM],
        out_specs=[pl.BlockSpec((width_s, slots), lambda i: (0, 0)), anywhere, anywhere],
        scratch_shapes=scratch,
        compiler_params=pltpu.CompilerParams(
            vmem_limit_bytes=BIG,
            dimension_semantics=("arbitrary",),
            collective_id=0,
            has_side_effects=True,
        ),
    )(sq, skv, dctx, e, g, pack, xs, dres, wq, wk, wv, rows)


def unpack_kernel(
    every,
    width_t,
    early_hbm,
    late_hbm,
    dx_in_ref,
    dx_ref,
    loss_ref,
    gq_hbm,
    gk_hbm,
    gv_hbm,
    gwo_hbm,
    ginner_hbm,
    gouter_hbm,
    ghid_hbm,
    bouter_ref,
    binner_ref,
    gain_one_ref,
    shift_one_ref,
    gain_two_ref,
    shift_two_ref,
    early_ref,
    late_ref,
    gq_ref,
    gk_ref,
    gv_ref,
    gwo_ref,
    ginner_ref,
    gouter_ref,
    ghid_ref,
    in_sem,
    out_sem,
):
    width_s = gq_ref.shape[0]
    units = ginner_ref.shape[1]
    scale = 1.0 / every
    full = lambda v: v.astype(F32) * scale
    main = units // 128 * 128
    rest = units - main
    cuts = (slice(3 * BLOCK, 3 * BLOCK + STRIP),) + tuple(slice(k * BLOCK, (k + 1) * BLOCK) for k in range(3))
    loads = [pltpu.make_async_copy(early_hbm.at[c], early_ref.at[c], in_sem.at[k]) for k, c in enumerate(cuts)]
    loads.append(pltpu.make_async_copy(late_hbm, late_ref, in_sem.at[4]))
    for c in loads:
        c.start()
    stores = []

    def store(source, target):
        stores.append(pltpu.make_async_copy(source, target, out_sem.at[len(stores)]))
        stores[-1].start()

    dx_ref[...] = dx_in_ref[...]
    loads[0].wait()
    strip = full(early_ref[3 * BLOCK : 3 * BLOCK + STRIP, :])
    turned = lambda at, n: jnp.transpose(strip[:, at : at + n])
    for k, ref in enumerate((gain_one_ref, shift_one_ref, gain_two_ref, shift_two_ref)):
        ref[...] = strip[rest + k, :width_s]
    bouter_ref[...] = strip[rest, STRIP_OUTER : STRIP_OUTER + width_s]
    loads[1].wait()
    gouter_ref[:, :main] = full(early_ref[:width_s, :main])
    gouter_ref[:, main:] = turned(STRIP_OUTER, STRIP_BIAS - STRIP_OUTER)[:width_s, :rest]
    store(gouter_ref, gouter_hbm)
    loads[2].wait()
    ginner_ref[:, :main] = full(early_ref[BLOCK : BLOCK + width_s, :main])
    ginner_ref[:, main:] = turned(0, STRIP_OUTER)[:width_s, :rest]
    store(ginner_ref, ginner_hbm)
    first = full(early_ref[BLOCK + width_s : BLOCK + width_s + 8, :main])[0:1]
    binner_ref[...] = jnp.concatenate([first, turned(STRIP_BIAS, 128)[0:1, :rest]], axis=1)[0]
    loads[3].wait()
    third = slice(2 * BLOCK, 2 * BLOCK + width_s)
    ghid_ref[...] = full(early_ref[third, :width_t])
    store(ghid_ref, ghid_hbm)
    gwo_ref[...] = full(early_ref[third, width_t : width_t + width_s])
    store(gwo_ref, gwo_hbm)
    loads[4].wait()
    for k, (ref, hbm) in enumerate(((gq_ref, gq_hbm), (gk_ref, gk_hbm), (gv_ref, gv_hbm))):
        ref[...] = full(late_ref[k * BLOCK : k * BLOCK + width_s, :width_s])
        store(ref, hbm)
    part = early_ref[2 * BLOCK + width_s : 2 * BLOCK + width_s + 8, :128].astype(F32)
    total = jnp.sum(jnp.sum(part, axis=0, keepdims=True), axis=1, keepdims=True)
    loss_ref[...] = total
    for c in stores:
        c.wait()


def unpack(every, width_t, units, early, late, dx):
    width_s = dx.shape[0]
    sds = lambda *shape: jax.ShapeDtypeStruct(shape, F32)
    square = sds(width_s, width_s)
    large = [square, square, square, square, sds(width_s, units), sds(width_s, units), sds(width_s, width_t)]
    vectors = [sds(width_s), sds(units)] + [sds(width_s)] * 4
    anywhere = pl.BlockSpec(memory_space=pl.ANY)
    return pl.pallas_call(
        partial(unpack_kernel, every, width_t),
        out_shape=[jax.ShapeDtypeStruct(dx.shape, BF16), sds(1, 1)] + large + vectors,
        in_specs=[anywhere, anywhere, VMEM],
        out_specs=[VMEM] * 2 + [anywhere] * len(large) + [VMEM] * len(vectors),
        scratch_shapes=[pltpu.VMEM(early.shape, BF16), pltpu.VMEM(late.shape, BF16)]
        + [pltpu.VMEM(a.shape, F32) for a in large]
        + [pltpu.SemaphoreType.DMA((5,)), pltpu.SemaphoreType.DMA((len(large),))],
        compiler_params=pltpu.CompilerParams(vmem_limit_bytes=BIG),
    )(early, late, dx)


def local(
    inputs,
    teacher_input,
    filled_slot_mask,
    seg_lengths,
    query_weight,
    key_weight,
    value_weight,
    w_output,
    gain_one,
    shift_one,
    w_inner,
    b_inner,
    w_outer,
    b_outer,
    gain_two,
    shift_two,
    w_hidden,
    teacher_query_weight,
    teacher_key_weight,
    teacher_value_weight,
    teacher_output,
    teacher_gain_one,
    teacher_shift_one,
    teacher_inner,
    teacher_outer,
    teacher_gain_two,
    teacher_shift_two,
):
    xs = jnp.transpose(inputs[0])
    xt = teacher_input[0]
    slots, width_t = xt.shape
    width_s = xs.shape[0]
    stats, loss_rows, rows, tctx, sctx, sq, skv, e, g = attend(
        filled_slot_mask,
        seg_lengths,
        xt,
        xs,
        teacher_query_weight,
        teacher_key_weight,
        teacher_value_weight,
        query_weight,
        key_weight,
        value_weight,
    )
    devices = lax.axis_size("seq") * lax.axis_size("batch")
    sizes = group_sizes()
    unit = 16 * sizes["core"] * sizes["batch"] * sizes["chain"]
    packed_rows = -(-3 * BLOCK // unit) * unit
    out, dctx, dres, pack = dense(
        packed_rows,
        (
            xt,
            tctx,
            teacher_output,
            xs,
            sctx,
            teacher_inner,
            teacher_outer,
            w_output,
            w_inner,
            jnp.transpose(w_outer),
            w_hidden,
        ),
        (stats, rows, loss_rows)
        + (
            teacher_gain_one,
            teacher_shift_one,
            teacher_gain_two,
            teacher_shift_two,
            gain_one,
            shift_one,
            b_outer,
            gain_two,
            shift_two,
            b_inner,
        ),
    )
    dx, early, late = back(sq, skv, dctx, e, g, rows, pack, xs, dres, query_weight, key_weight, value_weight)
    dx, loss, gq, gk, gv, gwo, ginner, gouter, ghid, *vectors = unpack(
        slots * devices, width_t, w_inner.shape[1], early, late, dx
    )
    g_b_outer, g_b_inner, g_gain_one, g_shift_one, g_gain_two, g_shift_two = vectors
    return (
        jnp.transpose(out)[None],
        jnp.transpose(dx)[None],
        loss[0, 0] / (slots * devices * width_t),
        gq,
        gk,
        gv,
        gwo,
        g_gain_one,
        g_shift_one,
        ginner,
        g_b_inner,
        jnp.transpose(gouter),
        g_b_outer,
        g_gain_two,
        g_shift_two,
        ghid,
    )


def solution(mesh):
    row_split = P("batch", "seq", None)
    return jax.shard_map(
        local,
        mesh=mesh,
        in_specs=(row_split, row_split, P("batch", None), P("batch", None)) + (P(),) * 23,
        out_specs=(row_split, row_split) + (P(),) * 14,
        check_vma=False,
    )
```

```python
from functools import partial

import jax
import jax.numpy as jnp
from jax import lax
from jax.experimental import pallas as pl
from jax.experimental.pallas import tpu as pltpu
from jax.sharding import PartitionSpec as P

HEADS = 12
HD_S = 26
HD_T = 64
WIN = 256
PAD = 32
SLOT_ONE = 26
PAIRS = HEADS // 2
CHUNK = 64
TAIL = 16
SLOTS = 4
BLOCK = 320
STRIP = 64
STRIP_OUTER = 384
STRIP_BIAS = 768
QKV_LANES = 384
MESH = pl.DeviceIdType.MESH
EPSILON = 1e-05
NEGATIVE = -1e30
LOG2E = 1.4426950408889634
F32 = jnp.float32
BF16 = jnp.bfloat16
VMEM = pl.BlockSpec(memory_space=pltpu.VMEM)
BIG = 60 << 20


def mm(left, right, dims):
    return lax.dot_general(left, right, ((dims[:1], dims[1:]), ((), ())), preferred_element_type=F32)


def nn(left, right):
    return mm(left, right, (1, 0))


def tn(left, right):
    return mm(left, right, (0, 0))


def nt(left, right):
    return mm(left, right, (1, 1))


def tt(left, right):
    return mm(left, right, (0, 1))


def pad_heads():
    row = lax.broadcasted_iota(jnp.int32, (HEADS * PAD, HEADS * HD_S), 0)
    col = lax.broadcasted_iota(jnp.int32, (HEADS * PAD, HEADS * HD_S), 1)
    spot = jnp.zeros((HEADS * PAD, HEADS * HD_S), F32)
    for head in range(HEADS):
        here = (row - head * PAD == col - head * HD_S) & (col >= head * HD_S) & (col < (head + 1) * HD_S)
        spot = jnp.where(here, 1.0, spot)
    return spot.astype(BF16)


def window_rows(mask_ref, lengths_ref, seq_index, windows, row_windows):
    lengths = lengths_ref[...].astype(F32)
    order = lax.broadcasted_iota(jnp.int32, lengths.shape, 1)
    lane = lax.broadcasted_iota(jnp.int32, (1, WIN), 1).astype(F32)
    out = []
    for j in range(windows + 2):
        number = seq_index * windows + (j - 1)
        inside = (number >= 0) & (number < row_windows)
        safe = jnp.clip(number, 0, row_windows - 1)
        start = jnp.sum(jnp.where(order < safe, lengths, 0.0), axis=1, keepdims=True)
        offset = start - (safe * WIN).astype(F32)
        late = (lane >= offset).astype(F32)
        filled = mask_ref[:, pl.ds(pl.multiple_of(safe * WIN, WIN), WIN)]
        filled = jnp.where(inside, filled.astype(F32), 0.0)
        out.append((late, filled))
    return out


def stack_rows(*rows):
    n = rows[0].shape[1]
    index = lax.broadcasted_iota(jnp.int32, (8, n), 0)
    block = jnp.zeros((8, n), F32)
    for k, row in enumerate(rows):
        block = jnp.where(index == k, row, block)
    return block.astype(BF16)


def attend_kernel(
    windows,
    row_windows,
    mask_ref,
    lengths_ref,
    xt_hbm,
    xs_ref,
    wtq_hbm,
    wtk_hbm,
    wtv_hbm,
    wq_ref,
    wk_ref,
    wv_ref,
    stats_ref,
    loss_ref,
    rows_ref,
    tctx_hbm,
    sctx_hbm,
    sq_hbm,
    skv_hbm,
    saved_e_hbm,
    saved_g_hbm,
    x_ref,
    xs_side_ref,
    wt_ref,
    bias_ref,
    wst_ref,
    tq_ref,
    tk_ref,
    tv_ref,
    sq_ref,
    skv_ref,
    tctx_ref,
    sctx_ref,
    e_ref,
    g_ref,
    work_ref,
    low_ref,
    in_sem,
    halo_send,
    halo_arrive,
    kv_sem,
    out_sem,
):
    slots = windows * WIN
    batch, seq = lax.axis_index("batch"), lax.axis_index("seq")
    peers = lax.axis_size("seq")
    has_left, has_right = seq > 0, seq < peers - 1
    width_t = x_ref.shape[1]
    extended = slots + 2 * WIN

    barrier = pltpu.get_barrier_semaphore()
    for move in (1, peers - 1):
        pl.semaphore_signal(barrier, inc=1, device_id=(batch, (seq + move) % peers), device_id_type=MESH)
    loads = [pltpu.make_async_copy(xt_hbm, x_ref.at[pl.ds(WIN, slots)], in_sem.at[0])]
    for k, w_hbm in enumerate((wtq_hbm, wtk_hbm, wtv_hbm)):
        loads.append(pltpu.make_async_copy(w_hbm, wt_ref.at[k], in_sem.at[1 + k]))
    for c in loads:
        c.start()
    pl.semaphore_wait(barrier, 2)

    def halo(side):
        device = (batch, seq - 1 + 2 * side)
        first = pl.multiple_of(side * (slots - WIN), WIN)
        return [
            pltpu.make_async_remote_copy(
                src_ref=xt_hbm.at[pl.ds(first, WIN)],
                dst_ref=x_ref.at[pl.ds(pl.multiple_of((1 - side) * (WIN + slots), WIN), WIN)],
                send_sem=halo_send.at[0, side],
                recv_sem=halo_arrive.at[0, 1 - side],
                device_id=device,
                device_id_type=MESH,
            ),
            pltpu.make_async_remote_copy(
                src_ref=xs_ref.at[:, pl.ds(first, WIN)],
                dst_ref=xs_side_ref.at[1 - side],
                send_sem=halo_send.at[1, side],
                recv_sem=halo_arrive.at[1, 1 - side],
                device_id=device,
                device_id_type=MESH,
            ),
        ]

    for side, present in ((0, has_left), (1, has_right)):

        @pl.when(present)
        def _():
            for c in halo(side):
                c.start()

        @pl.when(jnp.logical_not(present))
        def _():
            x_ref[side * (WIN + slots) : side * (WIN + slots) + WIN, :] = jnp.zeros((WIN, width_t), BF16)
            xs_side_ref[side] = jnp.zeros(xs_side_ref.shape[1:], BF16)

    info = window_rows(mask_ref, lengths_ref, seq, windows, row_windows)
    eye = lax.broadcasted_iota(jnp.int32, (WIN, WIN), 0) == lax.broadcasted_iota(jnp.int32, (WIN, WIN), 1)
    rows_ref[...] = jnp.zeros_like(rows_ref)
    for w in range(windows):
        late, filled = info[w + 1]
        late_l, filled_l = info[w]
        late_r, filled_r = info[w + 2]
        early = 1.0 - late
        here = slice(w * WIN, (w + 1) * WIN)
        rows_ref[0:1, here] = early
        rows_ref[1:2, here] = late
        rows_ref[2:3, here] = filled
        query = stack_rows(early, late)
        own = tn(stack_rows(NEGATIVE * (1.0 - early * filled), NEGATIVE * (1.0 - late * filled)), query)
        bias_ref[w, :WIN, :] = jnp.where(eye, 0.0, own)
        bias_ref[w, WIN:, :] = tn(
            stack_rows(
                NEGATIVE * (1.0 - late_l * filled_l), NEGATIVE * (1.0 - (1.0 - late_r) * filled_r)
            ),
            query,
        )
    loss_ref[...] = jnp.zeros_like(loss_ref)
    stats_ref[...] = jnp.zeros_like(stats_ref)
    spot = pad_heads()
    padded = HEADS * PAD
    row = lax.broadcasted_iota(jnp.int32, (padded, 1), 0) % PAD
    ones = (row >= SLOT_ONE) & (row < SLOT_ONE + 3)

    xs = xs_ref[...]
    for k, w_ref in enumerate((wq_ref, wk_ref, wv_ref)):
        wst_ref[k] = nt(spot, w_ref[...]).astype(BF16)
        made = nn(wst_ref[k], xs)
        if k == 0:
            sq_ref[...] = (made * (LOG2E * HD_S**-0.5)).astype(BF16)
        else:
            if k == 2:
                made = jnp.where(ones, 1.0, made)
            skv_ref[k - 1, :, WIN : WIN + slots] = made.astype(BF16)
    tail = (lax.broadcasted_iota(jnp.int32, (TAIL, extended), 0) == 0).astype(BF16)
    for head in range(HEADS):
        tv_ref[head * (HD_T + TAIL) + HD_T : (head + 1) * (HD_T + TAIL), :] = tail

    def put_values(made, first_head, lanes):
        for j in range(made.shape[0] // HD_T):
            at = pl.multiple_of((first_head + j) * (HD_T + TAIL), TAIL)
            tv_ref[pl.ds(at, HD_T), lanes] = made[j * HD_T : (j + 1) * HD_T]

    part = width_t // 2
    loads[0].wait()
    for k in range(3):
        loads[1 + k].wait()

        def project(half, carry, k=k):
            rows = pl.ds(pl.multiple_of(half * part, 128), part)
            made = tt(wt_ref[k, :, rows], x_ref[WIN : WIN + slots, :])
            if k == 0:
                tq_ref[rows, :] = (made * (LOG2E * HD_T**-0.5)).astype(BF16)
            elif k == 1:
                tk_ref[rows, WIN : WIN + slots] = made.astype(BF16)
            else:
                put_values(made.astype(BF16), half * (HEADS // 2), slice(WIN, WIN + slots))
            return carry

        lax.fori_loop(0, 2, project, 0)

    def project_side(side, carry):
        @pl.when(jnp.where(side == 0, has_left, has_right))
        def _():
            for sent, landed in zip(halo(side), halo(1 - side)):
                sent.wait_send()
                landed.wait_recv()

        lanes = pl.ds(pl.multiple_of(side * (WIN + slots), WIN), WIN)
        for k in (1, 2):
            made = tt(wt_ref[k], x_ref[lanes, :]).astype(BF16)
            if k == 1:
                tk_ref[:, lanes] = made
            else:
                put_values(made, 0, lanes)
            made = nn(wst_ref[k], xs_side_ref[side])
            if k == 2:
                made = jnp.where(ones, 1.0, made)
            skv_ref[k - 1, :, lanes] = made.astype(BF16)
        return carry

    lax.fori_loop(0, 2, project_side, 0)
    finals = [
        pltpu.make_async_copy(sq_ref, sq_hbm, kv_sem.at[0]),
        pltpu.make_async_copy(skv_ref, skv_hbm, kv_sem.at[1]),
    ]
    for c in finals:
        c.start()

    def stores(pair, which):
        slot = pair % 2
        t_rows = pl.ds(pl.multiple_of(pair * 2 * HD_T, 2 * HD_T), 2 * HD_T)
        s_rows = pl.ds(pl.multiple_of(pair * 2 * PAD, 2 * PAD), 2 * PAD)
        heads = pl.ds(pair * 2, 2)
        ends = (
            (e_ref.at[slot], saved_e_hbm.at[:, heads]),
            (g_ref.at[slot], saved_g_hbm.at[:, heads]),
            (tctx_ref.at[t_rows], tctx_hbm.at[t_rows]),
            (sctx_ref.at[s_rows], sctx_hbm.at[s_rows]),
        )
        return [pltpu.make_async_copy(*ends[k], out_sem.at[k, pair]) for k in which]

    def one_pair(pair, carry):
        @pl.when(pair >= 2)
        def _():
            for c in stores(pair - 2, (0, 1)):
                c.wait()

        attend_pair(pair)
        for c in stores(pair, range(4)):
            c.start()
        return carry

    def attend_pair(pair):
        e_out, g_out = e_ref.at[pair % 2], g_ref.at[pair % 2]
        def rows_of(w):
            left = slice(w * WIN, (w + 1) * WIN)
            own = slice((w + 1) * WIN, (w + 2) * WIN)
            right = slice((w + 2) * WIN, (w + 3) * WIN)
            return left, own, right, rows_ref[0:1, left], rows_ref[1:2, left], rows_ref[2:3, left]

        def first_pass(w, q_ref, k_ref, rows, work_ref):
            left, own, right, early, late, _ = rows_of(w)
            query = q_ref[rows, left]
            query_fold = jnp.concatenate([query * early.astype(BF16), query * late.astype(BF16)], axis=0)
            keys = k_ref[rows, own]
            keys_fold = jnp.concatenate([k_ref[rows, left], k_ref[rows, right]], axis=0)
            top = None
            for part, (a, b) in enumerate(((keys, query), (keys_fold, query_fold))):
                raw = tn(a, b)
                for c in range(0, WIN, CHUNK):
                    block = raw[c : c + CHUNK] + bias_ref[w, part * WIN + c : part * WIN + c + CHUNK, :]
                    work_ref[part * WIN + c : part * WIN + c + CHUNK, :] = block
                    for r in range(0, CHUNK, 8):
                        piece = block[r : r + 8]
                        top = piece if top is None else jnp.maximum(top, piece)
            return jnp.max(top, axis=0, keepdims=True)

        def second_pass(work_ref, top, low_ref):
            for c in range(0, 2 * WIN, CHUNK):
                e = jnp.exp2(work_ref[c : c + CHUNK, :] - top)
                work_ref[c : c + CHUNK, :] = e
                low_ref[c : c + CHUNK, :] = e.astype(BF16)

        def mix(w, v_ref, rows, low_ref, head_width):
            left, own, right, early, late, _ = rows_of(w)
            values = v_ref[rows, own]
            values_fold = jnp.concatenate([v_ref[rows, left], v_ref[rows, right]], axis=0)
            mixed = nn(values, low_ref[:WIN, :])
            side = nn(values_fold, low_ref[WIN:, :])
            n = values.shape[0]
            mixed = mixed + early * side[:n] + late * side[n:]
            inverse = 1.0 / mixed[head_width : head_width + 1]
            return mixed[: -TAIL if head_width == HD_T else n] * inverse, inverse

        units = [(w, h) for w in range(windows) for h in range(2)]
        state = {}

        def refs(u):
            w, h = units[u]
            head = 2 * pair + h
            t_rows = pl.ds(pl.multiple_of(head * HD_T, HD_T), HD_T)
            s_rows = pl.ds(pl.multiple_of(head * PAD, PAD), PAD)
            v_rows = pl.ds(pl.multiple_of(head * (HD_T + TAIL), TAIL), HD_T + TAIL)
            slot = u % SLOTS
            return w, h, t_rows, s_rows, v_rows, work_ref.at[2 * slot], work_ref.at[2 * slot + 1], low_ref.at[slot]

        def score_stage(u):
            w, h, t_rows, s_rows, _, work_t, work_s, _ = refs(u)
            state[u] = [
                first_pass(w, tq_ref, tk_ref, t_rows, work_t),
                first_pass(w, sq_ref, skv_ref.at[0], s_rows, work_s),
            ]

        def power_stage(u):
            w, h, _, _, _, work_t, work_s, low_t = refs(u)
            second_pass(work_t, state[u][0], low_t)
            second_pass(work_s, state[u][1], e_out.at[w, h])

        def mix_stage(u):
            w, h, t_rows, s_rows, v_rows, _, _, low_t = refs(u)
            left = rows_of(w)[0]
            t_mixed, t_inv = mix(w, tv_ref, v_rows, low_t, HD_T)
            s_mixed, s_inv = mix(w, skv_ref.at[1], s_rows, e_out.at[w, h], SLOT_ONE)
            tctx_ref[t_rows, left] = t_mixed.astype(BF16)
            sctx_ref[s_rows, left] = s_mixed
            state[u] = [t_inv, s_inv]

        def gap_stage(u):
            w, h, _, _, _, work_t, work_s, _ = refs(u)
            left, _, _, _, _, filled = rows_of(w)
            t_inv, s_inv = state.pop(u)
            width = 2.0 * HEADS * HD_T
            scale_s = (width * filled) * s_inv * s_inv
            scale_t = (width * filled) * s_inv * t_inv
            square = jnp.zeros((8, WIN), F32)
            cross = jnp.zeros((8, WIN), F32)
            for c in range(0, 2 * WIN, CHUNK):
                s = work_s[c : c + CHUNK, :]
                gap = s * scale_s - work_t[c : c + CHUNK, :] * scale_t
                g_out[w, h, c : c + CHUNK, :] = gap.astype(BF16)
                for r in range(0, CHUNK, 8):
                    piece = gap[r : r + 8]
                    square += piece * piece
                    cross += piece * s[r : r + 8]
            square = jnp.sum(square, axis=0, keepdims=True)
            cross = jnp.sum(cross, axis=0, keepdims=True)
            back = 1.0 / (s_inv * width)
            stats_ref[pair, h : h + 1, left] = s_inv
            stats_ref[pair, 2 + h : 3 + h, left] = cross
            loss_ref[0:1, left] += square * back * back

        last = len(units)
        for u in range(last + 2):
            if u < last:
                score_stage(u)
            if 0 <= u - 1 < last:
                power_stage(u - 1)
            if 0 <= u - 2 < last:
                mix_stage(u - 2)
                gap_stage(u - 2)


    lax.fori_loop(0, PAIRS, one_pair, 0)
    for pair in range(PAIRS):
        for c in stores(pair, range(0 if pair >= PAIRS - 2 else 2, 4)):
            c.wait()
    for c in finals:
        c.wait()


def attend(mask, lengths, xt, xs, wtq, wtk, wtv, wq, wk, wv):
    slots, width_t = xt.shape
    width_s = xs.shape[0]
    windows = slots // WIN
    row_windows = mask.shape[1] // WIN
    padded = HEADS * PAD
    extended = slots + 2 * WIN
    sds = jax.ShapeDtypeStruct
    anywhere = pl.BlockSpec(memory_space=pl.ANY)
    saved = (windows, HEADS, 2 * WIN, WIN)
    return pl.pallas_call(
        partial(attend_kernel, windows, row_windows),
        out_shape=(
            sds((PAIRS, 8, slots), F32),
            sds((8, slots), F32),
            sds((8, slots), F32),
            sds((width_t, slots), BF16),
            sds((padded, slots), F32),
            sds((padded, slots), BF16),
            sds((2, padded, extended), BF16),
            sds(saved, BF16),
            sds(saved, BF16),
        ),
        in_specs=[VMEM, VMEM, anywhere, VMEM] + [anywhere] * 3 + [VMEM] * 3,
        out_specs=[VMEM] * 3 + [anywhere] * 6,
        scratch_shapes=[
            pltpu.VMEM((extended, width_t), BF16),
            pltpu.VMEM((2, width_s, WIN), BF16),
            pltpu.VMEM((3, width_t, width_t), BF16),
            pltpu.VMEM((windows, 2 * WIN, WIN), F32),
            pltpu.VMEM((3, padded, width_s), BF16),
            pltpu.VMEM((width_t, slots), BF16),
            pltpu.VMEM((width_t, extended), BF16),
            pltpu.VMEM((HEADS * (HD_T + TAIL), extended), BF16),
            pltpu.VMEM((padded, slots), BF16),
            pltpu.VMEM((2, padded, extended), BF16),
            pltpu.VMEM((width_t, slots), BF16),
            pltpu.VMEM((padded, slots), F32),
            pltpu.VMEM((2, windows, 2, 2 * WIN, WIN), BF16),
            pltpu.VMEM((2, windows, 2, 2 * WIN, WIN), BF16),
            pltpu.VMEM((2 * SLOTS, 2 * WIN, WIN), F32),
            pltpu.VMEM((SLOTS, 2 * WIN, WIN), BF16),
            pltpu.SemaphoreType.DMA((4,)),
            pltpu.SemaphoreType.DMA((2, 2)),
            pltpu.SemaphoreType.DMA((2, 2)),
            pltpu.SemaphoreType.DMA((2,)),
            pltpu.SemaphoreType.DMA((4, PAIRS)),
        ],
        compiler_params=pltpu.CompilerParams(
            vmem_limit_bytes=BIG, collective_id=1, has_side_effects=True
        ),
    )(mask, lengths, xt, xs, wtq, wtk, wtv, wq, wk, wv)


def normalize(values, gain, shift):
    n = values.shape[0]
    center = values - jnp.sum(values, axis=0, keepdims=True) * (1.0 / n)
    rscale = lax.rsqrt(jnp.sum(center * center, axis=0, keepdims=True) * (1.0 / n) + EPSILON)
    unit = center * rscale
    return unit * gain + shift, unit, rscale


def normalize_back(grad, unit, rscale, gain):
    n = grad.shape[0]
    scaled = grad * gain
    first = jnp.sum(scaled, axis=0, keepdims=True) * (1.0 / n)
    second = jnp.sum(scaled * unit, axis=0, keepdims=True) * (1.0 / n)
    return rscale * (scaled - first - unit * second)


def fold_lanes(values):
    total = values[:, :128]
    for at in range(128, values.shape[1], 128):
        total = total + values[:, at : at + 128]
    return total


ROOT_HALF = 0.7071067811865476
ROOT_PI = 0.3989422804014327


DENSE_IN = ("xt", "tctx", "two", "xs", "sctx", "tin", "tout", "wo", "w1", "w2", "wh")


def dense_kernel(
    xt_hbm,
    tctx_hbm,
    two_hbm,
    xs_hbm,
    sctx_hbm,
    tin_hbm,
    tout_hbm,
    wo_hbm,
    w1_hbm,
    w2_hbm,
    wh_hbm,
    stats_ref,
    rows_ref,
    loss_ref,
    t_gain_one_ref,
    t_shift_one_ref,
    t_gain_two_ref,
    t_shift_two_ref,
    gain_one_ref,
    shift_one_ref,
    b_outer_ref,
    gain_two_ref,
    shift_two_ref,
    b_inner_ref,
    out_hbm,
    dctx_hbm,
    dres_hbm,
    pack_hbm,
    xt_ref,
    tctx_ref,
    two_ref,
    xs_ref,
    sctx_ref,
    tin_ref,
    tout_ref,
    wo_ref,
    w1_ref,
    w2_ref,
    wh_ref,
    out_ref,
    dctx_ref,
    dres_ref,
    pack_ref,
    act_ref,
    slope_ref,
    t_low_ref,
    t_sum_ref,
    in_sem,
    out_sem,
):
    sources = (
        xt_hbm, tctx_hbm, two_hbm, xs_hbm, sctx_hbm, tin_hbm, tout_hbm, wo_hbm, w1_hbm, w2_hbm, wh_hbm
    )
    targets = (xt_ref, tctx_ref, two_ref, xs_ref, sctx_ref, tin_ref, tout_ref, wo_ref, w1_ref, w2_ref, wh_ref)
    loads = {
        name: pltpu.make_async_copy(source, target, in_sem.at[k])
        for k, (name, source, target) in enumerate(zip(DENSE_IN, sources, targets))
    }
    for c in loads.values():
        c.start()
    width_s, units_s = w1_ref.shape
    width_t, units_t = tin_ref.shape
    slots = xt_ref.shape[0]
    low = lambda v: v.astype(BF16)
    stores = []

    def store(source, target):
        stores.append(pltpu.make_async_copy(source, target, out_sem.at[len(stores)]))
        stores[-1].start()

    def columns(*refs):
        n = refs[0].shape[0]
        index = lax.broadcasted_iota(jnp.int32, (8, n), 0)
        block = jnp.zeros((8, n), F32)
        for k, ref in enumerate(refs):
            block = jnp.where(index == k, ref[...].reshape(1, n), block)
        turned = jnp.transpose(block)
        return [turned[:, k : k + 1] for k in range(len(refs))]

    t_gain_one, t_shift_one, t_gain_two, t_shift_two = columns(
        t_gain_one_ref, t_shift_one_ref, t_gain_two_ref, t_shift_two_ref
    )
    gain_one, shift_one, b_outer, gain_two, shift_two = columns(
        gain_one_ref, shift_one_ref, b_outer_ref, gain_two_ref, shift_two_ref
    )
    (b_inner,) = columns(b_inner_ref)
    spot = pad_heads()
    pack_ref[...] = jnp.zeros_like(pack_ref)
    act_ref[units_s:, :] = jnp.ones((act_ref.shape[0] - units_s, slots), BF16)
    for name in ("xt", "tctx", "two"):
        loads[name].wait()
    start = jnp.transpose(xt_ref[...]).astype(F32) + tn(two_ref[...], tctx_ref[...])
    t_normed = normalize(start, t_gain_one, t_shift_one)[0]
    t_low_ref[...] = low(t_normed)
    t_sum_ref[...] = t_normed
    for name in ("xs", "sctx", "tin", "tout"):
        loads[name].wait()

    def feed_forward(c, carry):
        units = pl.ds(pl.multiple_of(c * width_t, width_t), width_t)
        pre = tn(tin_ref[:, units], t_low_ref[...])
        active = low(0.5 * pre * (1.0 + lax.erf(pre * ROOT_HALF)))
        t_sum_ref[...] += tn(tout_ref[units, :], active)
        return carry

    lax.fori_loop(0, units_t // width_t, feed_forward, 0)
    target = normalize(t_sum_ref[...], t_gain_two, t_shift_two)[0]
    for name in ("wo", "w1", "w2", "wh"):
        loads[name].wait()
    wop = low(nn(spot, wo_ref[...]))
    context = sctx_ref[...]
    context_low = low(context)
    normed, unit_one, rscale_one = normalize(
        xs_ref[...].astype(F32) + tn(wop, context_low), gain_one, shift_one
    )
    normed_low = low(normed)
    pre = tn(w1_ref[...], normed_low) + b_inner
    half = 0.5 * (1.0 + lax.erf(pre * ROOT_HALF))
    slope_ref[...] = half + pre * (ROOT_PI * jnp.exp(-0.5 * pre * pre))
    act_ref[:units_s, :] = low(pre * half)
    student, unit_two, rscale_two = normalize(
        normed + nn(w2_ref[...], act_ref[:units_s, :]) + b_outer, gain_two, shift_two
    )
    student_low = low(student)
    out_ref[...] = student_low
    store(out_ref, out_hbm)
    gap = tn(wh_ref[...], student_low) - target
    filled = rows_ref[2:3, :]
    masked = filled * gap
    d_proj = low(2.0 * masked)
    third = slice(2 * BLOCK, 2 * BLOCK + width_s)
    pack_ref[third, :width_t] = low(nt(student_low, d_proj))
    d_student = nn(wh_ref[...], d_proj)
    d_two = normalize_back(d_student, unit_two, rscale_two, gain_two)
    d_outer = low(d_two)
    main = units_s // 128 * 128
    spare = units_s - main
    strip = 3 * BLOCK
    pack_ref[:width_s, :main] = low(nt(d_outer, act_ref[:main, :]))
    pack_ref[strip : strip + STRIP, STRIP_OUTER : STRIP_OUTER + width_s] = low(
        nt(act_ref[main : main + STRIP, :], d_outer)
    )
    store(pack_ref.at[:BLOCK], pack_hbm.at[:BLOCK])
    d_inner = low(tn(w2_ref[...], d_outer) * slope_ref[...])
    ones = jnp.ones((8, slots), BF16)
    pack_ref[BLOCK : BLOCK + width_s, :main] = low(nt(normed_low, d_inner[:main]))
    pack_ref[BLOCK + width_s : BLOCK + width_s + 8, :main] = low(nt(ones, d_inner[:main]))
    pack_ref[strip : strip + spare, :width_s] = low(nt(d_inner[main:], normed_low))
    pack_ref[strip : strip + spare, STRIP_BIAS : STRIP_BIAS + 8] = low(nt(d_inner[main:], ones))
    store(pack_ref.at[BLOCK : 2 * BLOCK], pack_hbm.at[BLOCK : 2 * BLOCK])
    d_normed = nn(w1_ref[...], d_inner) + d_two
    d_one = normalize_back(d_normed, unit_one, rscale_one, gain_one)
    dres_ref[...] = d_one
    store(dres_ref, dres_hbm)
    d_att = low(d_one)
    gwo = low(nt(context_low, d_att))
    pack_ref[third, width_t : width_t + width_s] = low(tn(spot, gwo))
    d_context = nn(wop, d_att)
    row = lax.broadcasted_iota(jnp.int32, (PAD, slots), 0)
    for head in range(HEADS):
        pair, h = head // 2, head % 2
        inverse = stats_ref[pair, h : h + 1, :]
        cross = stats_ref[pair, 2 + h : 3 + h, :]
        rows = slice(head * PAD, (head + 1) * PAD)
        part = low(d_context[rows] * inverse).astype(F32)
        delta = -jnp.sum(part * context[rows], axis=0, keepdims=True) - inverse * cross
        high = low(delta).astype(F32)
        rest = delta - high
        middle = low(rest).astype(F32)
        part = jnp.where(row == SLOT_ONE, high, part)
        part = jnp.where(row == SLOT_ONE + 1, middle, part)
        part = jnp.where(row == SLOT_ONE + 2, rest - middle, part)
        dctx_ref[rows, :] = low(part)
    store(dctx_ref, dctx_hbm)
    lane = lax.broadcasted_iota(jnp.int32, (width_s, 128), 1)
    sums = jnp.zeros((width_s, 128), F32)
    for k, values in enumerate((d_normed * unit_one, d_normed, d_student * unit_two, d_student)):
        sums = jnp.where(lane == k, jnp.sum(fold_lanes(values), axis=1, keepdims=True), sums)
    pack_ref[strip + spare : strip + spare + 8, :width_s] = low(jnp.transpose(sums)[:8])
    square = jnp.sum(fold_lanes(masked * gap).reshape(-1, 8, 128), axis=0)
    row = lax.broadcasted_iota(jnp.int32, (8, 128), 0)
    for c in range(slots // 128):
        square += jnp.where(row == c % 8, width_t * loss_ref[0:1, c * 128 : (c + 1) * 128], 0.0)
    pack_ref[2 * BLOCK + width_s : 2 * BLOCK + width_s + 8, :128] = low(square)
    store(pack_ref.at[2 * BLOCK :], pack_hbm.at[2 * BLOCK :])
    for c in stores:
        c.wait()


def dense(packed_rows, big, small):
    xt, tctx, two, xs, sctx, tin, tout, wo, w1, w2, wh = big
    slots, width_t = xt.shape
    width_s, units_s = w1.shape
    padded = HEADS * PAD
    inner_pad = -(-units_s // 128) * 128
    sds = jax.ShapeDtypeStruct
    outs = [
        sds((width_s, slots), BF16),
        sds((padded, slots), BF16),
        sds((width_s, slots), F32),
        sds((packed_rows, units_s // 128 * 128), BF16),
    ]
    anywhere = pl.BlockSpec(memory_space=pl.ANY)
    return pl.pallas_call(
        dense_kernel,
        out_shape=outs,
        in_specs=[anywhere] * len(big) + [VMEM] * len(small),
        out_specs=[anywhere] * len(outs),
        scratch_shapes=[pltpu.VMEM(a.shape, a.dtype) for a in big]
        + [pltpu.VMEM(a.shape, a.dtype) for a in outs]
        + [
            pltpu.VMEM((inner_pad, slots), BF16),
            pltpu.VMEM((units_s, slots), F32),
            pltpu.VMEM((width_t, slots), BF16),
            pltpu.VMEM((width_t, slots), F32),
            pltpu.SemaphoreType.DMA((len(big),)),
            pltpu.SemaphoreType.DMA((6,)),
        ],
        compiler_params=pltpu.CompilerParams(vmem_limit_bytes=BIG),
    )(*big, *small)


def group_sizes():
    seq = lax.axis_size("seq")
    core = 2 if seq % 2 == 0 else 1
    chain = 4 if seq // core % 4 == 0 else 1
    return {"core": core, "batch": lax.axis_size("batch"), "chain": chain, "outer": seq // core // chain}


class Group:
    def __init__(self, name):
        batch, seq = lax.axis_index("batch"), lax.axis_index("seq")
        sizes = group_sizes()
        self.size = sizes[name]
        if name == "batch":
            self.place = batch
            self.device = lambda j: (j, seq)
        else:
            stride = {"core": 1, "chain": sizes["core"], "outer": sizes["core"] * sizes["chain"]}[name]
            self.place = seq // stride % self.size
            self.device = lambda j: (batch, seq + (j - self.place) * stride)

    def other(self, k):
        return (self.place + k) % self.size


class Chain:
    def __init__(self, names, source, scratch, local=None):
        self.names, self.source, self.local = names, source, local
        self.groups = [Group(n) for n in names]
        count = len(names)
        self.outer = Group("outer")
        self.received, self.sums = scratch[:count], scratch[count : 2 * count]
        self.around, self.whole, self.send, self.arrive = scratch[2 * count :]
        rows = self.whole.shape[0]
        self.rows, self.base, base = [], [], 0
        for g in self.groups:
            self.base.append(base)
            rows //= g.size
            base = base + g.place * rows
            self.rows.append(rows)
        self.mine = base
        self.sem = 0
        self.pending = []

    @staticmethod
    def scratch(names, rows, lanes):
        received, sums, copies = [], [], 0
        total, sizes = rows, group_sizes()
        for size in (sizes[n] for n in names):
            rows = rows // size
            received.append(pltpu.VMEM((max(size - 1, 1), rows, lanes), BF16))
            sums.append(pltpu.VMEM((rows, lanes), BF16))
            copies += 2 * (size - 1)
        copies = max(copies + sizes["outer"] - 1, 1)
        return (
            received
            + sums
            + [
                pltpu.VMEM((max(sizes["outer"] - 1, 1), rows, lanes), BF16),
                pltpu.VMEM((total, lanes), BF16),
                pltpu.SemaphoreType.DMA((copies,)),
                pltpu.SemaphoreType.DMA((copies,)),
            ]
        )

    def copy(self, ends):
        at = self.sem
        self.sem += 1

        def form():
            source, target, device = ends()
            return pltpu.make_async_remote_copy(
                src_ref=source,
                dst_ref=target,
                send_sem=self.send.at[at],
                recv_sem=self.arrive.at[at],
                device_id=device,
                device_id_type=MESH,
            )

        form().start()
        self.pending.append(form)

    def scatter(self, k):
        g, rows = self.groups[k], self.rows[k]
        source = self.source if k == 0 else self.sums[k - 1]

        def ends(step):
            other = g.other(step)
            there = pl.ds(pl.multiple_of(other * rows, 16), rows)
            return source.at[there], self.received[k].at[step - 1], g.device(other)

        for step in range(1, g.size):
            self.copy(partial(ends, step))

    def wait(self):
        for form in self.pending:
            form().wait()
        self.pending = []

    def add(self, k):
        self.wait()
        g, rows = self.groups[k], self.rows[k]
        source = self.source if k == 0 else self.sums[k - 1]
        if k == 0 and self.local is not None:
            total = self.local[...].astype(F32)
        else:
            total = source[pl.ds(pl.multiple_of(g.place * rows, 16), rows), :].astype(F32)
        for step in range(1, g.size):
            total = total + self.received[k][step - 1].astype(F32)
        total = total.astype(BF16)
        if k < len(self.groups) - 1 or self.outer.size > 1:
            self.sums[k][...] = total
        if k == len(self.groups) - 1:
            if self.outer.size > 1:
                total = self.exchange(total)
            self.whole[pl.ds(pl.multiple_of(self.mine, 16), rows), :] = total

    def exchange(self, total):
        g = self.outer

        def ends(step):
            return self.sums[-1], self.around.at[step - 1], g.device(g.other(step))

        for step in range(1, g.size):
            self.copy(partial(ends, step))
        self.wait()
        total = total.astype(F32)
        for step in range(1, g.size):
            total = total + self.around[step - 1].astype(F32)
        return total.astype(BF16)

    def gather(self, k):
        g, rows = self.groups[k], self.rows[k]

        def ends(step):
            here = self.whole.at[pl.ds(pl.multiple_of(self.base[k] + g.place * rows, 16), rows)]
            return here, here, g.device(g.other(step))

        for step in range(1, g.size):
            self.copy(partial(ends, step))

    def advance(self, stage):
        count = len(self.groups)
        if 0 < stage <= count:
            self.add(stage - 1)
        else:
            self.wait()
        if stage < count:
            self.scatter(stage)
        elif stage < 2 * count:
            self.gather(2 * count - 1 - stage)


EARLY = (
    (0, 384, ("core", "batch", "chain")),
    (384, 768, ("core", "batch", "chain")),
    (768, 1152, ("core", "chain", "batch")),
)
LATE = (
    (0, 128, ("core", "batch", "chain")),
    (128, 256, ("core", "batch", "chain")),
    (256, 384, ("core", "chain", "batch")),
)


def back_kernel(
    windows,
    sq_hbm,
    skv_hbm,
    dctx_hbm,
    e_hbm,
    g_hbm,
    pack_hbm,
    xs_hbm,
    dres_hbm,
    wq_hbm,
    wk_hbm,
    wv_hbm,
    rows_ref,
    dx_ref,
    early_ref,
    late_ref,
    sq_ref,
    skv_ref,
    dctx_ref,
    e_ref,
    g_ref,
    half_ref,
    xs_ref,
    dres_ref,
    wq_ref,
    wk_ref,
    wv_ref,
    in_sem,
    block_sem,
    dq_ref,
    dkv_ref,
    give_ref,
    take_ref,
    qkv_ref,
    halo_send,
    halo_arrive,
    out_sem,
    *scratch,
):
    step = pl.program_id(0)
    w = (windows - step) % windows
    slots = windows * WIN
    width_s = xs_ref.shape[0]
    batch, seq = lax.axis_index("batch"), lax.axis_index("seq")
    peers = lax.axis_size("seq")
    chains, used = [], 0
    for source, local, cuts in ((pack_hbm, half_ref, EARLY), (qkv_ref, None, LATE)):
        for first, last, names in cuts:
            size = 2 * len(names) + 4
            mine = local.at[:, first:last] if local is not None else None
            chains.append(Chain(names, source.at[:, first:last], scratch[used : used + size], mine))
            used += size
    soon, late = chains[: len(EARLY)], chains[len(EARLY) :]
    first_seq, last_seq = seq == 0, seq == peers - 1

    def halo(side):
        return pltpu.make_async_remote_copy(
            src_ref=give_ref.at[side],
            dst_ref=take_ref.at[1 - side],
            send_sem=halo_send.at[side],
            recv_sem=halo_arrive.at[1 - side],
            device_id=(batch, seq - 1 + 2 * side),
            device_id_type=MESH,
        )

    half_rows = half_ref.shape[0]
    ends = {
        "half": (pack_hbm.at[pl.ds(pl.multiple_of(seq % group_sizes()["core"] * half_rows, 16), half_rows)], half_ref),
        "sq": (sq_hbm, sq_ref),
        "skv": (skv_hbm, skv_ref),
        "dctx": (dctx_hbm, dctx_ref),
        "xs": (xs_hbm, xs_ref),
        "dres": (dres_hbm, dres_ref),
        "wq": (wq_hbm, wq_ref),
        "wk": (wk_hbm, wk_ref),
        "wv": (wv_hbm, wv_ref),
    }
    load = lambda name: pltpu.make_async_copy(*ends[name], in_sem.at[list(ends).index(name)])

    def blocks(number):
        slot, window = number % 2, (windows - number) % windows
        return [
            pltpu.make_async_copy(source.at[window], target.at[slot], block_sem.at[k, slot])
            for k, (source, target) in enumerate(((e_hbm, e_ref), (g_hbm, g_ref)))
        ]

    @pl.when(step == 0)
    def _():
        load("half").start()
        dkv_ref[...] = jnp.zeros_like(dkv_ref)
        take_ref[...] = jnp.zeros_like(take_ref)
        qkv_ref[...] = jnp.zeros_like(qkv_ref)
        barrier = pltpu.get_barrier_semaphore()
        count = 0
        for g in (Group(n) for n in ("core", "batch", "chain", "outer")):
            for k in range(1, g.size):
                pl.semaphore_signal(barrier, inc=1, device_id=g.device(g.other(k)), device_id_type=MESH)
                count += 1

        for move in (1, peers - 1):
            pl.semaphore_signal(
                barrier, inc=1, device_id=(batch, (seq + move) % peers), device_id_type=MESH
            )
        pl.semaphore_wait(barrier, count + 2)

        for c in soon:
            c.advance(0)
        for c in blocks(0):
            c.start()
        for name in ("sq", "skv", "dctx"):
            load(name).start()
        for c in blocks(1):
            c.start()
        for name in ("xs", "dres", "wq", "wk", "wv"):
            load(name).start()
        for name in ("sq", "skv", "dctx", "half"):
            load(name).wait()

    for c in blocks(step):
        c.wait()
    slot = step % 2
    at = pl.multiple_of(w * WIN, WIN)
    left = pl.ds(at, WIN)
    own = pl.ds(pl.multiple_of(at + WIN, WIN), WIN)
    right = pl.ds(pl.multiple_of(at + 2 * WIN, WIN), WIN)
    early_row, late_row = rows_ref[0:1, left], rows_ref[1:2, left]
    early_low, late_low = early_row.astype(BF16), late_row.astype(BF16)

    def one_head(head):
        rows = pl.ds(pl.multiple_of(head * PAD, PAD), PAD)
        query, grad = sq_ref[rows, left], dctx_ref[rows, left]
        stacked = lambda a: jnp.concatenate([a * early_low, a * late_low], axis=0)
        query_fold, grad_fold = stacked(query), stacked(grad)
        beside = lambda k: jnp.concatenate([skv_ref[k, rows, left], skv_ref[k, rows, right]], axis=0)
        keys_fold, values_fold = beside(0), beside(1)
        keys, values = skv_ref[0, rows, own], skv_ref[1, rows, own]
        e_own, e_side = e_ref[slot, head, :WIN, :], e_ref[slot, head, WIN:, :]
        d_own = (e_own.astype(F32) * (tn(values, grad) + g_ref[slot, head, :WIN, :].astype(F32))).astype(BF16)
        d_side = (
            e_side.astype(F32) * (tn(values_fold, grad_fold) + g_ref[slot, head, WIN:, :].astype(F32))
        ).astype(BF16)
        side = nn(keys_fold, d_side)
        d_query = nn(keys, d_own) + early_row * side[:PAD] + late_row * side[PAD:]
        dq_ref[rows, left] = (d_query * HD_S**-0.5).astype(BF16)
        for k, (a, a_fold, b, b_fold, scale) in enumerate(
            ((query, query_fold, d_own, d_side, 1.0 / LOG2E), (grad, grad_fold, e_own, e_side, None))
        ):
            fix = (lambda v: v * scale) if scale else (lambda v: v)
            side = fix(nt(a_fold, b_fold))
            dkv_ref[k, rows, own] += fix(nt(a, b))
            dkv_ref[k, rows, left] += side[:PAD]
            dkv_ref[k, rows, right] += side[PAD:]

    def body(pair, carry):
        one_head(2 * pair)
        one_head(2 * pair + 1)
        return carry

    def send_halo():
        for side, lanes in ((0, slice(0, WIN)), (1, slice(WIN + slots, 2 * WIN + slots))):
            give_ref[side] = dkv_ref[:, :, lanes].astype(BF16)

        @pl.when(jnp.logical_not(first_seq))
        def _():
            halo(0).start()

        @pl.when(jnp.logical_not(last_seq))
        def _():
            halo(1).start()

    def advance(which, stage):
        for c in which:
            c.advance(stage)

    half = PAIRS // 2
    plan = {
        (0, 0): [partial(advance, soon, 1)],
        (1, 1): [send_halo],
        (2, 0): [partial(advance, soon, 2)],
        (3, 0): [partial(advance, soon, 3)],
    }
    for part in range(2):
        lax.fori_loop(part * half, (part + 1) * half, body, 0)
        for k in range(windows):
            for action in plan.get((k, part), []):
                pl.when(step == k)(action)

    @pl.when(step < windows - 2)
    def _():
        for c in blocks(step + 2):
            c.start()

    @pl.when(step == windows - 1)
    def _():
        for name in ("xs", "dres", "wq", "wk", "wv"):
            load(name).wait()

        @pl.when(jnp.logical_not(first_seq))
        def _():
            halo(0).wait_send()
            halo(1).wait_recv()

        @pl.when(jnp.logical_not(last_seq))
        def _():
            halo(1).wait_send()
            halo(0).wait_recv()

        advance(soon, 4)
        spot = pad_heads()
        plains = []
        for k in range(3):
            if k == 0:
                grad = dq_ref[...]
            else:
                mine = dkv_ref[k - 1, :, WIN : WIN + slots]
                first = mine[:, :WIN] + take_ref[0, k - 1].astype(F32)
                last = mine[:, slots - WIN :] + take_ref[1, k - 1].astype(F32)
                grad = jnp.concatenate([first, mine[:, WIN : slots - WIN], last], axis=1).astype(BF16)
            plain = tn(spot, grad).astype(BF16)
            plains.append(plain)
            qkv_ref[k * BLOCK : k * BLOCK + width_s, :width_s] = nt(xs_ref[...], plain).astype(BF16)
        advance(late, 0)
        total = dres_ref[...]
        for w_ref, plain in zip((wq_ref, wk_ref, wv_ref), plains):
            total = total + nn(w_ref[...], plain)
        dx_ref[...] = total.astype(BF16)
        advance(late, 1)
        advance(late, 2)
        advance(soon, 5)
        advance(late, 3)
        advance(soon, 6)

        def put(group, cuts, target, first_sem):
            made = []
            for n, (c, (first, last, _)) in enumerate(zip(group, cuts)):
                made.append(pltpu.make_async_copy(c.whole, target.at[:, first:last], out_sem.at[first_sem + n]))
                made[-1].start()
            return made

        copies = put(soon, EARLY, early_ref, 0)
        advance(late, 4)
        advance(late, 5)
        advance(late, 6)
        copies += put(late, LATE, late_ref, len(EARLY))
        for c in copies:
            c.wait()


def back(sq, skv, dctx, e, g, rows, pack, xs, dres, wq, wk, wv):
    padded, slots = sq.shape
    windows = slots // WIN
    width_s = xs.shape[0]
    packed_rows = pack.shape[0]
    anywhere = pl.BlockSpec(memory_space=pl.ANY)
    held = lambda a: pltpu.VMEM(a.shape, a.dtype)
    scratch = [held(sq), held(skv), held(dctx)]
    scratch += [pltpu.VMEM((2,) + a.shape[1:], a.dtype) for a in (e, g)]
    scratch += [pltpu.VMEM((packed_rows // group_sizes()["core"], pack.shape[1]), BF16)]
    scratch += [held(a) for a in (xs, dres, wq, wk, wv)]
    scratch += [
        pltpu.SemaphoreType.DMA((9,)),
        pltpu.SemaphoreType.DMA((2, 2)),
        pltpu.VMEM((padded, slots), BF16),
        pltpu.VMEM((2, padded, slots + 2 * WIN), F32),
        pltpu.VMEM((2, 2, padded, WIN), BF16),
        pltpu.VMEM((2, 2, padded, WIN), BF16),
        pltpu.VMEM((packed_rows, QKV_LANES), BF16),
        pltpu.SemaphoreType.DMA((2,)),
        pltpu.SemaphoreType.DMA((2,)),
        pltpu.SemaphoreType.DMA((len(EARLY) + len(LATE),)),
    ]
    for first, last, names in EARLY + LATE:
        scratch += Chain.scratch(names, packed_rows, last - first)
    return pl.pallas_call(
        partial(back_kernel, windows),
        grid=(windows,),
        out_shape=[
            jax.ShapeDtypeStruct((width_s, slots), BF16),
            jax.ShapeDtypeStruct(pack.shape, BF16),
            jax.ShapeDtypeStruct((packed_rows, QKV_LANES), BF16),
        ],
        in_specs=[anywhere] * 11 + [VMEM],
        out_specs=[pl.BlockSpec((width_s, slots), lambda i: (0, 0)), anywhere, anywhere],
        scratch_shapes=scratch,
        compiler_params=pltpu.CompilerParams(
            vmem_limit_bytes=BIG,
            dimension_semantics=("arbitrary",),
            collective_id=0,
            has_side_effects=True,
        ),
    )(sq, skv, dctx, e, g, pack, xs, dres, wq, wk, wv, rows)


def unpack_kernel(
    every,
    width_t,
    early_hbm,
    late_hbm,
    dx_in_hbm,
    dx_hbm,
    loss_ref,
    gq_hbm,
    gk_hbm,
    gv_hbm,
    gwo_hbm,
    ginner_hbm,
    gouter_hbm,
    ghid_hbm,
    bouter_ref,
    binner_ref,
    gain_one_ref,
    shift_one_ref,
    gain_two_ref,
    shift_two_ref,
    early_ref,
    late_ref,
    gq_ref,
    gk_ref,
    gv_ref,
    gwo_ref,
    ginner_ref,
    gouter_ref,
    ghid_ref,
    in_sem,
    out_sem,
):
    width_s = gq_ref.shape[0]
    units = ginner_ref.shape[1]
    scale = 1.0 / every
    full = lambda v: v.astype(F32) * scale
    main = units // 128 * 128
    rest = units - main
    cuts = (slice(3 * BLOCK, 3 * BLOCK + STRIP),) + tuple(slice(k * BLOCK, (k + 1) * BLOCK) for k in range(3))
    loads = [pltpu.make_async_copy(early_hbm.at[c], early_ref.at[c], in_sem.at[k]) for k, c in enumerate(cuts)]
    loads.append(pltpu.make_async_copy(late_hbm, late_ref, in_sem.at[4]))
    for c in loads:
        c.start()
    stores = []

    def store(source, target):
        stores.append(pltpu.make_async_copy(source, target, out_sem.at[len(stores)]))
        stores[-1].start()

    store(dx_in_hbm, dx_hbm)
    loads[0].wait()
    strip = full(early_ref[3 * BLOCK : 3 * BLOCK + STRIP, :])
    turned = lambda at, n: jnp.transpose(strip[:, at : at + n])
    for k, ref in enumerate((gain_one_ref, shift_one_ref, gain_two_ref, shift_two_ref)):
        ref[...] = strip[rest + k, :width_s]
    bouter_ref[...] = strip[rest, STRIP_OUTER : STRIP_OUTER + width_s]
    loads[1].wait()
    gouter_ref[:, :main] = full(early_ref[:width_s, :main])
    gouter_ref[:, main:] = turned(STRIP_OUTER, STRIP_BIAS - STRIP_OUTER)[:width_s, :rest]
    store(gouter_ref, gouter_hbm)
    loads[2].wait()
    ginner_ref[:, :main] = full(early_ref[BLOCK : BLOCK + width_s, :main])
    ginner_ref[:, main:] = turned(0, STRIP_OUTER)[:width_s, :rest]
    store(ginner_ref, ginner_hbm)
    first = full(early_ref[BLOCK + width_s : BLOCK + width_s + 8, :main])[0:1]
    binner_ref[...] = jnp.concatenate([first, turned(STRIP_BIAS, 128)[0:1, :rest]], axis=1)[0]
    loads[3].wait()
    third = slice(2 * BLOCK, 2 * BLOCK + width_s)
    ghid_ref[...] = full(early_ref[third, :width_t])
    store(ghid_ref, ghid_hbm)
    gwo_ref[...] = full(early_ref[third, width_t : width_t + width_s])
    store(gwo_ref, gwo_hbm)
    loads[4].wait()
    for k, (ref, hbm) in enumerate(((gq_ref, gq_hbm), (gk_ref, gk_hbm), (gv_ref, gv_hbm))):
        ref[...] = full(late_ref[k * BLOCK : k * BLOCK + width_s, :width_s])
        store(ref, hbm)
    part = early_ref[2 * BLOCK + width_s : 2 * BLOCK + width_s + 8, :128].astype(F32)
    total = jnp.sum(jnp.sum(part, axis=0, keepdims=True), axis=1, keepdims=True)
    loss_ref[...] = total
    for c in stores:
        c.wait()


def unpack(every, width_t, units, early, late, dx):
    width_s = dx.shape[0]
    sds = lambda *shape: jax.ShapeDtypeStruct(shape, F32)
    square = sds(width_s, width_s)
    large = [square, square, square, square, sds(width_s, units), sds(width_s, units), sds(width_s, width_t)]
    vectors = [sds(width_s), sds(units)] + [sds(width_s)] * 4
    anywhere = pl.BlockSpec(memory_space=pl.ANY)
    return pl.pallas_call(
        partial(unpack_kernel, every, width_t),
        out_shape=[jax.ShapeDtypeStruct(dx.shape, BF16), sds(1, 1)] + large + vectors,
        in_specs=[anywhere] * 3,
        out_specs=[anywhere, VMEM] + [anywhere] * len(large) + [VMEM] * len(vectors),
        scratch_shapes=[pltpu.VMEM(early.shape, BF16), pltpu.VMEM(late.shape, BF16)]
        + [pltpu.VMEM(a.shape, F32) for a in large]
        + [pltpu.SemaphoreType.DMA((5,)), pltpu.SemaphoreType.DMA((len(large) + 1,))],
        compiler_params=pltpu.CompilerParams(vmem_limit_bytes=BIG),
    )(early, late, dx)


def local(
    inputs,
    teacher_input,
    filled_slot_mask,
    seg_lengths,
    query_weight,
    key_weight,
    value_weight,
    w_output,
    gain_one,
    shift_one,
    w_inner,
    b_inner,
    w_outer,
    b_outer,
    gain_two,
    shift_two,
    w_hidden,
    teacher_query_weight,
    teacher_key_weight,
    teacher_value_weight,
    teacher_output,
    teacher_gain_one,
    teacher_shift_one,
    teacher_inner,
    teacher_outer,
    teacher_gain_two,
    teacher_shift_two,
):
    xs = jnp.transpose(inputs[0])
    xt = teacher_input[0]
    slots, width_t = xt.shape
    width_s = xs.shape[0]
    stats, loss_rows, rows, tctx, sctx, sq, skv, e, g = attend(
        filled_slot_mask,
        seg_lengths,
        xt,
        xs,
        teacher_query_weight,
        teacher_key_weight,
        teacher_value_weight,
        query_weight,
        key_weight,
        value_weight,
    )
    devices = lax.axis_size("seq") * lax.axis_size("batch")
    sizes = group_sizes()
    unit = 16 * sizes["core"] * sizes["batch"] * sizes["chain"]
    packed_rows = -(-3 * BLOCK // unit) * unit
    out, dctx, dres, pack = dense(
        packed_rows,
        (
            xt,
            tctx,
            teacher_output,
            xs,
            sctx,
            teacher_inner,
            teacher_outer,
            w_output,
            w_inner,
            jnp.transpose(w_outer),
            w_hidden,
        ),
        (stats, rows, loss_rows)
        + (
            teacher_gain_one,
            teacher_shift_one,
            teacher_gain_two,
            teacher_shift_two,
            gain_one,
            shift_one,
            b_outer,
            gain_two,
            shift_two,
            b_inner,
        ),
    )
    dx, early, late = back(sq, skv, dctx, e, g, rows, pack, xs, dres, query_weight, key_weight, value_weight)
    dx, loss, gq, gk, gv, gwo, ginner, gouter, ghid, *vectors = unpack(
        slots * devices, width_t, w_inner.shape[1], early, late, dx
    )
    g_b_outer, g_b_inner, g_gain_one, g_shift_one, g_gain_two, g_shift_two = vectors
    return (
        jnp.transpose(out)[None],
        jnp.transpose(dx)[None],
        loss[0, 0] / (slots * devices * width_t),
        gq,
        gk,
        gv,
        gwo,
        g_gain_one,
        g_shift_one,
        ginner,
        g_b_inner,
        jnp.transpose(gouter),
        g_b_outer,
        g_gain_two,
        g_shift_two,
        ghid,
    )


def solution(mesh):
    row_split = P("batch", "seq", None)
    return jax.shard_map(
        local,
        mesh=mesh,
        in_specs=(row_split, row_split, P("batch", None), P("batch", None)) + (P(),) * 23,
        out_specs=(row_split, row_split) + (P(),) * 14,
        check_vma=False,
    )
```
